32 devices in a mesh: seq: 8 (over z, x), head: 4 (over y, core).
Axes of the slice: x: 2, y: 2, z: 4, core: 2. Of those that a mesh axis runs over, the one named last changes fastest.
Arguments:
- word_input: bfloat16 [4096, 512], P('seq'), may hold values from -6 to 6
- char_input: bfloat16 [4096, 16, 256], P('seq'), may hold values from -6 to 6
- char_count: int32 [4096], P('seq'), may hold values from 1 to 16
- document_ids: int32 [4096], P('seq'), may hold values from 0 to 2, as said below
- output_grad: bfloat16 [4096, 512], P('seq'), may hold values from -6 to 6
- char_gain: float32 [256], replicated, may hold values from 0.5 to 1.5
- char_proj: bfloat16 [3, 256, 256], P(None, None, 'head'), may hold values from -0.375 to 0.375
- char_out: bfloat16 [256, 256], P('head'), may hold values from -1.5 to 1.5
- pool_gain: float32 [256], replicated, may hold values from 0.5 to 1.5
- pool_proj: bfloat16 [256, 512], replicated, may hold values from -0.375 to 0.375
- attn_gain: float32 [512], replicated, may hold values from 0.5 to 1.5
- attn_proj: bfloat16 [3, 512, 512], P(None, None, 'head'), may hold values from -0.25 to 0.25
- attn_out: bfloat16 [512, 512], P('head'), may hold values from -6 to 6
- ffn_gain: float32 [512], replicated, may hold values from 0.5 to 1.5
- ffn_up: bfloat16 [512, 2048], P(None, 'head'), may hold values from -0.25 to 0.25
- ffn_down: bfloat16 [2048, 512], P('head'), may hold values from -0.5 to 0.5
Outputs:
- layer_out: bfloat16 [4096, 512], P('seq')
- grad_words: bfloat16 [4096, 512], P('seq')
- grad_chars: bfloat16 [4096, 16, 256], P(('seq', 'head'))
- grad_char_gain: float32 [256], replicated
- grad_char_proj: float32 [3, 256, 256], P(None, None, 'head')
- grad_char_out: float32 [256, 256], P('head')
- grad_pool_gain: float32 [256], replicated
- grad_pool_proj: float32 [256, 512], replicated
- grad_attn_gain: float32 [512], replicated
- grad_attn_proj: float32 [3, 512, 512], P(None, None, 'head')
- grad_attn_out: float32 [512, 512], P('head')
- grad_ffn_gain: float32 [512], replicated
- grad_ffn_up: float32 [512, 2048], P(None, 'head')
- grad_ffn_down: float32 [2048, 512], P('head')
The draws below stay inside these ranges and needn't reach their ends.
Inputs may be any that keep to these rules, and one draw needn't show every extreme that they name: `document_ids`: document numbers begin at 0 with the first word, never fall, and rise by at most one from a word to the next; the sequence holds three documents.
All inputs are finite; a program needn't handle non-finite values.
Results may differ from the reference program's by a relative error of at most 0.024.
Values may be sent and summed in bfloat16 or wider, within the bound.
A program may use at most 320 MiB of HBM per device.

```python
import math
import jax
import jax.numpy as jnp
from jax import lax

D = 512
HEADS = 8
FF = 2048
CD = 256
CHEADS = 4
CHARS = 16
WORDS_DEV = 512
WORDS = 4096
N_SEQ = 8


def draw_document_ids(key, part):
    key = jax.random.fold_in(key, 11)
    all_words = WORDS_DEV * N_SEQ
    first_key, second_key = jax.random.split(key, 2)
    opening = jax.random.randint(first_key, (), 1, WORDS_DEV // 2 + 1)
    closing = all_words - jax.random.randint(second_key, (), 1, WORDS_DEV // 2 + 1)
    positions = jnp.arange(all_words, dtype=jnp.int32)
    starts = (positions == opening) | (positions == closing)
    return jnp.cumsum(starts.astype(jnp.int32)).astype(jnp.int32)


def set_ends(result, stream_key, least, high):
    dims = result.shape
    index_at = [jax.random.randint(jax.random.fold_in(stream_key, axis), (), 0, dims[axis]) for axis in range(len(dims))]
    result = result.at[tuple(index_at)].set(least)
    longest = dims.index(max(dims))
    index_at[longest] = (index_at[longest] + 1) % dims[longest]
    return result.at[tuple(index_at)].set(high)


def block_scale(stream_key, dims, cuts, low, largest):
    gain, own = 1.0, jax.random.fold_in(stream_key, 6)
    for dim, shards_of in cuts:
        steps = jnp.exp(jax.random.uniform(jax.random.fold_in(own, dim), (shards_of,), jnp.float32, low / len(cuts), largest / len(cuts)))
        gain = gain * jnp.repeat(steps, dims[dim] // shards_of).reshape([-1 if axis == dim else 1 for axis in range(len(dims))])
    return gain


def gaussian(rng, extent, width, most, shards=(), kind=jnp.bfloat16):
    array = jax.random.normal(rng, extent, jnp.float32) * width
    if len(shards) > 0:
        array = block_scale(rng, extent, shards, -0.22, 0.18) * array
    return jnp.clip(array, min=-most, max=most).astype(kind)


def setup_inputs(seed: int = 0) -> dict:
    streams_of = jax.random.split(jax.random.key(seed), 17)
    return {
        "word_input": gaussian(streams_of[0], (WORDS, D), 1.0, 6.0, ((0, 8),)),
        "char_input": gaussian(streams_of[1], (WORDS, CHARS, CD), 1.0, 6.0, ((0, 8),)),
        "char_count": set_ends(jax.random.randint(streams_of[2], (WORDS,), 1, CHARS + 1), jax.random.fold_in(streams_of[2], 1), 1, CHARS).astype(jnp.int32),
        "document_ids": draw_document_ids(jax.random.fold_in(streams_of[16], 71), 0),
        "output_grad": gaussian(streams_of[4], (WORDS, D), 1.0, 6.0, ((0, 8),)),
        "char_gain": jnp.clip(1.0 + 0.1 * jax.random.normal(streams_of[5], (CD,), jnp.float32), 0.5, 1.5),
        "char_proj": gaussian(streams_of[6], (3, CD, CD), CD ** -0.5, 0.375, ((2, 4),)),
        "char_out": gaussian(streams_of[7], (CD, CD), (CD // 16) ** -0.5, 1.5, ((0, 4),)),
        "pool_gain": jnp.clip(1.0 + 0.1 * jax.random.normal(streams_of[8], (CD,), jnp.float32), 0.5, 1.5),
        "pool_proj": gaussian(streams_of[9], (CD, D), CD ** -0.5, 0.375),
        "attn_gain": jnp.clip(1.0 + 0.1 * jax.random.normal(streams_of[10], (D,), jnp.float32), 0.5, 1.5),
        "attn_proj": gaussian(streams_of[11], (3, D, D), D ** -0.5, 0.25, ((2, 4),)),
        "attn_out": gaussian(streams_of[12], (D, D), 1.0, 6.0, ((0, 4),)),
        "ffn_gain": jnp.clip(1.0 + 0.1 * jax.random.normal(streams_of[13], (D,), jnp.float32), 0.5, 1.5),
        "ffn_up": gaussian(streams_of[14], (D, FF), D ** -0.5, 0.25, ((1, 4),)),
        "ffn_down": gaussian(streams_of[15], (FF, D), (FF // 16) ** -0.5, 0.5, ((0, 4),)),
    }


@jax.custom_vjp
def low(v):
    return lax.optimization_barrier(v.astype(jnp.bfloat16)).astype(jnp.float32)

@jax.custom_vjp
def low_back(v):
    return v

def low_keep(v):
    return (low(v), None)

def low_pass(kept, grad):
    return (grad,)

def back_keep(v):
    return (v, None)

def back_low(kept, grad):
    return (low(grad),)
low.defvjp(low_keep, low_pass)
low_back.defvjp(back_keep, back_low)
EPSILON = 1e-06
NEGATIVE = -1e+30
HIGHEST = lax.Precision.HIGHEST

def both_ways(values):
    return low(low_back(values))

def rms_norm(values, gain_vec):
    factor = lax.rsqrt(lax.optimization_barrier(jnp.mean(values * values, axis=-1, keepdims=True)) + EPSILON)
    return values * factor * gain_vec

def softmax_rows(scores):
    row_peak = lax.optimization_barrier(jnp.max(scores, axis=-1, keepdims=True))
    raised = jnp.exp(scores - row_peak)
    return raised / lax.optimization_barrier(jnp.sum(raised, axis=-1, keepdims=True))

def char_block(char_values, char_count, char_gain, char_proj, char_out):
    word_count, letters = (char_values.shape[0], char_values.shape[1])
    char_size = CD // CHEADS
    char_valid = jnp.arange(letters, dtype=jnp.int32)[None, :] < char_count[:, None]
    letter_mask = char_valid.astype(jnp.float32)
    number = char_count.astype(jnp.float32)
    normed = low(rms_norm(char_values, char_gain))
    mapped = both_ways(jnp.einsum('wlc,sce->swle', normed, char_proj, precision=HIGHEST))
    mapped = mapped.reshape(3, word_count, letters, CHEADS, char_size)
    scores = low_back(jnp.einsum('wqhd,wkhd->whqk', mapped[0], mapped[1], precision=HIGHEST) * char_size ** (-0.5))
    weights = low(softmax_rows(jnp.where(char_valid[:, None, None, :], scores, NEGATIVE)))
    mixed = low_back(jnp.einsum('whqk,wkhd->wqhd', weights, mapped[2], precision=HIGHEST))
    pooled = lax.optimization_barrier(jnp.sum(mixed * letter_mask[:, :, None, None], axis=1)) / number[:, None, None]
    branch = low_back(jnp.dot(low(pooled.reshape(word_count, CD)), char_out, precision=HIGHEST))
    mean_chars = lax.optimization_barrier(jnp.sum(char_values * letter_mask[:, :, None], axis=1)) / number[:, None]
    return mean_chars + branch

def word_attention(queries, keys, values, document_ids):
    all_words = queries.shape[0]
    head_size = D // HEADS
    block_rows = math.gcd(all_words, 128)
    key_pos = jnp.arange(all_words, dtype=jnp.int32)

    def one_block(block_index):
        block_start = (block_index * block_rows).astype(jnp.int32)
        query_rows = lax.dynamic_slice_in_dim(queries, block_start, block_rows, 0)
        row_pos = block_start + jnp.arange(block_rows, dtype=jnp.int32)
        row_doc = lax.dynamic_slice_in_dim(document_ids, block_start, block_rows, 0)
        scores = low_back(jnp.einsum('qhd,khd->hqk', query_rows, keys, precision=HIGHEST) * head_size ** (-0.5))
        allowed = (key_pos[None, :] <= row_pos[:, None]) & (document_ids[None, :] == row_doc[:, None])
        weights = low(softmax_rows(jnp.where(allowed[None], scores, NEGATIVE)))
        return jnp.einsum('hqk,khd->qhd', weights, values, precision=HIGHEST)
    blocks_out = lax.map(jax.checkpoint(one_block), jnp.arange(all_words // block_rows, dtype=jnp.int32))
    return blocks_out.reshape(all_words, HEADS, head_size)

def forward(word_input, char_input, char_gain, char_proj, char_out, pool_gain, pool_proj, attn_gain, attn_proj, attn_out, ffn_gain, ffn_up, ffn_down, char_count, document_ids):
    all_words = word_input.shape[0]
    head_size = D // HEADS
    group_rows = math.gcd(all_words, 1024)
    groups = all_words // group_rows
    char_groups = char_input.reshape(groups, group_rows, char_input.shape[1], CD)
    count_groups = char_count.reshape(groups, group_rows)

    def char_group(pieces):
        return char_block(pieces[0], pieces[1], char_gain, char_proj, char_out)
    summary = lax.map(jax.checkpoint(char_group), (char_groups, count_groups)).reshape(all_words, CD)
    hidden = word_input + low_back(jnp.dot(low(rms_norm(summary, pool_gain)), pool_proj, precision=HIGHEST))
    normed = low(rms_norm(hidden, attn_gain))
    mapped = both_ways(jnp.einsum('wc,sce->swe', normed, attn_proj, precision=HIGHEST))
    mapped = mapped.reshape(3, all_words, HEADS, head_size)
    mixed = both_ways(word_attention(mapped[0], mapped[1], mapped[2], document_ids).reshape(all_words, D))
    second = hidden + low_back(jnp.dot(mixed, attn_out, precision=HIGHEST))
    upward = low_back(jnp.dot(low(rms_norm(second, ffn_gain)), ffn_up, precision=HIGHEST))
    active = low(jax.nn.gelu(upward))
    return second + low_back(jnp.dot(active, ffn_down, precision=HIGHEST))

def reference(word_input, char_input, char_count, document_ids, output_grad, char_gain, char_proj, char_out, pool_gain, pool_proj, attn_gain, attn_proj, attn_out, ffn_gain, ffn_up, ffn_down):
    params = tuple((argument.astype(jnp.float32) for argument in (word_input, char_input, char_gain, char_proj, char_out, pool_gain, pool_proj, attn_gain, attn_proj, attn_out, ffn_gain, ffn_up, ffn_down)))

    def layer(*inputs):
        return forward(*inputs, char_count, document_ids)
    layer_out, pullback = jax.vjp(layer, *params)
    gradients = pullback(output_grad.astype(jnp.float32))
    weight_grads = tuple((gradient.astype(jnp.float32) for gradient in gradients[2:]))
    return (layer_out.astype(jnp.bfloat16), gradients[0].astype(jnp.bfloat16), gradients[1].astype(jnp.bfloat16), weight_grads[0], weight_grads[1], weight_grads[2], weight_grads[3], weight_grads[4], weight_grads[5], weight_grads[6], weight_grads[7], weight_grads[8], weight_grads[9], weight_grads[10])
```

```python
import functools
from types import SimpleNamespace

import jax
import jax.numpy as jnp
from jax import lax
from jax.experimental import pallas as pl
from jax.experimental.pallas import tpu as pltpu
from jax.sharding import PartitionSpec as P

MESH = pl.DeviceIdType.MESH
BF = jnp.bfloat16
F32 = jnp.float32
EPSILON = 1e-06
NEGATIVE = -1e30

D = 512
C = 256
L = 16
G = 4
Q = 128
W = G * Q
PW = 2 * W
R = Q * L
FS = 512
GROUPS = R // 128
QT = 256
KU = 512
MARKS = 8
SLOTS = 8
FR = 1024
AR = 512

INPUTS = [
    "word_input",
    "char_input",
    "char_count",
    "document_ids",
    "output_grad",
    "char_gain",
    "char_proj",
    "char_out",
    "pool_gain",
    "pool_proj",
    "attn_gain",
    "attn_proj",
    "attn_out",
    "ffn_gain",
    "ffn_up",
    "ffn_down",
]
OUTPUTS = ["o_layer", "o_words", "o_chars", "o_ffn", "o_att", "o_chr", "o_pool", "o_gain"]


def dot(a, b):
    return lax.dot_general(a, b, (((1,), (0,)), ((), ())), preferred_element_type=F32)


def dot_t(a, b):
    return lax.dot_general(a, b, (((1,), (1,)), ((), ())), preferred_element_type=F32)


def dot_l(a, b):
    return lax.dot_general(a, b, (((0,), (0,)), ((), ())), preferred_element_type=F32)


def iota(shape, axis):
    return lax.broadcasted_iota(jnp.int32, shape, axis)


def swap(a):
    return pltpu.roll(a, 64, 1)


def rms_factor(values):
    return lax.rsqrt(jnp.mean(values * values, axis=-1, keepdims=True) + EPSILON)


def rms_back(upstream, values, gain):
    factor = rms_factor(values)
    unit = values * factor
    scaled = upstream * gain
    centre = jnp.mean(scaled * unit, axis=-1, keepdims=True)
    return factor * (scaled - unit * centre), jnp.sum(upstream * unit, axis=0, keepdims=True)


def scratch_list(nz):
    n = 2 * nz
    vm = pltpu.VMEM
    dma = pltpu.SemaphoreType.DMA
    return dict(
        xin=vm((Q, L, C), BF),
        cnt=vm((G, 128), jnp.int32),
        docs=vm((n, G, 128), jnp.int32),
        cpr=vm((3, C, 64), BF),
        win=vm((Q, D), BF),
        ogp=vm((2, W, D), BF),
        cg=vm((1, C), F32),
        pg=vm((1, C), F32),
        ag=vm((1, D), F32),
        fg=vm((1, D), F32),
        cw=vm((G, C, 256), BF),
        cwt=vm((G, C, 256), BF),
        co=vm((G, 128, C), BF),
        pw=vm((C, D), BF),
        aw=vm((G, 3, D, 128), BF),
        ao=vm((G, 128, D), BF),
        fu=vm((G, D, FS), BF),
        fd=vm((G, FS, D), BF),
        low=vm((R, C), BF),
        cntm=vm((128, 128), F32),
        share=vm((GROUPS, 8, 128), F32),
        shc=vm((R, 128), F32),
        msel=vm((GROUPS, 16, 128), BF),
        bias=vm((GROUPS, 128, 128), F32),
        kq=vm((G, R, 256), BF),
        pt=vm((G, GROUPS, 128, 128), BF),
        pooled=vm((G, Q, 128), F32),
        gp=vm((G, Q, 128), F32),
        mean=vm((Q, C), F32),
        summ=vm((Q, C), F32),
        plow=vm((Q, C), BF),
        hid=vm((Q, D), F32),
        alow=vm((Q, D), BF),
        sec=vm((Q, D), F32),
        flow=vm((Q, D), BF),
        lay=vm((Q, D), BF),
        fsum=vm((Q, D), F32),
        act=vm((G, Q, FS), BF),
        lsum=vm((Q, D), F32),
        gsec=vm((Q, D), F32),
        gb=vm((Q, D), BF),
        gw=vm((Q, D), BF),
        gsum=vm((Q, C), F32),
        skv=vm((8, Q, 128), BF),
        sq=vm((8, 64, 128), BF),
        rq=vm((8, 64, 128), BF),
        kv=vm((nz * PW, 128), BF),
        marks=vm((min(n, MARKS) * KU, 128), BF),
        qd=vm((PW, 256), BF),
        m=vm((PW, 128), F32),
        l=vm((PW, 128), F32),
        acc=vm((PW, 128), F32),
        ob=vm((PW, 128), BF),
        lser=vm((PW // QT, 8, QT), F32),
        dlr=vm((PW // QT, 8, QT), F32),
        smx=vm((8, 64, 128), BF),
        rmx=vm((8, 64, 128), BF),
        sgm=vm((8, 64, 128), BF),
        rgm=vm((8, 64, 128), BF),
        gz=vm((PW, 128), BF),
        xg=vm((PW, 128), BF),
        acck=vm((KU, 128), F32),
        accv=vm((KU, 128), F32),
        dq=vm((PW, 128), F32),
        dkv=vm((PW, 128), F32),
        sdk=vm((min(n, SLOTS), KU, 128), BF),
        rdk=vm((nz, 2, KU, 128), BF),
        dqb=vm((PW, 128), BF),
        sdkv=vm((8, Q, 128), BF),
        rdkv=vm((8, Q, 128), BF),
        sdq=vm((8, 64, 128), BF),
        rdq=vm((8, 64, 128), BF),
        alp=vm((PW, D), BF),
        flp=vm((PW, D), BF),
        gbp=vm((PW, D), BF),
        sag=vm((8, Q, 512), BF),
        rag=vm((PW, 512), BF),
        fw=vm((FR, 256), BF),
        frs=vm((nz, FR // nz, 256), BF),
        ffin=vm((FR // nz, 256), BF),
        aw_g=vm((AR, 256), BF),
        ars=vm((nz, AR // nz, 256), BF),
        afin=vm((AR // nz, 256), BF),
        scw=vm((G, C, 256), BF),
        rcw=vm((8, 128, 256), BF),
        zcw=vm((nz, 128, 256), BF),
        cfin=vm((128, 256), BF),
        spw=vm((C, D), BF),
        rpw=vm((8, 32, D), BF),
        zpw=vm((nz, 32, D), BF),
        pfin=vm((32, D), BF),
        gn=vm((8, D), F32),
        rgn=vm((8, 8, D), F32),
        zgn=vm((nz, 8, D), F32),
        gnf=vm((8, D), F32),
        lsem=dma((24,)),
        wg_s=dma((6, 3)),
        wg_r=dma((6, 3)),
        kv_s=dma((8,)),
        kv_r=dma((8,)),
        q_s=dma((8,)),
        q_r=dma((8,)),
        mx_s=dma((8,)),
        mx_r=dma((8,)),
        gm_s=dma((8,)),
        gm_r=dma((8,)),
        dkv_s=dma((8,)),
        dkv_r=dma((8,)),
        dq_s=dma((8,)),
        dq_r=dma((8,)),
        al_s=dma((8,)),
        al_r=dma((8,)),
        fl_s=dma((8,)),
        fl_r=dma((8,)),
        gb_s=dma((8,)),
        gb_r=dma((8,)),
        ac_s=dma((8,)),
        ac_r=dma((8,)),
        cw_s=dma((8,)),
        cw_r=dma((8,)),
        pw_s=dma((8,)),
        pw_r=dma((8,)),
        pa_s=dma((8,)),
        pa_r=dma((8,)),
        gn_s=dma((8,)),
        gn_r=dma((8,)),
        kz_s=dma((n,)),
        kz_r=dma((n,)),
        dz_s=dma((nz,)),
        dz_r=dma((nz,)),
        x_s=dma((5,)),
        x_r=dma((5,)),
        dk_s=dma((n,)),
        dk_r=dma((nz, 2)),
        fr_s=dma((nz,)),
        fr_r=dma((nz,)),
        fa_s=dma((nz,)),
        fa_r=dma((nz,)),
        ar_s=dma((nz,)),
        ar_r=dma((nz,)),
        aa_s=dma((nz,)),
        aa_r=dma((nz,)),
        cz_s=dma((nz,)),
        cz_r=dma((nz,)),
        pz_s=dma((nz,)),
        pz_r=dma((nz,)),
        gz_s=dma((nz,)),
        gz_r=dma((nz,)),
        ly_s=dma((4,)),
        ly_r=dma((4,)),
        gw_s=dma((4,)),
        gw_r=dma((4,)),
    )


def rows(index, size):
    return pl.ds(pl.multiple_of(index * size, size), size)


def layer_kernel(nz, names, *refs):
    r = SimpleNamespace(**dict(zip(names, refs)))
    s = lax.axis_index("seq")
    h = lax.axis_index("head")
    x, z = lax.rem(s, 2), lax.div(s, 2)
    y, c = lax.div(h, 2), lax.rem(h, 2)
    p = 4 * x + h
    sends = []

    def peer(mask):
        px = 1 - x if mask & 4 else x
        py = 1 - y if mask & 2 else y
        pc = 1 - c if mask & 1 else c
        ph = 2 * py + pc
        return (2 * z + px, ph), 4 * px + ph

    def plane(t):
        pz = lax.rem(z + t, nz)
        return (2 * pz + x, h), pz

    def remote(src, dst, ssem, rsem, device):
        return pltpu.make_async_remote_copy(
            src_ref=src, dst_ref=dst, send_sem=ssem, recv_sem=rsem,
            device_id=device, device_id_type=MESH,
        )

    def send(src, dst, ssem, rsem, device):
        copy = remote(src, dst, ssem, rsem, device)
        copy.start()
        sends.append(copy)

    def arrive(dst, ssem, rsem):
        remote(dst, dst, ssem, rsem, peer(1)[0]).wait_recv()

    def load(src, dst, k):
        copy = pltpu.make_async_copy(src, dst, r.lsem.at[k])
        copy.start()
        return copy

    low_half = iota((1, 128), 1) < 64

    def pick(a, b):
        shape = a.shape
        return jnp.where(iota(shape, 1) < 64, a, b)

    def pack(a):
        return pick(a[:64], swap(a[64:]))

    def pack_high(a):
        return pick(swap(a[:64]), a[64:])

    barrier = pltpu.get_barrier_semaphore()
    for mask in range(1, 8):
        pl.semaphore_signal(barrier, inc=1, device_id=peer(mask)[0], device_id_type=MESH)
    for t in range(1, nz):
        pl.semaphore_signal(barrier, inc=1, device_id=plane(t)[0], device_id_type=MESH)

    ld_x = load(r.char_input.at[rows(h, Q)], r.xin, 0)
    ld_cg = load(r.char_gain, r.cg, 1)
    ld_cnt = load(r.char_count, r.cnt, 2)
    ld_cp = load(r.char_proj, r.cpr, 3)
    ld_doc = load(r.document_ids, r.docs.at[s], 4)
    ld_co = load(r.char_out, r.co.at[h, pl.ds(64, 64)], 5)
    ld_pw = load(r.pool_proj, r.pw, 6)
    ld_word = load(r.word_input.at[rows(h, Q)], r.win, 7)
    ld_pg = load(r.pool_gain, r.pg, 8)
    ld_ag = load(r.attn_gain, r.ag, 9)
    ld_fg = load(r.ffn_gain, r.fg, 10)
    ld_aw = load(r.attn_proj, r.aw.at[h], 11)
    ld_ao = load(r.attn_out, r.ao.at[h], 12)
    ld_og = load(r.output_grad, r.ogp.at[x], 13)
    ld_fu = load(r.ffn_up, r.fu.at[h], 14)
    ld_fd = load(r.ffn_down, r.fd.at[h], 15)

    r.co[:, 0:64, :] = jnp.zeros((G, 64, C), BF)

    ld_cp.wait()
    place = (iota((64, 128), 0) == iota((64, 128), 1)).astype(F32).astype(BF)
    place_high = (iota((64, 128), 0) + 64 == iota((64, 128), 1)).astype(F32).astype(BF)
    wq, wk, wv = r.cpr[0], r.cpr[1], r.cpr[2]
    r.cw[h, :, 0:128] = (dot(wk, place) + dot(wq, place_high)).astype(BF)
    r.cw[h, :, 128:256] = (dot(wq, place) + dot(wv, place_high)).astype(BF)

    ld_x.wait()
    ld_cg.wait()

    def char_norm(i, carry):
        values = r.xin[pl.ds(i * 8, 8)].astype(F32).reshape(128, C)
        r.low[rows(i, 128), :] = (values * rms_factor(values) * r.cg[...]).astype(BF)
        return carry

    lax.fori_loop(0, GROUPS, char_norm, 0, unroll=2)

    ld_cnt.wait()
    count_row = jnp.broadcast_to(r.cnt[pl.ds(h, 1), :].astype(F32), (128, 128))
    r.cntm[...] = count_row.T

    def char_masks(g, carry):
        eight = r.cntm[rows(g, 8), :]
        lane8 = iota((8, 128), 1)
        of_lane = jnp.sum(
            jnp.where(iota((8, 128), 0) == lax.div(lane8, L), eight, 0.0), axis=0, keepdims=True
        )
        lane16 = iota((16, 128), 1)
        count16 = jnp.broadcast_to(of_lane, (16, 128))
        letter16 = lax.rem(lane16, L).astype(F32)
        r.share[g] = jnp.where(letter16 < count16, 1.0 / count16, 0.0)[:8]
        r.msel[g] = jnp.where(
            (iota((16, 128), 0) == lax.div(lane16, L)) & (letter16 < count16), 1.0, 0.0
        ).astype(BF)
        row, lane = iota((128, 128), 0), iota((128, 128), 1)
        spread = jnp.where(lane == g * 8 + lax.div(row, L), 1.0, 0.0).astype(BF)
        count = dot(spread, r.cntm[...].astype(BF))
        valid = lax.rem(row, L).astype(F32) < count
        r.bias[g] = jnp.where(valid & (lax.div(row, L) == lax.div(lane, L)), 0.0, NEGATIVE)
        r.shc[rows(g, 128), :] = jnp.where(valid, 1.0 / count, 0.0)
        return carry

    lax.fori_loop(0, GROUPS, char_masks, 0)

    pl.semaphore_wait(barrier, 7 + nz - 1)

    def gather_start(k, slots):
        mine = slots(h)
        send(mine, mine, r.wg_s.at[k, 0], r.wg_r.at[k, 0], peer(1)[0])
        send(mine, mine, r.wg_s.at[k, 1], r.wg_r.at[k, 1], peer(2)[0])

    def gather_forward(k, slots):
        far = slots(2 * (1 - y) + c)
        arrive(far, r.wg_s.at[k, 1], r.wg_r.at[k, 1])
        send(far, far, r.wg_s.at[k, 2], r.wg_r.at[k, 2], peer(1)[0])

    def gather_near(k, slots):
        arrive(slots(2 * y + 1 - c), r.wg_s.at[k, 0], r.wg_r.at[k, 0])

    def gather_last(k, slots):
        arrive(slots(2 * (1 - y) + 1 - c), r.wg_s.at[k, 2], r.wg_r.at[k, 2])

    order = [h, 2 * y + 1 - c, 2 * (1 - y) + c, 2 * (1 - y) + 1 - c]
    cw_at = lambda i: r.cw.at[i]
    co_at = lambda i: r.co.at[i, pl.ds(64, 64)]
    aw_at = lambda i: r.aw.at[i]
    ao_at = lambda i: r.ao.at[i]
    fu_at = lambda i: r.fu.at[i]
    fd_at = lambda i: r.fd.at[i]

    gather_start(0, cw_at)
    ld_co.wait()
    gather_start(1, co_at)
    ld_doc.wait()
    send(r.docs.at[s], r.docs.at[s], r.x_s.at[0], r.x_r.at[0], peer(4)[0])
    ld_aw.wait()
    gather_start(2, aw_at)

    lane_scale = jnp.where((iota((1, 256), 1) < 64) | (iota((1, 256), 1) >= 192), 1.0, 0.125)
    keep_low = jnp.where(low_half, 1.0, 0.0)
    keep_high = 1.0 - keep_low

    def char_head(hh):
        def project(i, carry):
            got = dot(r.low[rows(i, 512), :], r.cw[hh]) * lane_scale
            r.kq[hh, rows(i, 512), :] = got.astype(BF)
            return carry

        lax.fori_loop(0, R // 512, project, 0)

        def attend(g, carry):
            kq = r.kq[hh, rows(g, 128), 0:128]
            qv = r.kq[hh, rows(g, 128), 128:256]
            query = (qv.astype(F32) * keep_low).astype(BF)
            scores = dot_t(kq, query) + r.bias[g]
            raised = jnp.exp(scores - jnp.max(scores, axis=0, keepdims=True))
            weights = (raised * (1.0 / jnp.sum(raised, axis=0, keepdims=True))).astype(BF)
            r.pt[hh, g] = weights
            taken = dot_t(r.msel[g], weights).astype(BF)
            got = dot(taken, qv)[:8] * (1.0 / r.cntm[rows(g, 8), :])
            r.pooled[hh, rows(g, 8), :] = got * keep_high
            return carry

        lax.fori_loop(0, GROUPS, attend, 0, unroll=4)

    char_head(order[0])
    gather_near(0, cw_at)
    char_head(order[1])
    gather_forward(0, cw_at)
    gather_forward(1, co_at)
    gather_forward(2, aw_at)
    char_head(order[2])
    gather_last(0, cw_at)
    char_head(order[3])

    def char_mean(g, carry):
        block = r.xin[pl.ds(g * 8, 8)].reshape(128, C)
        r.mean[rows(g, 8), :] = dot(r.msel[g], block)[:8] * (1.0 / r.cntm[rows(g, 8), 0:1])
        return carry

    lax.fori_loop(0, GROUPS, char_mean, 0, unroll=4)
    gather_near(1, co_at)
    gather_last(1, co_at)
    summary = r.mean[...]
    for hh in range(G):
        summary = summary + dot(r.pooled[hh].astype(BF), r.co[hh])
    r.summ[...] = summary
    ld_pg.wait()
    ld_pw.wait()
    ld_word.wait()
    ld_ag.wait()
    r.plow[...] = (summary * rms_factor(summary) * r.pg[...]).astype(BF)
    hidden = r.win[...].astype(F32) + dot(r.plow[...], r.pw[...])
    r.hid[...] = hidden
    r.alow[...] = (hidden * rms_factor(hidden) * r.ag[...]).astype(BF)

    gather_near(2, aw_at)
    gather_last(2, aw_at)
    kv_mine = lambda i: r.kv.at[rows(z * 8 + i, Q)]
    for t in range(G):
        hh = order[t]
        query = dot(r.alow[...], r.aw[hh, 0]) * 0.125
        key = dot(r.alow[...], r.aw[hh, 1])
        value = dot(r.alow[...], r.aw[hh, 2])
        r.skv[hh] = pick(key, swap(value)).astype(BF)
        r.skv[4 + hh] = pick(swap(key), value).astype(BF)
        r.sq[hh] = pack(query).astype(BF)
        r.sq[4 + hh] = pack_high(query).astype(BF)
        for mask in ((4,) if t == 0 else (t, t + 4)):
            device, to = peer(mask)
            send(r.skv.at[to], kv_mine(p), r.kv_s.at[mask], r.kv_r.at[mask], device)
            send(r.sq.at[to], r.rq.at[p], r.q_s.at[mask], r.q_r.at[mask], device)
    r.kv[rows(z * 8 + p, Q), :] = r.skv[p]
    r.rq[p] = r.sq[p]

    arrive(r.docs.at[2 * z + 1 - x], r.x_s.at[0], r.x_r.at[0])
    docs_mine = r.docs.at[pl.ds(2 * z, 2)]

    def docs_copy(t, source):
        return remote(
            r.docs.at[pl.ds(2 * source, 2)], r.docs.at[pl.ds(2 * source, 2)],
            r.dz_s.at[t], r.dz_r.at[source], (2 * lax.rem(z + t, nz) + x, h),
        )

    for t in range(1, nz):
        @pl.when(z + t < nz)
        def _():
            docs_copy(t, z).start()

    def key_marks(chunk, carry):
        row = r.docs[lax.div(chunk, 4), pl.ds(lax.rem(chunk, 4), 1), :]
        sub = iota((128, 128), 0)
        marks = jnp.where((sub < 3) & (jnp.broadcast_to(row, (128, 128)) != sub), 1.0, 0.0)
        slot = lax.rem(chunk, 4 * min(2 * nz, MARKS))
        r.marks[rows(slot, 128), :] = marks.T.astype(BF)
        return carry

    def query_marks(chunk, carry):
        row = r.docs[lax.div(z * 8 + chunk, 4), pl.ds(lax.rem(chunk, 4), 1), :]
        sub = iota((128, 128), 0)
        marks = jnp.where((sub < 3) & (jnp.broadcast_to(row, (128, 128)) == sub), NEGATIVE, 0.0)
        r.qd[rows(chunk, 128), 128:256] = marks.T.astype(BF)
        return carry

    lax.fori_loop(z * 8, z * 8 + 8, key_marks, 0)
    lax.fori_loop(0, 8, query_marks, 0)
    r.m[...] = jnp.full((PW, 128), NEGATIVE, F32)
    r.l[...] = jnp.zeros((PW, 128), F32)
    r.acc[...] = jnp.zeros((PW, 128), F32)

    for mask in range(1, 8):
        arrive(kv_mine(peer(mask)[1]), r.kv_s.at[mask], r.kv_r.at[mask])

    def unit_copy(u):
        block = r.kv.at[rows(u, KU)]
        return remote(
            block, block, r.kz_s.at[u], r.kz_r.at[u], (2 * lax.rem(z + 1, nz) + x, h)
        )

    @pl.when(z + 1 < nz)
    def _():
        unit_copy(2 * z).start()
        unit_copy(2 * z + 1).start()

    for mask in range(1, 8):
        arrive(r.rq.at[peer(mask)[1]], r.q_s.at[mask], r.q_r.at[mask])

    def unpack_queries(i, carry):
        got = r.rq[i].astype(F32)
        r.qd[rows(2 * i, 64), 0:128] = (got * keep_low).astype(BF)
        r.qd[rows(2 * i + 1, 64), 0:128] = (swap(got) * keep_low).astype(BF)
        return carry

    lax.fori_loop(0, 8, unpack_queries, 0)

    ld_ao.wait()
    gather_start(3, ao_at)
    ld_fu.wait()
    gather_start(4, fu_at)
    ld_fd.wait()
    gather_start(5, fd_at)
    ld_og.wait()
    send(r.ogp.at[x], r.ogp.at[x], r.x_s.at[1], r.x_r.at[1], peer(4)[0])
    for mask in range(1, 8):
        send(r.alow, r.alp.at[rows(p, Q)], r.al_s.at[mask], r.al_r.at[mask], peer(mask)[0])
    r.alp[rows(p, Q), :] = r.alow[...]

    def marked(kv, u):
        marks = r.marks[rows(lax.rem(u, min(2 * nz, MARKS)), KU), :]
        return jnp.concatenate([kv, marks], axis=1)

    def mark_again(u):
        if 2 * nz > MARKS:
            lax.fori_loop(4 * u, 4 * u + 4, key_marks, 0)

    def forward_tile(qt, u, causal):
        at = rows(qt, QT)
        kv = r.kv[rows(u, KU), :]
        scores = dot_t(r.qd[at, :], marked(kv, u))
        if causal:
            gap = (qt * QT - (u - 2 * z) * KU) + iota((QT, KU), 0) - iota((QT, KU), 1)
            scores = jnp.where(gap >= 0, scores, NEGATIVE)
        old = r.m[at, :]
        new = jnp.maximum(old, jnp.max(scores, axis=1, keepdims=True))
        raised = jnp.exp(scores - new[:, 0:1])
        fade = jnp.exp(old - new)
        r.m[at, :] = new
        r.l[at, :] = r.l[at, :] * fade + jnp.sum(raised, axis=1, keepdims=True)
        r.acc[at, :] = r.acc[at, :] * fade + dot(raised.astype(BF), kv)

    def forward_first(qt, carry):
        forward_tile(qt, 2 * z, True)
        return carry

    def forward_second(qt, carry):
        forward_tile(qt, 2 * z + 1, True)
        return carry

    lax.fori_loop(0, PW // QT, forward_first, 0)
    lax.fori_loop(KU // QT, PW // QT, forward_second, 0)

    def wait_docs(source, carry):
        docs_copy(1, source).wait_recv()
        return carry

    lax.fori_loop(0, z, wait_docs, 0)
    if 2 * nz <= MARKS:
        lax.fori_loop(0, z * 8, key_marks, 0)

    def forward_unit(i, carry):
        u = 2 * z - 1 - i
        unit_copy(u).wait_recv()
        mark_again(u)

        @pl.when(z + 1 < nz)
        def _():
            unit_copy(u).start()

        def step(qt, inner):
            forward_tile(qt, u, False)
            return inner

        return lax.fori_loop(0, PW // QT, step, carry)

    lax.fori_loop(0, 2 * z, forward_unit, 0)

    def finish_rows(qt, carry):
        for half in range(2):
            i = 2 * qt + half
            at = rows(i, 128)
            total = r.l[at, :]
            out = r.acc[at, :] * (1.0 / total) * keep_high
            r.acc[at, :] = out
            r.ob[at, :] = out.astype(BF)
            r.smx[i] = pack_high(out).astype(BF)
            lse = (r.m[at, :] + jnp.log(total)).T
            r.lser[qt, :, half * 128 : half * 128 + 128] = lse[:8]
        return carry

    lax.fori_loop(0, PW // QT, finish_rows, 0)
    for mask in range(1, 8):
        device, to = peer(mask)
        send(r.smx.at[to], r.rmx.at[p], r.mx_s.at[mask], r.mx_r.at[mask], device)
    r.rmx[p] = r.smx[p]
    gather_forward(3, ao_at)
    gather_forward(4, fu_at)
    gather_forward(5, fd_at)
    gather_near(3, ao_at)
    gather_last(3, ao_at)
    ld_fg.wait()
    for mask in range(1, 8):
        arrive(r.rmx.at[peer(mask)[1]], r.mx_s.at[mask], r.mx_r.at[mask])

    def two_heads(a, b):
        a, b = a.astype(F32), b.astype(F32)
        return jnp.concatenate([pick(a, swap(b)), pick(swap(a), b)], axis=0).astype(BF)

    second = r.hid[...]
    for hh in range(G):
        second = second + dot(two_heads(r.rmx[hh], r.rmx[4 + hh]), r.ao[hh])
    r.sec[...] = second
    r.flow[...] = (second * rms_factor(second) * r.fg[...]).astype(BF)

    grad_rows = r.ogp[x, rows(h, Q), :]
    r.fsum[...] = jnp.zeros((Q, D), F32)
    for t in range(G):
        hh = order[t]
        if t == 1:
            gather_near(4, fu_at)
            gather_near(5, fd_at)
        if t == 3:
            gather_last(4, fu_at)
            gather_last(5, fd_at)
        upward = dot(r.flow[...], r.fu[hh])
        square = upward * upward
        inner = 0.7978845608028654 * upward * (1.0 + 0.044715 * square)
        bent = jnp.tanh(inner)
        half_up = 0.5 * (1.0 + bent)
        active = (upward * half_up).astype(BF)
        slope = half_up + 0.5 * upward * (1.0 - bent * bent) * (
            0.7978845608028654 * (1.0 + 0.134145 * square)
        )
        r.act[hh] = active
        grad_up = (dot_t(grad_rows, r.fd[hh]) * slope).astype(BF)
        r.fsum[...] += dot_t(grad_up, r.fu[hh])
        r.sag[hh, :, 0:256] = active[:, 0:256]
        r.sag[hh, :, 256:512] = grad_up[:, 0:256]
        r.sag[4 + hh, :, 0:256] = active[:, 256:512]
        r.sag[4 + hh, :, 256:512] = grad_up[:, 256:512]
    back, gain_ffn = rms_back(r.fsum[...], r.sec[...], r.fg[...])
    grad_second = grad_rows.astype(F32) + back
    r.gsec[...] = grad_second
    r.gb[...] = grad_second.astype(BF)
    r.gn[0:1, :] = gain_ffn

    for t in range(G):
        hh = order[t]
        grad = dot_t(r.gb[...], r.ao[hh])
        r.sgm[hh] = pack(grad).astype(BF)
        r.sgm[4 + hh] = pack_high(grad).astype(BF)
        for mask in ((4,) if t == 0 else (t, t + 4)):
            device, to = peer(mask)
            send(r.sgm.at[to], r.rgm.at[p], r.gm_s.at[mask], r.gm_r.at[mask], device)
    r.rgm[p] = r.sgm[p]
    r.dq[...] = jnp.zeros((PW, 128), F32)
    r.lsum[...] = r.sec[...]

    def layer_part(hh, carry):
        r.lsum[...] += dot(r.act[hh], r.fd[hh])
        return carry

    lax.fori_loop(0, G, layer_part, 0)
    r.lay[...] = r.lsum[...].astype(BF)
    for mask in range(1, 8):
        arrive(r.rgm.at[peer(mask)[1]], r.gm_s.at[mask], r.gm_r.at[mask])

    def unpack_grads(qt, carry):
        for half in range(2):
            i = 2 * qt + half
            at = rows(i, 128)
            got = r.rgm[i].astype(F32)
            grad = jnp.concatenate([swap(got), got], axis=0) * keep_high
            r.gz[at, :] = grad.astype(BF)
            r.xg[at, :] = pick(r.qd[at, 0:128].astype(F32), grad).astype(BF)
            delta = jnp.sum(grad * r.acc[at, :], axis=1, keepdims=True)
            r.dlr[qt, :, half * 128 : half * 128 + 128] = jnp.broadcast_to(delta, (128, 128)).T[:8]
        return carry

    lax.fori_loop(0, PW // QT, unpack_grads, 0)

    for mask in range(1, 8):
        device, to = peer(mask)
        send(r.sag.at[to], r.rag.at[rows(p, Q)], r.ac_s.at[mask], r.ac_r.at[mask], device)
        send(r.flow, r.flp.at[rows(p, Q)], r.fl_s.at[mask], r.fl_r.at[mask], device)
        send(r.gb, r.gbp.at[rows(p, Q)], r.gb_s.at[mask], r.gb_r.at[mask], device)
    r.rag[rows(p, Q), :] = r.sag[p]
    r.flp[rows(p, Q), :] = r.flow[...]
    r.gbp[rows(p, Q), :] = r.gb[...]
    for mask in range(1, 4):
        mine = r.o_layer.at[rows(h, Q)]
        send(r.lay, mine, r.ly_s.at[mask], r.ly_r.at[mask], peer(mask)[0])
    st_lay = load(r.lay, r.o_layer.at[rows(h, Q)], 16)

    def backward_tile(qt, u, causal):
        at = rows(qt, QT)
        kv = r.kv[rows(u, KU), :]
        scores = dot_t(marked(kv, u), r.qd[at, :])
        weights = jnp.exp(scores - r.lser[qt, 0:1, :])
        if causal:
            gap = (qt * QT - (u - 2 * z) * KU) + iota((KU, QT), 1) - iota((KU, QT), 0)
            weights = jnp.where(gap >= 0, weights, 0.0)
        dweights = dot_t(kv, r.gz[at, :])
        dscores = (weights * (dweights - r.dlr[qt, 0:1, :])).astype(BF)
        other = r.xg[at, :]
        r.acck[...] += dot(dscores, other)
        r.accv[...] += dot(weights.astype(BF), other)
        r.dq[at, :] += dot_l(dscores, kv)

    def clear_unit():
        r.acck[...] = jnp.zeros((KU, 128), F32)
        r.accv[...] = jnp.zeros((KU, 128), F32)

    def grad_copy(u):
        pz = lax.div(u, 2)
        return remote(
            r.sdk.at[lax.rem(u, min(2 * nz, SLOTS))], r.rdk.at[z, lax.rem(u, 2)], r.dk_s.at[u], r.dk_r.at[z, lax.rem(u, 2)],
            (2 * pz + x, h),
        )

    def backward_unit(u, carry):
        clear_unit()
        mark_again(u)
        if 2 * nz > SLOTS:
            @pl.when(u >= SLOTS)
            def _():
                grad_copy(u - SLOTS).wait_send()

        def step(qt, inner):
            backward_tile(qt, u, False)
            return inner

        lax.fori_loop(0, PW // QT, step, 0)
        r.sdk[lax.rem(u, min(2 * nz, SLOTS))] = pick(r.acck[...], r.accv[...]).astype(BF)
        grad_copy(u).start()
        return carry

    lax.fori_loop(0, 2 * z, backward_unit, 0)
    for own in range(2):
        clear_unit()
        mark_again(2 * z + own)

        def own_step(qt, carry):
            backward_tile(qt, 2 * z + own, True)
            return carry

        lax.fori_loop(own * (KU // QT), PW // QT, own_step, 0)
        r.dkv[own * KU : own * KU + KU, :] = pick(r.acck[...], r.accv[...])

    def all_arrive(dst, ssem, rsem):
        for mask in range(1, 8):
            arrive(dst.at[rows(peer(mask)[1], Q)], ssem.at[mask], rsem.at[mask])

    all_arrive(r.rag, r.ac_s, r.ac_r)
    all_arrive(r.flp, r.fl_s, r.fl_r)
    arrive(r.ogp.at[1 - x], r.x_s.at[1], r.x_r.at[1])
    for i in range(2):
        r.fw[i * 256 : i * 256 + 256, :] = dot_l(
            r.flp[:, i * 256 : i * 256 + 256], r.rag[:, 256:512]
        ).astype(BF)
        r.fw[512 + i * 256 : 768 + i * 256, :] = (
            dot_l(r.rag[0:W, 0:256], r.ogp[0, :, i * 256 : i * 256 + 256])
            + dot_l(r.rag[W:PW, 0:256], r.ogp[1, :, i * 256 : i * 256 + 256])
        ).astype(BF)

    def spread_start(src, size, slots, ssem, rsem):
        for t in range(1, nz):
            device, pz = plane(t)
            send(src.at[rows(pz, size)], slots.at[z], ssem.at[t], rsem.at[z], device)

    def spread_sum(src, size, slots, ssem, rsem):
        slots[z] = src[rows(z, size), :]
        for t in range(1, nz):
            pz = plane(t)[1]
            arrive(slots.at[pz], ssem.at[t], rsem.at[pz])
        total = slots[0].astype(F32)
        for i in range(1, nz):
            total = total + slots[i].astype(F32)
        return total.astype(BF)

    def final_start(src, out, size, ssem, rsem, lk):
        mine = out.at[x, rows(z, size)]
        for t in range(1, nz):
            send(src, mine, ssem.at[t], rsem.at[z], plane(t)[0])
        return load(src, mine, lk)

    def final_cross(out, size, ssem, rsem, copy, k):
        copy.wait()
        for t in range(1, nz):
            pz = plane(t)[1]
            arrive(out.at[x, rows(pz, size)], ssem.at[t], rsem.at[pz])
        send(out.at[x], out.at[x], r.x_s.at[k], r.x_r.at[k], peer(4)[0])

    spread_start(r.fw, FR // nz, r.frs, r.fr_s, r.fr_r)

    def add_grads(pz, carry):
        for own in range(2):
            part = r.rdk.at[pz, own]
            remote(part, part, r.dk_s.at[own], r.dk_r.at[pz, own], peer(1)[0]).wait_recv()
            r.dkv[own * KU : own * KU + KU, :] += r.rdk[pz, own].astype(F32)
        return carry

    lax.fori_loop(z + 1, nz, add_grads, 0)

    def back_rows(i, carry):
        at = rows(i, 128)
        r.sdkv[i] = r.dkv[at, :].astype(BF)
        grad = r.dq[at, :] * 0.125
        r.sdq[i] = pack(grad).astype(BF)
        r.dqb[at, :] = (grad * keep_low).astype(BF)
        return carry

    lax.fori_loop(0, 8, back_rows, 0)
    for mask in range(1, 8):
        device, to = peer(mask)
        send(r.sdkv.at[to], r.rdkv.at[p], r.dkv_s.at[mask], r.dkv_r.at[mask], device)
        send(r.sdq.at[to], r.rdq.at[p], r.dq_s.at[mask], r.dq_r.at[mask], device)
    r.rdkv[p] = r.sdkv[p]
    r.rdq[p] = r.sdq[p]

    all_arrive(r.alp, r.al_s, r.al_r)
    all_arrive(r.gbp, r.gb_s, r.gb_r)
    for i in range(2):
        cols = slice(i * 256, i * 256 + 256)
        r.aw_g[cols, 0:128] = (
            dot_l(r.alp[:, cols], r.dqb[...]) + dot_l(r.gbp[:, cols], r.ob[...])
        ).astype(BF)
        r.aw_g[cols, 128:256] = dot_l(r.alp[:, cols], r.sdkv[...].reshape(PW, 128)).astype(BF)
    spread_start(r.aw_g, AR // nz, r.ars, r.ar_s, r.ar_r)

    for mask in range(1, 8):
        arrive(r.rdkv.at[peer(mask)[1]], r.dkv_s.at[mask], r.dkv_r.at[mask])
        arrive(r.rdq.at[peer(mask)[1]], r.dq_s.at[mask], r.dq_r.at[mask])

    attn_sum = jnp.zeros((Q, D), F32)
    for hh in range(G):
        first, other = r.rdkv[hh].astype(F32), r.rdkv[4 + hh].astype(F32)
        attn_sum = attn_sum + dot_t(two_heads(r.rdq[hh], r.rdq[4 + hh]), r.aw[hh, 0])
        attn_sum = attn_sum + dot_t(pick(first, swap(other)).astype(BF), r.aw[hh, 1])
        attn_sum = attn_sum + dot_t(pick(swap(first), other).astype(BF), r.aw[hh, 2])
    back, gain_attn = rms_back(attn_sum, r.hid[...], r.ag[...])
    r.gw[...] = (r.gsec[...] + back).astype(BF)
    r.gn[1:2, :] = gain_attn
    for mask in range(1, 4):
        mine = r.o_words.at[rows(h, Q)]
        send(r.gw, mine, r.gw_s.at[mask], r.gw_r.at[mask], peer(mask)[0])
    st_gw = load(r.gw, r.o_words.at[rows(h, Q)], 17)
    grad_summary, gain_pool = rms_back(dot_t(r.gw[...], r.pw[...]), r.summ[...], r.pg[...])
    r.gsum[...] = grad_summary
    gs_low = grad_summary.astype(BF)
    r.gn[2:3, 0:256] = gain_pool
    r.spw[...] = dot_l(r.plow[...], r.gw[...]).astype(BF)
    for mask in range(1, 8):
        device, to = peer(mask)
        send(r.spw.at[rows(to, 32)], r.rpw.at[p], r.pw_s.at[mask], r.pw_r.at[mask], device)
    r.rpw[p] = r.spw[rows(p, 32), :]

    r.ffin[...] = spread_sum(r.fw, FR // nz, r.frs, r.fr_s, r.fr_r)
    st_ffn = final_start(r.ffin, r.o_ffn, FR // nz, r.fa_s, r.fa_r, 18)

    def char_head_back(hh):
        r.gp[hh] = dot_t(gs_low, r.co[hh])
        w = r.cw[hh].astype(F32)
        r.cwt[hh, :, 0:128] = swap(w[:, 0:128]).astype(BF)
        r.cwt[hh, :, 128:256] = (w[:, 128:256] * keep_high).astype(BF)

        def attend(g, carry):
            at = rows(g, 128)
            kq = r.kq[hh, at, 0:128]
            value = r.kq[hh, at, 128:256].astype(F32)
            grad8 = r.gp[hh, rows(g, 8), :]
            grad = jnp.broadcast_to(grad8[:, None, :], (8, L, 128)).reshape(128, 128)
            weights = r.pt[hh, g].astype(F32)
            share = r.share[g, 0:1, :]
            gain = jnp.sum(value * grad, axis=1, keepdims=True)
            lifted = weights * gain
            centre = jnp.sum(lifted, axis=0, keepdims=True)
            dscores = ((lifted - weights * centre) * share).astype(BF)
            taken = jnp.sum(weights * share, axis=1, keepdims=True)
            grads = pick(dot_l(dscores, kq) * 0.125, dot(dscores, kq))
            r.kq[hh, at, 0:128] = grads.astype(BF)
            r.kq[hh, at, 128:256] = (taken * grad).astype(BF)
            return carry

        lax.fori_loop(0, GROUPS, attend, 0, unroll=4)
        term = dot_l(r.low[...], r.kq[hh])
        pooled = swap(r.pooled[hh]).astype(BF)
        r.scw[hh, :, 0:128] = term[:, 0:128].astype(BF)
        r.scw[hh, :, 128:256] = (term[:, 128:256] + dot_l(gs_low, pooled)).astype(BF)

    for t in (3, 2, 1, 0):
        hh = order[t]
        char_head_back(hh)
        for mask in ((4,) if t == 0 else (t, t + 4)):
            device, to = peer(mask)
            px = 1 - x if mask & 4 else x
            send(
                r.scw.at[hh, rows(px, 128)], r.rcw.at[p], r.cw_s.at[mask], r.cw_r.at[mask], device
            )
    r.rcw[p] = r.scw[h, rows(x, 128), :]

    r.afin[...] = spread_sum(r.aw_g, AR // nz, r.ars, r.ar_s, r.ar_r)
    st_att = final_start(r.afin, r.o_att, AR // nz, r.aa_s, r.aa_r, 19)

    def plane_sum(slots, ssem, rsem):
        for mask in range(1, 8):
            arrive(slots.at[peer(mask)[1]], ssem.at[mask], rsem.at[mask])
        total = slots[0].astype(F32)
        for i in range(1, 8):
            total = total + slots[i].astype(F32)
        return total

    def planes_start(slots, ssem, rsem):
        for t in range(1, nz):
            send(slots.at[z], slots.at[z], ssem.at[t], rsem.at[z], plane(t)[0])

    def planes_sum(slots, ssem, rsem):
        for t in range(1, nz):
            pz = plane(t)[1]
            arrive(slots.at[pz], ssem.at[t], rsem.at[pz])
        total = slots[0].astype(F32)
        for i in range(1, nz):
            total = total + slots[i].astype(F32)
        return total

    r.zpw[z] = plane_sum(r.rpw, r.pw_s, r.pw_r).astype(BF)
    planes_start(r.zpw, r.pz_s, r.pz_r)

    def char_back(i, gain_sum):
        at = rows(i, 128)
        upstream = dot_t(r.kq[0, at, :], r.cwt[0])
        for hh in range(1, G):
            upstream = upstream + dot_t(r.kq[hh, at, :], r.cwt[hh])
        values = r.xin[pl.ds(i * 8, 8)].astype(F32).reshape(128, C)
        back, gain = rms_back(upstream, values, r.cg[...])
        of_word = jnp.broadcast_to(r.gsum[rows(i, 8), :][:, None, :], (8, L, C)).reshape(128, C)
        full = back + r.shc[at, 0:1] * of_word
        r.xin[pl.ds(i * 8, 8)] = full.astype(BF).reshape(8, L, C)
        return gain_sum + gain

    gain_char = lax.fori_loop(0, GROUPS, char_back, jnp.zeros((1, C), F32))
    st_chars = load(r.xin, r.o_chars, 20)
    r.gn[2:3, 256:512] = gain_char
    r.gn[3:8, :] = jnp.zeros((5, D), F32)
    for mask in range(1, 8):
        send(r.gn, r.rgn.at[p], r.gn_s.at[mask], r.gn_r.at[mask], peer(mask)[0])
    r.rgn[p] = r.gn[...]

    r.zcw[z] = plane_sum(r.rcw, r.cw_s, r.cw_r).astype(BF)
    planes_start(r.zcw, r.cz_s, r.cz_r)
    r.zgn[z] = plane_sum(r.rgn, r.gn_s, r.gn_r)
    planes_start(r.zgn, r.gz_s, r.gz_r)
    final_cross(r.o_ffn, FR // nz, r.fa_s, r.fa_r, st_ffn, 2)
    r.pfin[...] = planes_sum(r.zpw, r.pz_s, r.pz_r).astype(BF)
    for mask in range(1, 8):
        mine = r.o_pool.at[rows(p, 32)]
        send(r.pfin, mine, r.pa_s.at[mask], r.pa_r.at[mask], peer(mask)[0])
    st_pool = load(r.pfin, r.o_pool.at[rows(p, 32)], 21)
    final_cross(r.o_att, AR // nz, r.aa_s, r.aa_r, st_att, 3)
    r.cfin[...] = planes_sum(r.zcw, r.cz_s, r.cz_r).astype(BF)
    send(r.cfin, r.o_chr.at[x], r.x_s.at[4], r.x_r.at[4], peer(4)[0])
    st_chr = load(r.cfin, r.o_chr.at[x], 22)
    r.gnf[...] = planes_sum(r.zgn, r.gz_s, r.gz_r)
    st_gain = load(r.gnf, r.o_gain, 23)

    arrive(r.o_ffn.at[1 - x], r.x_s.at[2], r.x_r.at[2])
    arrive(r.o_att.at[1 - x], r.x_s.at[3], r.x_r.at[3])
    arrive(r.o_chr.at[1 - x], r.x_s.at[4], r.x_r.at[4])
    for mask in range(1, 8):
        arrive(r.o_pool.at[rows(peer(mask)[1], 32)], r.pa_s.at[mask], r.pa_r.at[mask])
    for mask in range(1, 4):
        from_head = peer(mask)[0][1]
        arrive(r.o_layer.at[rows(from_head, Q)], r.ly_s.at[mask], r.ly_r.at[mask])
        arrive(r.o_words.at[rows(from_head, Q)], r.gw_s.at[mask], r.gw_r.at[mask])
    for copy in (st_lay, st_gw, st_chars, st_pool, st_chr, st_gain):
        copy.wait()
    for copy in sends:
        copy.wait_send()
    for t in range(1, nz):
        @pl.when(z + t < nz)
        def _():
            docs_copy(t, z).wait_send()

    @pl.when(z + 1 < nz)
    def _():
        def sent(u, carry):
            unit_copy(u).wait_send()
            return carry

        lax.fori_loop(0, 2 * z + 2, sent, 0)

    def grads_sent(u, carry):
        grad_copy(u).wait_send()
        return carry

    lax.fori_loop(jnp.maximum(2 * z - SLOTS, 0), 2 * z, grads_sent, 0)


def per_device(nz, *arguments):
    given = dict(zip(INPUTS, arguments))
    for name in ("char_count", "document_ids"):
        given[name] = given[name].reshape(G, 128)
    for name in ("char_gain", "pool_gain", "attn_gain", "ffn_gain"):
        given[name] = given[name].reshape(1, -1)
    scratch = scratch_list(nz)
    any_space = pl.BlockSpec(memory_space=pl.ANY)
    out_shape = [
        jax.ShapeDtypeStruct((W, D), BF),
        jax.ShapeDtypeStruct((W, D), BF),
        jax.ShapeDtypeStruct((Q, L, C), BF),
        jax.ShapeDtypeStruct((2, FR, 256), BF),
        jax.ShapeDtypeStruct((2, AR, 256), BF),
        jax.ShapeDtypeStruct((2, 128, 256), BF),
        jax.ShapeDtypeStruct((C, D), BF),
        jax.ShapeDtypeStruct((8, D), F32),
    ]
    names = INPUTS + OUTPUTS + list(scratch)
    layer, words, chars, ffn, att, chr_grad, pool, gain = pl.pallas_call(
        functools.partial(layer_kernel, nz, names),
        out_shape=out_shape,
        in_specs=[any_space] * len(INPUTS),
        out_specs=[any_space] * len(OUTPUTS),
        scratch_shapes=list(scratch.values()),
        compiler_params=pltpu.CompilerParams(
            collective_id=0, has_side_effects=True, vmem_limit_bytes=62 << 20
        ),
    )(*[given[name] for name in INPUTS])

    ffn, att, chr_grad = ffn.astype(F32), att.astype(F32), chr_grad.astype(F32)
    grad_ffn_up = jnp.concatenate([ffn[0, :512], ffn[1, :512]], axis=1)
    grad_ffn_down = jnp.concatenate(
        [jnp.concatenate([ffn[i, 512:768], ffn[i, 768:1024]], axis=1) for i in range(2)], axis=0
    )
    both = lambda a, b: jnp.concatenate([att[0, :, a:b], att[1, :, a:b]], axis=1)
    grad_attn_proj = jnp.stack([both(0, 64), both(128, 192), both(192, 256)])
    grad_attn_out = both(64, 128).T
    merged = chr_grad.reshape(C, 256)
    grad_char_proj = jnp.stack([merged[:, 0:64], merged[:, 64:128], merged[:, 192:256]])
    grad_char_out = merged[:, 128:192].T
    return (
        layer, words, chars,
        gain[2, 256:512], grad_char_proj, grad_char_out,
        gain[2, 0:256], pool.astype(F32),
        gain[1], grad_attn_proj, grad_attn_out,
        gain[0], grad_ffn_up, grad_ffn_down,
    )


def solution(mesh):
    nz = mesh.shape["seq"] // 2
    placed = (
        P("seq", None),
        P("seq", None, None),
        P("seq"),
        P("seq"),
        P("seq", None),
        P(),
        P(None, None, "head"),
        P("head", None),
        P(),
        P(),
        P(),
        P(None, None, "head"),
        P("head", None),
        P(),
        P(None, "head"),
        P("head", None),
    )
    return jax.shard_map(
        functools.partial(per_device, nz),
        mesh=mesh,
        in_specs=placed,
        out_specs=(
            P("seq", None),
            P("seq", None),
            P(("seq", "head"), None, None),
            P(),
            P(None, None, "head"),
            P("head", None),
            P(),
            P(),
            P(),
            P(None, None, "head"),
            P("head", None),
            P(),
            P(None, "head"),
            P("head", None),
        ),
        check_vma=False,
    )
```

```python
import functools
from types import SimpleNamespace

import jax
import jax.numpy as jnp
from jax import lax
from jax.experimental import pallas as pl
from jax.experimental.pallas import tpu as pltpu
from jax.sharding import PartitionSpec as P

MESH = pl.DeviceIdType.MESH
BF = jnp.bfloat16
F32 = jnp.float32
EPSILON = 1e-06
NEGATIVE = -1e30

D = 512
C = 256
L = 16
G = 4
Q = 128
W = G * Q
PW = 2 * W
R = Q * L
FS = 512
GROUPS = R // 128
KU = 512
MARKS = 8
SLOTS = 8
FR = 1024
AR = 512

INPUTS = [
    "word_input",
    "char_input",
    "char_count",
    "document_ids",
    "output_grad",
    "char_gain",
    "char_proj",
    "char_out",
    "pool_gain",
    "pool_proj",
    "attn_gain",
    "attn_proj",
    "attn_out",
    "ffn_gain",
    "ffn_up",
    "ffn_down",
]
OUTPUTS = ["o_layer", "o_words", "o_chars", "o_ffn", "o_att", "o_chr", "o_pool", "o_gain"]


def dot(a, b):
    return lax.dot_general(a, b, (((1,), (0,)), ((), ())), preferred_element_type=F32)


def dot_t(a, b):
    return lax.dot_general(a, b, (((1,), (1,)), ((), ())), preferred_element_type=F32)


def dot_l(a, b):
    return lax.dot_general(a, b, (((0,), (0,)), ((), ())), preferred_element_type=F32)


def bdot(a, b):
    return lax.dot_general(a, b, (((2,), (1,)), ((0,), (0,))), preferred_element_type=F32)


def bdot_t(a, b):
    return lax.dot_general(a, b, (((2,), (2,)), ((0,), (0,))), preferred_element_type=F32)


def bdot_l(a, b):
    return lax.dot_general(a, b, (((1,), (1,)), ((0,), (0,))), preferred_element_type=F32)


def iota(shape, axis):
    return lax.broadcasted_iota(jnp.int32, shape, axis)


def swap(a):
    return pltpu.roll(a, 64, 1)


def rms_factor(values):
    return lax.rsqrt(jnp.mean(values * values, axis=-1, keepdims=True) + EPSILON)


def rms_back(upstream, values, gain):
    factor = rms_factor(values)
    unit = values * factor
    scaled = upstream * gain
    centre = jnp.mean(scaled * unit, axis=-1, keepdims=True)
    return factor * (scaled - unit * centre), jnp.sum(upstream * unit, axis=0, keepdims=True)


def scratch_list(nz):
    n = 2 * nz
    vm = pltpu.VMEM
    dma = pltpu.SemaphoreType.DMA
    return dict(
        xin=vm((Q, L, C), BF),
        cnt=vm((G, 128), jnp.int32),
        docs=vm((n, G, 128), jnp.int32),
        cpr=vm((3, 64, C), BF),
        win=vm((Q, D), BF),
        ogp=vm((2, W, D), BF),
        cg=vm((1, C), F32),
        pg=vm((1, C), F32),
        ag=vm((1, D), F32),
        fg=vm((1, D), F32),
        cw=vm((G, C, 256), BF),
        cwt=vm((G, C, 256), BF),
        co=vm((G, 128, C), BF),
        pw=vm((C, D), BF),
        aw=vm((G, 3, D, 128), BF),
        ao=vm((G, 128, D), BF),
        fu=vm((G, D, FS), BF),
        fd=vm((G, FS, D), BF),
        low=vm((R, C), BF),
        cntm=vm((128, 128), F32),
        share=vm((GROUPS, 8, 128), F32),
        shc=vm((R, 128), F32),
        msel=vm((GROUPS, 16, 128), BF),
        live=vm((GROUPS, 128, 128), BF),
        took=vm((G if nz <= 8 else 1, R, 128), BF),
        bias=vm((GROUPS, 128, 128), BF),
        kq=vm((G, R, 256), BF),
        pt=vm((G, GROUPS, 128, 128), BF),
        pooled=vm((G, Q, 128), F32),
        gp=vm((G, Q, 128), F32),
        mean=vm((Q, C), F32),
        summ=vm((Q, C), F32),
        plow=vm((Q, C), BF),
        hid=vm((Q, D), F32),
        alow=vm((Q, D), BF),
        sec=vm((Q, D), F32),
        flow=vm((Q, D), BF),
        lay=vm((Q, D), BF),
        fsum=vm((Q, D), F32),
        lsum=vm((Q, D), F32),
        gsec=vm((Q, D), F32),
        gb=vm((Q, D), BF),
        gw=vm((Q, D), BF),
        gsum=vm((Q, C), F32),
        wsel=vm((D, 256), BF),
        kv=vm((nz * PW, 128), BF),
        marks=vm((min(n, MARKS) * KU, 128), BF),
        qd=vm((PW, 256), BF),
        top=vm((8, PW), F32),
        total=vm((8, PW), F32),
        lse=vm((8, PW), F32),
        delta=vm((8, PW), F32),
        acct=vm((128, PW), F32),
        out=vm((PW, 128), F32),
        ob=vm((PW, 128), BF),
        smx=vm((8, 64, 128), BF),
        rmx=vm((8, 64, 128), BF),
        sgm=vm((8, 64, 128), BF),
        rgm=vm((8, 64, 128), BF),
        gz=vm((PW, 128), BF),
        xg=vm((PW, 128), BF),
        dkv=vm((PW, 128), F32),
        sdk=vm((min(n, SLOTS), KU, 128), BF),
        rdk=vm((n, KU, 128), BF),
        dqb=vm((PW, 128), BF),
        sdkv=vm((8, Q, 128), BF),
        rdkv=vm((8, Q, 128), BF),
        sdq=vm((8, 64, 128), BF),
        rdq=vm((8, 64, 128), BF),
        alp=vm((PW, D), BF),
        flp=vm((PW, D), BF),
        gbp=vm((PW, D), BF),
        sag=vm((8, Q, 512), BF),
        rag=vm((PW, 512), BF),
        fw=vm((FR, 256), BF),
        frs=vm((nz, FR // nz, 256), BF),
        ffin=vm((FR // nz, 256), BF),
        aw_g=vm((AR, 256), BF),
        ars=vm((nz, AR // nz, 256), BF),
        afin=vm((AR // nz, 256), BF),
        scw=vm((G, C, 256), BF),
        rcw=vm((8, 128, 256), BF),
        zcw=vm((nz, 128, 256), BF),
        cfin=vm((128, 256), BF),
        spw=vm((C, D), BF),
        rpw=vm((8, 32, D), BF),
        zpw=vm((nz, 32, D), BF),
        pfin=vm((32, D), BF),
        gn=vm((8, D), F32),
        rgn=vm((8, 8, D), F32),
        zgn=vm((nz, 8, D), F32),
        gnf=vm((8, D), F32),
        lsem=dma((24,)),
        wg_s=dma((2, 3)),
        wg_r=dma((2, 3)),
        ws_s=dma((4, 5)),
        ws_r=dma((4, 5)),
        og_s=dma((2,)),
        og_r=dma((2,)),
        mx_s=dma((8,)),
        mx_r=dma((8,)),
        gm_s=dma((8,)),
        gm_r=dma((8,)),
        dkv_s=dma((8,)),
        dkv_r=dma((8,)),
        dq_s=dma((8,)),
        dq_r=dma((8,)),
        al_s=dma((8,)),
        al_r=dma((8,)),
        fl_s=dma((8,)),
        fl_r=dma((8,)),
        gb_s=dma((8,)),
        gb_r=dma((8,)),
        ac_s=dma((8,)),
        ac_r=dma((8,)),
        cw_s=dma((8,)),
        cw_r=dma((8,)),
        pw_s=dma((8,)),
        pw_r=dma((8,)),
        pa_s=dma((8,)),
        pa_r=dma((8,)),
        gn_s=dma((8,)),
        gn_r=dma((8,)),
        kz_s=dma((n,)),
        kz_r=dma((n,)),
        dz_s=dma((nz,)),
        dz_r=dma((nz,)),
        x_s=dma((5,)),
        x_r=dma((5,)),
        dk_s=dma((n,)),
        dk_r=dma((n,)),
        xf_s=dma((nz,)),
        xf_r=dma((nz,)),
        xa_s=dma((nz,)),
        xa_r=dma((nz,)),
        fr_s=dma((nz,)),
        fr_r=dma((nz,)),
        fa_s=dma((nz,)),
        fa_r=dma((nz,)),
        ar_s=dma((nz,)),
        ar_r=dma((nz,)),
        aa_s=dma((nz,)),
        aa_r=dma((nz,)),
        cz_s=dma((nz,)),
        cz_r=dma((nz,)),
        pz_s=dma((nz,)),
        pz_r=dma((nz,)),
        gz_s=dma((nz,)),
        gz_r=dma((nz,)),
        ly_s=dma((4,)),
        ly_r=dma((4,)),
        gw_s=dma((4,)),
        gw_r=dma((4,)),
    )


def rows(index, size):
    return pl.ds(pl.multiple_of(index * size, size), size)


def layer_kernel(nz, names, *refs):
    r = SimpleNamespace(**dict(zip(names, refs)))
    s = lax.axis_index("seq")
    h = lax.axis_index("head")
    x, z = lax.rem(s, 2), lax.div(s, 2)
    y, c = lax.div(h, 2), lax.rem(h, 2)
    p = 4 * x + h
    sends = []

    def peer(mask):
        px = 1 - x if mask & 4 else x
        py = 1 - y if mask & 2 else y
        pc = 1 - c if mask & 1 else c
        ph = 2 * py + pc
        return (2 * z + px, ph), 4 * px + ph

    def plane(t):
        pz = lax.rem(z + t, nz)
        return (2 * pz + x, h), pz

    def remote(src, dst, ssem, rsem, device):
        return pltpu.make_async_remote_copy(
            src_ref=src, dst_ref=dst, send_sem=ssem, recv_sem=rsem,
            device_id=device, device_id_type=MESH,
        )

    def send(src, dst, ssem, rsem, device):
        copy = remote(src, dst, ssem, rsem, device)
        copy.start()
        sends.append(copy)

    def arrive(dst, ssem, rsem):
        remote(dst, dst, ssem, rsem, peer(1)[0]).wait_recv()

    def load(src, dst, k):
        copy = pltpu.make_async_copy(src, dst, r.lsem.at[k])
        copy.start()
        return copy

    low_half = iota((1, 128), 1) < 64

    def pick(a, b):
        shape = a.shape
        return jnp.where(iota(shape, 1) < 64, a, b)

    def pack(a):
        return pick(a[:64], swap(a[64:]))

    def pack_high(a):
        return pick(swap(a[:64]), a[64:])

    barrier = pltpu.get_barrier_semaphore()
    for mask in range(1, 8):
        pl.semaphore_signal(barrier, inc=1, device_id=peer(mask)[0], device_id_type=MESH)
    for t in range(1, nz):
        pl.semaphore_signal(barrier, inc=1, device_id=plane(t)[0], device_id_type=MESH)

    ld_x = load(r.char_input.at[rows(h, Q)], r.xin, 0)
    ld_cg = load(r.char_gain, r.cg, 1)
    ld_cnt = load(r.char_count, r.cnt, 2)
    ld_cp = load(r.char_proj, r.cpr, 3)
    ld_doc = load(r.document_ids, r.docs.at[s], 4)
    ld_co = load(r.char_out, r.co.at[h, pl.ds(64, 64)], 5)
    ld_pw = load(r.pool_proj, r.pw, 6)
    ld_word = load(r.word_input.at[rows(h, Q)], r.win, 7)
    ld_pg = load(r.pool_gain, r.pg, 8)
    ld_ag = load(r.attn_gain, r.ag, 9)
    ld_fg = load(r.ffn_gain, r.fg, 10)
    ld_aw = load(r.attn_proj, r.aw.at[h], 11)
    ld_ao = load(r.attn_out, r.ao.at[h], 12)
    ld_og = load(r.output_grad, r.ogp.at[x], 13)
    ld_fu = load(r.ffn_up, r.fu.at[h], 14)
    ld_fd = load(r.ffn_down, r.fd.at[h], 15)

    r.co[:, 0:64, :] = jnp.zeros((G, 64, C), BF)

    ld_cp.wait()
    place = (iota((64, 128), 0) == iota((64, 128), 1)).astype(F32).astype(BF)
    place_high = (iota((64, 128), 0) + 64 == iota((64, 128), 1)).astype(F32).astype(BF)
    wq, wk, wv = r.cpr[0], r.cpr[1], r.cpr[2]
    r.cw[h, :, 0:128] = (dot_l(wk, place) + dot_l(wq, place_high)).astype(BF)
    r.cw[h, :, 128:256] = (dot_l(wq, place) + dot_l(wv, place_high)).astype(BF)

    ld_x.wait()
    ld_cg.wait()

    def char_norm(i, carry):
        values = r.xin[pl.ds(i * 32, 32)].astype(F32).reshape(512, C)
        r.low[rows(i, 512), :] = (values * rms_factor(values) * r.cg[...]).astype(BF)
        return carry

    lax.fori_loop(0, R // 512, char_norm, 0)

    ld_cnt.wait()
    count_row = jnp.broadcast_to(r.cnt[pl.ds(h, 1), :].astype(F32), (128, 128))
    r.cntm[...] = count_row.T

    def char_masks(g, carry):
        eight = r.cntm[rows(g, 8), :]
        lane8 = iota((8, 128), 1)
        of_lane = jnp.sum(
            jnp.where(iota((8, 128), 0) == lax.div(lane8, L), eight, 0.0), axis=0, keepdims=True
        )
        lane16 = iota((16, 128), 1)
        count16 = jnp.broadcast_to(of_lane, (16, 128))
        letter16 = lax.rem(lane16, L).astype(F32)
        r.share[g] = jnp.where(letter16 < count16, 1.0 / count16, 0.0)[:8]
        r.msel[g] = jnp.where(
            (iota((16, 128), 0) == lax.div(lane16, L)) & (letter16 < count16), 1.0, 0.0
        ).astype(BF)
        row, lane = iota((128, 128), 0), iota((128, 128), 1)
        spread = jnp.where(lane == g * 8 + lax.div(row, L), 1.0, 0.0).astype(BF)
        count = dot(spread, r.cntm[...].astype(BF))
        valid = lax.rem(row, L).astype(F32) < count
        r.bias[g] = jnp.where(
            valid & (lax.div(row, L) == lax.div(lane, L)), 0.0, NEGATIVE
        ).astype(BF)
        r.shc[rows(g, 128), :] = jnp.where(valid, 1.0 / count, 0.0)
        r.live[g] = jnp.where(valid, 1.0, 0.0).astype(BF)
        return carry

    lax.fori_loop(0, GROUPS, char_masks, 0, unroll=4)

    pl.semaphore_wait(barrier, 7 + nz - 1)

    def gather_start(k, slots):
        mine = slots(h)
        send(mine, mine, r.wg_s.at[k, 0], r.wg_r.at[k, 0], peer(1)[0])
        send(mine, mine, r.wg_s.at[k, 1], r.wg_r.at[k, 1], peer(2)[0])

    def gather_forward(k, slots):
        far = slots(2 * (1 - y) + c)
        arrive(far, r.wg_s.at[k, 1], r.wg_r.at[k, 1])
        send(far, far, r.wg_s.at[k, 2], r.wg_r.at[k, 2], peer(1)[0])

    def gather_near(k, slots):
        arrive(slots(2 * y + 1 - c), r.wg_s.at[k, 0], r.wg_r.at[k, 0])

    def gather_last(k, slots):
        arrive(slots(2 * (1 - y) + 1 - c), r.wg_s.at[k, 2], r.wg_r.at[k, 2])

    def share_start(k, full, part):
        send(full(h), full(h), r.ws_s.at[k, 0], r.ws_r.at[k, 0], peer(1)[0])
        send(part(h, x), part(h, x), r.ws_s.at[k, 1], r.ws_r.at[k, 1], peer(2)[0])

    def share_middle(k, full, part):
        mine = part(2 * (1 - y) + c, x)
        arrive(mine, r.ws_s.at[k, 1], r.ws_r.at[k, 1])
        send(mine, mine, r.ws_s.at[k, 2], r.ws_r.at[k, 2], peer(4)[0])
        send(mine, mine, r.ws_s.at[k, 3], r.ws_r.at[k, 3], peer(1)[0])

    def share_end(k, full, part):
        other = part(2 * (1 - y) + c, 1 - x)
        arrive(other, r.ws_s.at[k, 2], r.ws_r.at[k, 2])
        send(other, other, r.ws_s.at[k, 4], r.ws_r.at[k, 4], peer(1)[0])

    def share_near(k, full, part):
        arrive(full(2 * y + 1 - c), r.ws_s.at[k, 0], r.ws_r.at[k, 0])

    def share_last(k, full, part):
        far = 2 * (1 - y) + 1 - c
        arrive(part(far, x), r.ws_s.at[k, 3], r.ws_r.at[k, 3])
        arrive(part(far, 1 - x), r.ws_s.at[k, 4], r.ws_r.at[k, 4])

    def fan_start(src, slots, ssem, rsem):
        for mask in (1, 2, 4, 6):
            send(src, slots.at[rows(p, Q)], ssem.at[mask], rsem.at[mask], peer(mask)[0])
        slots[rows(p, Q), :] = src[...]

    def fan_forward(slots, ssem, rsem):
        for mask in (2, 4, 6):
            got = slots.at[rows(peer(mask)[1], Q)]
            arrive(got, ssem.at[mask], rsem.at[mask])
            send(got, got, ssem.at[mask + 1], rsem.at[mask + 1], peer(1)[0])

    def fan_last(slots, ssem, rsem):
        for mask in (1, 3, 5, 7):
            arrive(slots.at[rows(peer(mask)[1], Q)], ssem.at[mask], rsem.at[mask])

    def head_rows_start(src, out, ssem, rsem):
        for mask in (1, 2):
            send(src, out.at[rows(h, Q)], ssem.at[mask], rsem.at[mask], peer(mask)[0])

    def head_rows_forward(out, ssem, rsem):
        got = out.at[rows(2 * (1 - y) + c, Q)]
        arrive(got, ssem.at[2], rsem.at[2])
        send(got, got, ssem.at[3], rsem.at[3], peer(1)[0])

    def head_rows_last(out, ssem, rsem):
        arrive(out.at[rows(2 * y + 1 - c, Q)], ssem.at[1], rsem.at[1])
        arrive(out.at[rows(2 * (1 - y) + 1 - c, Q)], ssem.at[3], rsem.at[3])

    order = [h, 2 * y + 1 - c, 2 * (1 - y) + c, 2 * (1 - y) + 1 - c]
    cw_at = lambda i: r.cw.at[i]
    co_at = lambda i: r.co.at[i, pl.ds(64, 64)]
    sh_aw = (0, lambda i: r.aw.at[i], lambda i, j: r.aw.at[i, :, rows(j, D // 2)])
    sh_ao = (1, lambda i: r.ao.at[i], lambda i, j: r.ao.at[i, rows(j, 64)])
    sh_fu = (2, lambda i: r.fu.at[i], lambda i, j: r.fu.at[i, rows(j, D // 2)])
    sh_fd = (3, lambda i: r.fd.at[i], lambda i, j: r.fd.at[i, rows(j, FS // 2)])

    gather_start(0, cw_at)
    ld_co.wait()
    gather_start(1, co_at)
    ld_doc.wait()
    send(r.docs.at[s], r.docs.at[s], r.x_s.at[0], r.x_r.at[0], peer(4)[0])
    ld_ao.wait()
    share_start(*sh_ao)
    ld_fu.wait()
    share_start(*sh_fu)
    ld_og.wait()
    og_half = lambda i, j: r.ogp.at[i, rows(j, W // 2)]
    send(og_half(x, c), og_half(x, c), r.og_s.at[0], r.og_r.at[0], peer(4)[0])

    lane_scale = jnp.where((iota((1, 256), 1) < 64) | (iota((1, 256), 1) >= 192), 1.0, 0.125)
    keep_low = jnp.where(low_half, 1.0, 0.0)
    keep_high = 1.0 - keep_low

    def char_head(hh):
        for i in range(2):
            part = pl.ds(i * (R // 2), R // 2)
            r.kq[hh, part, :] = (dot(r.low[part, :], r.cw[hh]) * lane_scale).astype(BF)
        kq = r.kq[hh, :, 0:128].reshape(GROUPS, 128, 128)
        qv = r.kq[hh, :, 128:256].astype(F32)
        query = (qv * keep_low).astype(BF).reshape(GROUPS, 128, 128)
        scores = bdot_t(kq, query) + r.bias[...].astype(F32)
        raised = jnp.exp(scores - jnp.max(scores, axis=1, keepdims=True))
        weights = (raised * (1.0 / jnp.sum(raised, axis=1, keepdims=True))).astype(BF)
        r.pt[hh] = weights
        took = bdot(weights, r.live[...]).reshape(R, 128)
        if nz <= 8:
            r.took[hh] = took.astype(BF)
        got = jnp.sum((took * qv).reshape(Q, L, 128), axis=1)
        r.pooled[hh] = got * (1.0 / r.cntm[...]) * keep_high

    ld_aw.wait()
    first, other = r.aw[h, 0].astype(F32), r.aw[h, 1].astype(F32)
    third = r.aw[h, 2].astype(F32)
    even = x == 0
    r.wsel[:, 0:128] = (jnp.where(even, first, swap(first)) * 0.125 * keep_low).astype(BF)
    r.wsel[:, 128:256] = jnp.where(even, pick(other, swap(third)), pick(swap(other), third)).astype(BF)
    char_head(h)
    gather_near(0, cw_at)
    gather_forward(0, cw_at)
    gather_forward(1, co_at)
    gather_last(0, cw_at)

    def other_head(t, carry):
        char_head(lax.rem(h + t, G))
        return carry

    lax.fori_loop(1, G, other_head, 0)

    def char_mean(g, carry):
        block = r.xin[pl.ds(g * 8, 8)].reshape(128, C)
        r.mean[rows(g, 8), :] = dot(r.msel[g], block)[:8] * (1.0 / r.cntm[rows(g, 8), 0:1])
        return carry

    lax.fori_loop(0, GROUPS, char_mean, 0, unroll=4)
    gather_near(1, co_at)
    gather_last(1, co_at)
    summary = r.mean[...]
    for hh in range(G):
        summary = summary + dot(r.pooled[hh].astype(BF), r.co[hh])
    r.summ[...] = summary
    ld_pg.wait()
    ld_pw.wait()
    ld_word.wait()
    ld_ag.wait()
    r.plow[...] = (summary * rms_factor(summary) * r.pg[...]).astype(BF)
    hidden = r.win[...].astype(F32) + dot(r.plow[...], r.pw[...])
    r.hid[...] = hidden
    r.alow[...] = (hidden * rms_factor(hidden) * r.ag[...]).astype(BF)

    fan_start(r.alow, r.alp, r.al_s, r.al_r)
    ld_fd.wait()
    share_start(*sh_fd)
    kv_mine = rows(z, PW)

    arrive(r.docs.at[2 * z + 1 - x], r.x_s.at[0], r.x_r.at[0])
    docs_mine = r.docs.at[pl.ds(2 * z, 2)]

    def docs_copy(t, source):
        return remote(
            r.docs.at[pl.ds(2 * source, 2)], r.docs.at[pl.ds(2 * source, 2)],
            r.dz_s.at[t], r.dz_r.at[source], (2 * lax.rem(z + t, nz) + x, h),
        )

    for t in range(1, nz):
        @pl.when(z + t < nz)
        def _():
            docs_copy(t, z).start()

    def key_marks(chunk, carry):
        row = r.docs[lax.div(chunk, 4), pl.ds(lax.rem(chunk, 4), 1), :]
        sub = iota((128, 128), 0)
        marks = jnp.where((sub < 3) & (jnp.broadcast_to(row, (128, 128)) != sub), 1.0, 0.0)
        slot = lax.rem(chunk, 4 * min(2 * nz, MARKS))
        r.marks[rows(slot, 128), :] = marks.T.astype(BF)
        return carry

    def query_marks(chunk, carry):
        row = r.docs[lax.div(z * 8 + chunk, 4), pl.ds(lax.rem(chunk, 4), 1), :]
        sub = iota((128, 128), 0)
        marks = jnp.where((sub < 3) & (jnp.broadcast_to(row, (128, 128)) == sub), NEGATIVE, 0.0)
        r.qd[rows(chunk, 128), 128:256] = marks.T.astype(BF)
        return carry

    lax.fori_loop(z * 8, z * 8 + 8, key_marks, 0)
    lax.fori_loop(0, 8, query_marks, 0)
    r.top[...] = jnp.full((8, PW), NEGATIVE, F32)
    r.total[...] = jnp.zeros((8, PW), F32)
    r.acct[...] = jnp.zeros((128, PW), F32)
    fan_forward(r.alp, r.al_s, r.al_r)
    fan_last(r.alp, r.al_s, r.al_r)
    mapped = dot(r.alp[...], r.wsel[...])
    r.qd[:, 0:128] = mapped[:, 0:128].astype(BF)
    r.kv[kv_mine, :] = mapped[:, 128:256].astype(BF)

    def unit_copy(u):
        block = r.kv.at[rows(u, KU)]
        return remote(
            block, block, r.kz_s.at[u], r.kz_r.at[u], (2 * lax.rem(z + 1, nz) + x, h)
        )

    @pl.when(z + 1 < nz)
    def _():
        unit_copy(2 * z).start()
        unit_copy(2 * z + 1).start()

    share_middle(*sh_ao)
    share_middle(*sh_fu)
    share_end(*sh_ao)
    arrive(og_half(1 - x, c), r.og_s.at[0], r.og_r.at[0])
    send(og_half(1 - x, c), og_half(1 - x, c), r.og_s.at[1], r.og_r.at[1], peer(1)[0])

    def marked(kv, u):
        marks = r.marks[rows(lax.rem(u, min(2 * nz, MARKS)), KU), :]
        return jnp.concatenate([kv, marks], axis=1)

    def mark_again(u):
        if 2 * nz > MARKS:
            lax.fori_loop(4 * u, 4 * u + 4, key_marks, 0)

    def forward_tile(u, start, causal):
        at = pl.ds(start, PW - start)
        kv = r.kv[rows(u, KU), :]
        scores = dot_t(marked(kv, u), r.qd[at, :])
        if causal:
            gap = iota(scores.shape, 1) - iota(scores.shape, 0)
            scores = jnp.where(gap >= 0, scores, NEGATIVE)
        old = r.top[0:1, at]
        new = jnp.maximum(old, jnp.max(scores, axis=0, keepdims=True))
        raised = jnp.exp(scores - new)
        fade = jnp.exp(old - new)
        r.top[0:1, at] = new
        r.total[0:1, at] = r.total[0:1, at] * fade + jnp.sum(raised, axis=0, keepdims=True)
        turned = kv.astype(F32).T.astype(BF)
        r.acct[:, at] = r.acct[:, at] * fade + dot(turned, raised.astype(BF))

    forward_tile(2 * z, 0, True)
    forward_tile(2 * z + 1, KU, True)

    def wait_docs(source, carry):
        docs_copy(1, source).wait_recv()
        return carry

    lax.fori_loop(0, z, wait_docs, 0)
    if 2 * nz <= MARKS:
        lax.fori_loop(0, z * 8, key_marks, 0)

    def forward_unit(i, carry):
        u = 2 * z - 1 - i
        unit_copy(u).wait_recv()
        mark_again(u)

        @pl.when(z + 1 < nz)
        def _():
            unit_copy(u).start()

        forward_tile(u, 0, False)
        return carry

    lax.fori_loop(0, jnp.minimum(2 * z, 2), forward_unit, 0)
    share_middle(*sh_fd)
    share_end(*sh_fu)
    lax.fori_loop(jnp.minimum(2 * z, 2), 2 * z, forward_unit, 0)
    share_end(*sh_fd)

    r.lse[0:1, :] = r.top[0:1, :] + jnp.log(r.total[0:1, :])
    over = 1.0 / r.total[0:1, :]
    for i in range(8):
        cols = slice(i * 128, i * 128 + 128)
        out = (r.acct[:, cols] * over[:, cols]).T * keep_high
        r.out[cols, :] = out
        r.ob[cols, :] = out.astype(BF)
        r.smx[i] = pack_high(out).astype(BF)
    for mask in range(1, 8):
        device, to = peer(mask)
        send(r.smx.at[to], r.rmx.at[p], r.mx_s.at[mask], r.mx_r.at[mask], device)
    r.rmx[p] = r.smx[p]
    share_near(*sh_ao)
    share_last(*sh_ao)
    ld_fg.wait()
    for mask in range(1, 8):
        arrive(r.rmx.at[peer(mask)[1]], r.mx_s.at[mask], r.mx_r.at[mask])

    def two_heads(a, b):
        a, b = a.astype(F32), b.astype(F32)
        return jnp.concatenate([pick(a, swap(b)), pick(swap(a), b)], axis=0).astype(BF)

    second = r.hid[...]
    for hh in range(G):
        second = second + dot(two_heads(r.rmx[hh], r.rmx[4 + hh]), r.ao[hh])
    r.sec[...] = second
    r.flow[...] = (second * rms_factor(second) * r.fg[...]).astype(BF)

    fan_start(r.flow, r.flp, r.fl_s, r.fl_r)

    grad_rows = r.ogp[x, rows(h, Q), :]
    r.fsum[...] = jnp.zeros((Q, D), F32)
    for t in range(G):
        hh = order[t]
        if t == 1:
            share_near(*sh_fu)
            share_near(*sh_fd)
        if t == 3:
            share_last(*sh_fu)
            share_last(*sh_fd)
        upward = dot(r.flow[...], r.fu[hh])
        square = upward * upward
        inner = 0.7978845608028654 * upward * (1.0 + 0.044715 * square)
        bent = jnp.tanh(inner)
        half_up = 0.5 * (1.0 + bent)
        active = (upward * half_up).astype(BF)
        slope = half_up + 0.5 * upward * (1.0 - bent * bent) * (
            0.7978845608028654 * (1.0 + 0.134145 * square)
        )
        grad_up = (dot_t(grad_rows, r.fd[hh]) * slope).astype(BF)
        r.fsum[...] += dot_t(grad_up, r.fu[hh])
        r.sag[hh, :, 0:256] = active[:, 0:256]
        r.sag[hh, :, 256:512] = grad_up[:, 0:256]
        r.sag[4 + hh, :, 0:256] = active[:, 256:512]
        r.sag[4 + hh, :, 256:512] = grad_up[:, 256:512]
    back, gain_ffn = rms_back(r.fsum[...], r.sec[...], r.fg[...])
    grad_second = grad_rows.astype(F32) + back
    r.gsec[...] = grad_second
    r.gb[...] = grad_second.astype(BF)
    r.gn[0:1, :] = gain_ffn

    for t in range(G):
        hh = order[t]
        grad = dot_t(r.gb[...], r.ao[hh])
        r.sgm[hh] = pack(grad).astype(BF)
        r.sgm[4 + hh] = pack_high(grad).astype(BF)
        for mask in ((4,) if t == 0 else (t, t + 4)):
            device, to = peer(mask)
            send(r.sgm.at[to], r.rgm.at[p], r.gm_s.at[mask], r.gm_r.at[mask], device)
    r.rgm[p] = r.sgm[p]
    for mask in range(1, 8):
        device, to = peer(mask)
        send(r.sag.at[to], r.rag.at[rows(p, Q)], r.ac_s.at[mask], r.ac_r.at[mask], device)
    r.rag[rows(p, Q), :] = r.sag[p]
    r.acct[...] = jnp.zeros((128, PW), F32)
    r.lsum[...] = r.sec[...]

    def layer_part(hh, carry):
        r.lsum[...] += dot(r.sag[hh, :, 0:256], r.fd[hh, 0:256, :])
        r.lsum[...] += dot(r.sag[4 + hh, :, 0:256], r.fd[hh, 256:512, :])
        return carry

    lax.fori_loop(0, G, layer_part, 0)
    r.lay[...] = r.lsum[...].astype(BF)
    for mask in range(1, 8):
        arrive(r.rgm.at[peer(mask)[1]], r.gm_s.at[mask], r.gm_r.at[mask])

    for i in range(8):
        cols = slice(i * 128, i * 128 + 128)
        got = r.rgm[i].astype(F32)
        grad = jnp.concatenate([swap(got), got], axis=0) * keep_high
        r.gz[cols, :] = grad.astype(BF)
        r.xg[cols, :] = pick(r.qd[cols, 0:128].astype(F32), grad).astype(BF)
        r.delta[0:1, cols] = jnp.sum((grad * r.out[cols, :]).T, axis=0, keepdims=True)

    fan_start(r.gb, r.gbp, r.gb_s, r.gb_r)
    share_start(*sh_aw)
    head_rows_start(r.lay, r.o_layer, r.ly_s, r.ly_r)
    fan_forward(r.flp, r.fl_s, r.fl_r)
    st_lay = load(r.lay, r.o_layer.at[rows(h, Q)], 16)

    def backward_tile(u, start, causal):
        at = pl.ds(start, PW - start)
        kv = r.kv[rows(u, KU), :]
        scores = dot_t(marked(kv, u), r.qd[at, :])
        weights = jnp.exp(scores - r.lse[0:1, at])
        if causal:
            gap = iota(scores.shape, 1) - iota(scores.shape, 0)
            weights = jnp.where(gap >= 0, weights, 0.0)
        dweights = dot_t(kv, r.gz[at, :])
        dscores = (weights * (dweights - r.delta[0:1, at])).astype(BF)
        other = r.xg[at, :]
        turned = kv.astype(F32).T.astype(BF)
        r.acct[:, at] += dot(turned, dscores)
        return pick(dot(dscores, other), dot(weights.astype(BF), other))

    last = 2 * nz <= SLOTS

    def grad_slot(u):
        return lax.rem(u, min(2 * nz, SLOTS))

    def grad_copy(u):
        return remote(
            r.sdk.at[grad_slot(u)], r.rdk.at[u], r.dk_s.at[u], r.dk_r.at[u],
            (2 * lax.rem(z + nz - 1, nz) + x, h),
        )

    def grad_join(u):
        arrive(r.rdk.at[u], r.dk_s.at[u], r.dk_r.at[u])
        slot = grad_slot(u)
        r.sdk[slot] = (r.sdk[slot].astype(F32) + r.rdk[u].astype(F32)).astype(BF)

    def backward_unit(u, carry):
        mark_again(u)
        if not last:
            @pl.when(u >= SLOTS)
            def _():
                grad_copy(u - SLOTS).wait_send()
        r.sdk[grad_slot(u)] = backward_tile(u, 0, False).astype(BF)
        if last:
            @pl.when(z == nz - 1)
            def _():
                grad_copy(u).start()
        else:
            @pl.when(z < nz - 1)
            def _():
                grad_join(u)
            grad_copy(u).start()
        return carry

    def pass_on(u, carry):
        grad_join(u)
        grad_copy(u).start()
        return carry

    lax.fori_loop(0, 2 * z, backward_unit, 0)
    if last:
        lax.fori_loop(0, jnp.where(z < nz - 1, 2 * z, 0), pass_on, 0)

    def own_units():
        for own in range(2):
            mark_again(2 * z + own)
            r.dkv[own * KU : own * KU + KU, :] = backward_tile(2 * z + own, own * KU, True)

    def all_arrive(dst, ssem, rsem):
        for mask in range(1, 8):
            arrive(dst.at[rows(peer(mask)[1], Q)], ssem.at[mask], rsem.at[mask])

    all_arrive(r.rag, r.ac_s, r.ac_r)
    fan_last(r.flp, r.fl_s, r.fl_r)
    fan_forward(r.gbp, r.gb_s, r.gb_r)
    head_rows_forward(r.o_layer, r.ly_s, r.ly_r)
    arrive(og_half(1 - x, 1 - c), r.og_s.at[1], r.og_r.at[1])
    for i in range(2):
        r.fw[i * 256 : i * 256 + 256, :] = dot_l(
            r.flp[:, i * 256 : i * 256 + 256], r.rag[:, 256:512]
        ).astype(BF)
        r.fw[512 + i * 256 : 768 + i * 256, :] = (
            dot_l(r.rag[0:W, 0:256], r.ogp[0, :, i * 256 : i * 256 + 256])
            + dot_l(r.rag[W:PW, 0:256], r.ogp[1, :, i * 256 : i * 256 + 256])
        ).astype(BF)

    def spread_start(src, size, slots, ssem, rsem):
        for t in range(1, nz):
            device, pz = plane(t)
            send(src.at[rows(pz, size)], slots.at[z], ssem.at[t], rsem.at[z], device)

    def spread_sum(src, size, slots, ssem, rsem):
        slots[z] = src[rows(z, size), :]
        for t in range(1, nz):
            pz = plane(t)[1]
            arrive(slots.at[pz], ssem.at[t], rsem.at[pz])
        total = slots[0].astype(F32)
        for i in range(1, nz):
            total = total + slots[i].astype(F32)
        return total.astype(BF)

    def final_start(src, out, size, ssem, rsem, xs, xr, lk):
        mine = out.at[x, rows(z, size)]
        for t in range(1, nz):
            send(src, mine, ssem.at[t], rsem.at[z], plane(t)[0])
        send(src, mine, xs.at[z], xr.at[z], peer(4)[0])
        return load(src, mine, lk)

    def final_cross(out, size, ssem, rsem, xs, xr):
        for t in range(1, nz):
            pz = plane(t)[1]
            part = out.at[x, rows(pz, size)]
            arrive(part, ssem.at[t], rsem.at[pz])
            send(part, part, xs.at[pz], xr.at[pz], peer(4)[0])

    def final_last(out, size, xs, xr):
        for i in range(nz):
            arrive(out.at[1 - x, rows(i, size)], xs.at[i], xr.at[i])

    spread_start(r.fw, FR // nz, r.frs, r.fr_s, r.fr_r)

    own_units()

    @pl.when(z < nz - 1)
    def _():
        for own in range(2):
            u = 2 * z + own
            arrive(r.rdk.at[u], r.dk_s.at[u], r.dk_r.at[u])
            r.dkv[own * KU : own * KU + KU, :] += r.rdk[u].astype(F32)

    for i in range(8):
        cols = slice(i * 128, i * 128 + 128)
        r.sdkv[i] = r.dkv[cols, :].astype(BF)
        grad = r.acct[:, cols].T * 0.125
        r.sdq[i] = pack(grad).astype(BF)
        r.dqb[cols, :] = (grad * keep_low).astype(BF)
    for mask in range(1, 8):
        device, to = peer(mask)
        send(r.sdkv.at[to], r.rdkv.at[p], r.dkv_s.at[mask], r.dkv_r.at[mask], device)
        send(r.sdq.at[to], r.rdq.at[p], r.dq_s.at[mask], r.dq_r.at[mask], device)
    r.rdkv[p] = r.sdkv[p]
    r.rdq[p] = r.sdq[p]

    fan_last(r.gbp, r.gb_s, r.gb_r)
    share_middle(*sh_aw)
    for i in range(2):
        cols = slice(i * 256, i * 256 + 256)
        r.aw_g[cols, 0:128] = (
            dot_l(r.alp[:, cols], r.dqb[...]) + dot_l(r.gbp[:, cols], r.ob[...])
        ).astype(BF)
        r.aw_g[cols, 128:256] = dot_l(r.alp[:, cols], r.sdkv[...].reshape(PW, 128)).astype(BF)
    spread_start(r.aw_g, AR // nz, r.ars, r.ar_s, r.ar_r)

    for mask in range(1, 8):
        arrive(r.rdkv.at[peer(mask)[1]], r.dkv_s.at[mask], r.dkv_r.at[mask])
        arrive(r.rdq.at[peer(mask)[1]], r.dq_s.at[mask], r.dq_r.at[mask])

    share_end(*sh_aw)
    share_near(*sh_aw)
    share_last(*sh_aw)

    attn_sum = jnp.zeros((Q, D), F32)
    for hh in range(G):
        first, other = r.rdkv[hh].astype(F32), r.rdkv[4 + hh].astype(F32)
        attn_sum = attn_sum + dot_t(two_heads(r.rdq[hh], r.rdq[4 + hh]), r.aw[hh, 0])
        attn_sum = attn_sum + dot_t(pick(first, swap(other)).astype(BF), r.aw[hh, 1])
        attn_sum = attn_sum + dot_t(pick(swap(first), other).astype(BF), r.aw[hh, 2])
    back, gain_attn = rms_back(attn_sum, r.hid[...], r.ag[...])
    r.gw[...] = (r.gsec[...] + back).astype(BF)
    r.gn[1:2, :] = gain_attn
    head_rows_start(r.gw, r.o_words, r.gw_s, r.gw_r)
    st_gw = load(r.gw, r.o_words.at[rows(h, Q)], 17)
    grad_summary, gain_pool = rms_back(dot_t(r.gw[...], r.pw[...]), r.summ[...], r.pg[...])
    r.gsum[...] = grad_summary
    gs_low = grad_summary.astype(BF)
    r.gn[2:3, 0:256] = gain_pool
    r.spw[...] = dot_l(r.plow[...], r.gw[...]).astype(BF)
    for mask in range(1, 8):
        device, to = peer(mask)
        send(r.spw.at[rows(to, 32)], r.rpw.at[p], r.pw_s.at[mask], r.pw_r.at[mask], device)
    r.rpw[p] = r.spw[rows(p, 32), :]

    r.ffin[...] = spread_sum(r.fw, FR // nz, r.frs, r.fr_s, r.fr_r)
    st_ffn = final_start(r.ffin, r.o_ffn, FR // nz, r.fa_s, r.fa_r, r.xf_s, r.xf_r, 18)

    ones = jnp.ones((128, 128), BF)

    def char_head_back(hh):
        r.gp[hh] = dot_t(gs_low, r.co[hh])
        w = r.cw[hh].astype(F32)
        r.cwt[hh, :, 0:128] = swap(w[:, 0:128]).astype(BF)
        r.cwt[hh, :, 128:256] = (w[:, 128:256] * keep_high).astype(BF)

        kq = r.kq[hh, :, 0:128].reshape(GROUPS, 128, 128)
        grad = jnp.broadcast_to(r.gp[hh][:, None, :], (Q, L, 128)).reshape(R, 128)
        gain = dot((r.kq[hh, :, 128:256].astype(F32) * grad).astype(BF), ones)
        gain = gain.reshape(GROUPS, 128, 128)
        weights = r.pt[hh].astype(F32)
        centre = jnp.sum(weights * gain, axis=1, keepdims=True)
        dscores = ((gain - centre) * (weights * r.share[:, 0:1, :])).astype(BF)
        dquery = (bdot_l(dscores, kq) * 0.125).reshape(R, 128)
        dkey = bdot(dscores, kq).reshape(R, 128)
        r.kq[hh, :, 0:128] = pick(dquery, dkey).astype(BF)
        if nz <= 8:
            took = r.took[hh].astype(F32)
        else:
            took = bdot(r.pt[hh], r.live[...]).reshape(R, 128)
        r.kq[hh, :, 128:256] = (took * r.shc[...] * grad).astype(BF)
        term = dot_l(r.low[...], r.kq[hh])
        pooled = swap(r.pooled[hh]).astype(BF)
        r.scw[hh, :, 0:128] = term[:, 0:128].astype(BF)
        r.scw[hh, :, 128:256] = (term[:, 128:256] + dot_l(gs_low, pooled)).astype(BF)

    def char_term(t):
        hh = order[t]
        char_head_back(hh)
        for mask in ((4,) if t == 0 else (t, t + 4)):
            device, to = peer(mask)
            px = 1 - x if mask & 4 else x
            send(
                r.scw.at[hh, rows(px, 128)], r.rcw.at[p], r.cw_s.at[mask], r.cw_r.at[mask], device
            )

    def plane_sum(slots, ssem, rsem):
        for mask in range(1, 8):
            arrive(slots.at[peer(mask)[1]], ssem.at[mask], rsem.at[mask])
        total = slots[0].astype(F32)
        for i in range(1, 8):
            total = total + slots[i].astype(F32)
        return total

    def planes_start(slots, ssem, rsem):
        for t in range(1, nz):
            send(slots.at[z], slots.at[z], ssem.at[t], rsem.at[z], plane(t)[0])

    def planes_sum(slots, ssem, rsem):
        for t in range(1, nz):
            pz = plane(t)[1]
            arrive(slots.at[pz], ssem.at[t], rsem.at[pz])
        total = slots[0].astype(F32)
        for i in range(1, nz):
            total = total + slots[i].astype(F32)
        return total

    char_term(3)

    r.afin[...] = spread_sum(r.aw_g, AR // nz, r.ars, r.ar_s, r.ar_r)
    st_att = final_start(r.afin, r.o_att, AR // nz, r.aa_s, r.aa_r, r.xa_s, r.xa_r, 19)
    head_rows_forward(r.o_words, r.gw_s, r.gw_r)

    char_term(2)
    r.zpw[z] = plane_sum(r.rpw, r.pw_s, r.pw_r).astype(BF)
    planes_start(r.zpw, r.pz_s, r.pz_r)

    char_term(1)

    char_term(0)
    r.rcw[p] = r.scw[h, rows(x, 128), :]

    def char_back(i):
        part = pl.ds(i * (R // 2), R // 2)
        words = pl.ds(i * (Q // 2), Q // 2)
        upstream = dot_t(r.kq[0, part, :], r.cwt[0])
        for hh in range(1, G):
            upstream = upstream + dot_t(r.kq[hh, part, :], r.cwt[hh])
        values = r.xin[words].astype(F32).reshape(R // 2, C)
        back, gain = rms_back(upstream, values, r.cg[...])
        of_word = jnp.broadcast_to(r.gsum[words, :][:, None, :], (Q // 2, L, C))
        full = back + r.shc[part, 0:1] * of_word.reshape(R // 2, C)
        r.xin[words] = full.astype(BF).reshape(Q // 2, L, C)
        return gain

    gain_char = char_back(0)

    r.zcw[z] = plane_sum(r.rcw, r.cw_s, r.cw_r).astype(BF)
    planes_start(r.zcw, r.cz_s, r.cz_r)
    gain_char = gain_char + char_back(1)
    st_chars = load(r.xin, r.o_chars, 20)
    r.gn[2:3, 256:512] = gain_char
    r.gn[3:8, :] = jnp.zeros((5, D), F32)
    for mask in range(1, 8):
        send(r.gn, r.rgn.at[p], r.gn_s.at[mask], r.gn_r.at[mask], peer(mask)[0])
    r.rgn[p] = r.gn[...]

    final_cross(r.o_att, AR // nz, r.aa_s, r.aa_r, r.xa_s, r.xa_r)
    final_cross(r.o_ffn, FR // nz, r.fa_s, r.fa_r, r.xf_s, r.xf_r)
    r.pfin[...] = planes_sum(r.zpw, r.pz_s, r.pz_r).astype(BF)
    for mask in range(1, 8):
        mine = r.o_pool.at[rows(p, 32)]
        send(r.pfin, mine, r.pa_s.at[mask], r.pa_r.at[mask], peer(mask)[0])
    st_pool = load(r.pfin, r.o_pool.at[rows(p, 32)], 21)
    r.zgn[z] = plane_sum(r.rgn, r.gn_s, r.gn_r)
    planes_start(r.zgn, r.gz_s, r.gz_r)
    r.cfin[...] = planes_sum(r.zcw, r.cz_s, r.cz_r).astype(BF)
    send(r.cfin, r.o_chr.at[x], r.x_s.at[4], r.x_r.at[4], peer(4)[0])
    st_chr = load(r.cfin, r.o_chr.at[x], 22)
    r.gnf[...] = planes_sum(r.zgn, r.gz_s, r.gz_r)
    st_gain = load(r.gnf, r.o_gain, 23)

    final_last(r.o_ffn, FR // nz, r.xf_s, r.xf_r)
    final_last(r.o_att, AR // nz, r.xa_s, r.xa_r)
    arrive(r.o_chr.at[1 - x], r.x_s.at[4], r.x_r.at[4])
    for mask in range(1, 8):
        arrive(r.o_pool.at[rows(peer(mask)[1], 32)], r.pa_s.at[mask], r.pa_r.at[mask])
    head_rows_last(r.o_layer, r.ly_s, r.ly_r)
    head_rows_last(r.o_words, r.gw_s, r.gw_r)
    for copy in (st_ffn, st_att, st_lay, st_gw, st_chars, st_pool, st_chr, st_gain):
        copy.wait()
    for copy in sends:
        copy.wait_send()
    for t in range(1, nz):
        @pl.when(z + t < nz)
        def _():
            docs_copy(t, z).wait_send()

    @pl.when(z + 1 < nz)
    def _():
        def sent(u, carry):
            unit_copy(u).wait_send()
            return carry

        lax.fori_loop(0, 2 * z + 2, sent, 0)

    def grads_sent(u, carry):
        grad_copy(u).wait_send()
        return carry

    lax.fori_loop(jnp.maximum(2 * z - SLOTS, 0), 2 * z, grads_sent, 0)


def per_device(nz, *arguments):
    given = dict(zip(INPUTS, arguments))
    for name in ("char_count", "document_ids"):
        given[name] = given[name].reshape(G, 128)
    given["char_proj"] = jnp.swapaxes(given["char_proj"], 1, 2)
    for name in ("char_gain", "pool_gain", "attn_gain", "ffn_gain"):
        given[name] = given[name].reshape(1, -1)
    scratch = scratch_list(nz)
    any_space = pl.BlockSpec(memory_space=pl.ANY)
    out_shape = [
        jax.ShapeDtypeStruct((W, D), BF),
        jax.ShapeDtypeStruct((W, D), BF),
        jax.ShapeDtypeStruct((Q, L, C), BF),
        jax.ShapeDtypeStruct((2, FR, 256), BF),
        jax.ShapeDtypeStruct((2, AR, 256), BF),
        jax.ShapeDtypeStruct((2, 128, 256), BF),
        jax.ShapeDtypeStruct((C, D), BF),
        jax.ShapeDtypeStruct((8, D), F32),
    ]
    names = INPUTS + OUTPUTS + list(scratch)
    layer, words, chars, ffn, att, chr_grad, pool, gain = pl.pallas_call(
        functools.partial(layer_kernel, nz, names),
        out_shape=out_shape,
        in_specs=[any_space] * len(INPUTS),
        out_specs=[any_space] * len(OUTPUTS),
        scratch_shapes=list(scratch.values()),
        compiler_params=pltpu.CompilerParams(
            collective_id=0, has_side_effects=True, vmem_limit_bytes=62 << 20
        ),
    )(*[given[name] for name in INPUTS])

    grads = [
        jax.ShapeDtypeStruct((W, D), BF),
        jax.ShapeDtypeStruct((W, D), BF),
        jax.ShapeDtypeStruct((Q, L, C), BF),
        jax.ShapeDtypeStruct((1, C), F32),
        jax.ShapeDtypeStruct((3, 64, C), F32),
        jax.ShapeDtypeStruct((64, C), F32),
        jax.ShapeDtypeStruct((1, C), F32),
        jax.ShapeDtypeStruct((C, D), F32),
        jax.ShapeDtypeStruct((1, D), F32),
        jax.ShapeDtypeStruct((3, D, 128), F32),
        jax.ShapeDtypeStruct((128, D), F32),
        jax.ShapeDtypeStruct((1, D), F32),
        jax.ShapeDtypeStruct((D, FS), F32),
        jax.ShapeDtypeStruct((FS, D), F32),
    ]
    result = pl.pallas_call(
        unpack_kernel,
        out_shape=grads,
        in_specs=[any_space] * len(out_shape),
        out_specs=[any_space] * len(grads),
        scratch_shapes=[pltpu.VMEM(a.shape, a.dtype) for a in out_shape + grads[3:]]
        + [pltpu.SemaphoreType.DMA((len(out_shape),)), pltpu.SemaphoreType.DMA((len(grads),))],
        compiler_params=pltpu.CompilerParams(vmem_limit_bytes=62 << 20),
    )(layer, words, chars, ffn, att, chr_grad, pool, gain)
    result = list(result)
    result[4] = jnp.swapaxes(result[4], 1, 2)
    for i in (3, 6, 8, 11):
        result[i] = result[i].reshape(-1)
    return tuple(result)


def unpack_kernel(*refs):
    given, out, held, made = refs[0:8], refs[8:22], refs[22:30], refs[30:41]
    in_sem, out_sem = refs[41:]
    ffn, att, chr_grad, pool, gain = held[3:]
    loads = [pltpu.make_async_copy(given[i], held[i], in_sem.at[i]) for i in range(8)]
    stores = [pltpu.make_async_copy(held[i], out[i], out_sem.at[i]) for i in range(3)]
    stores += [pltpu.make_async_copy(made[i], out[3 + i], out_sem.at[3 + i]) for i in range(11)]
    for i in (3, 4, 2, 0, 1, 6, 5, 7):
        loads[i].start()
    (g_char, g_proj, g_out, g_pool, g_pproj, g_attn, g_aproj, g_aout, g_ffn, g_up, g_down) = made

    def pick(a, b):
        return jnp.where(iota(a.shape, 1) < 64, a, b)

    loads[3].wait()
    for i in range(2):
        cols = slice(i * 256, i * 256 + 256)
        g_up[:, cols] = ffn[i, 0:512, :].astype(F32)
        g_down[cols, 0:256] = ffn[i, 512:768, :].astype(F32)
        g_down[cols, 256:512] = ffn[i, 768:1024, :].astype(F32)
    stores[12].start()
    stores[13].start()
    for i in (2, 0, 1):
        loads[i].wait()
        stores[i].start()
    loads[4].wait()
    first, other = att[0, :, 0:128].astype(F32), att[1, :, 0:128].astype(F32)
    g_aproj[0] = pick(first, swap(other))
    g_aout[...] = pick(swap(first), other).T
    first, other = att[0, :, 128:256].astype(F32), att[1, :, 128:256].astype(F32)
    g_aproj[1] = pick(first, swap(other))
    g_aproj[2] = pick(swap(first), other)
    stores[9].start()
    stores[10].start()
    loads[6].wait()
    g_pproj[...] = pool[...].astype(F32)
    stores[7].start()
    loads[5].wait()
    for i in range(2):
        cols = slice(i * 128, i * 128 + 128)
        block = chr_grad[i].astype(F32)
        first, other = block[:, 0:128].T, block[:, 128:256].T
        g_proj[0, :, cols] = first[0:64]
        g_proj[1, :, cols] = first[64:128]
        g_out[:, cols] = other[0:64]
        g_proj[2, :, cols] = other[64:128]
    stores[4].start()
    stores[5].start()
    loads[7].wait()
    g_ffn[...] = gain[0:1, :]
    g_attn[...] = gain[1:2, :]
    g_pool[...] = gain[2:3, 0:256]
    g_char[...] = gain[2:3, 256:512]
    for i in (3, 6, 8, 11):
        stores[i].start()
    for copy in stores:
        copy.wait()


def solution(mesh):
    nz = mesh.shape["seq"] // 2
    placed = (
        P("seq", None),
        P("seq", None, None),
        P("seq"),
        P("seq"),
        P("seq", None),
        P(),
        P(None, None, "head"),
        P("head", None),
        P(),
        P(),
        P(),
        P(None, None, "head"),
        P("head", None),
        P(),
        P(None, "head"),
        P("head", None),
    )
    return jax.shard_map(
        functools.partial(per_device, nz),
        mesh=mesh,
        in_specs=placed,
        out_specs=(
            P("seq", None),
            P("seq", None),
            P(("seq", "head"), None, None),
            P(),
            P(None, None, "head"),
            P("head", None),
            P(),
            P(),
            P(),
            P(None, None, "head"),
            P("head", None),
            P(),
            P(None, "head"),
            P("head", None),
        ),
        check_vma=False,
    )
```

```python
import functools
from types import SimpleNamespace

import jax
import jax.numpy as jnp
from jax import lax
from jax.experimental import pallas as pl
from jax.experimental.pallas import tpu as pltpu
from jax.sharding import PartitionSpec as P

MESH = pl.DeviceIdType.MESH
BF = jnp.bfloat16
F32 = jnp.float32
EPSILON = 1e-06
NEGATIVE = -1e30

D = 512
C = 256
L = 16
G = 4
Q = 128
W = G * Q
PW = 2 * W
R = Q * L
FS = 512
GROUPS = R // 128
KU = 512
MARKS = 8
SLOTS = 8
FR = 1024
FEW = 8
AR = 512

INPUTS = [
    "word_input",
    "char_input",
    "char_count",
    "document_ids",
    "output_grad",
    "char_gain",
    "char_proj",
    "char_out",
    "pool_gain",
    "pool_proj",
    "attn_gain",
    "attn_proj",
    "attn_out",
    "ffn_gain",
    "ffn_up",
    "ffn_down",
]
OUTPUTS = ["o_layer", "o_words", "o_chars", "o_ffn", "o_att", "o_chr", "o_pool", "o_gain"]


def dot(a, b):
    return lax.dot_general(a, b, (((1,), (0,)), ((), ())), preferred_element_type=F32)


def dot_t(a, b):
    return lax.dot_general(a, b, (((1,), (1,)), ((), ())), preferred_element_type=F32)


def dot_l(a, b):
    return lax.dot_general(a, b, (((0,), (0,)), ((), ())), preferred_element_type=F32)


def bdot(a, b):
    return lax.dot_general(a, b, (((2,), (1,)), ((0,), (0,))), preferred_element_type=F32)


def bdot_t(a, b):
    return lax.dot_general(a, b, (((2,), (2,)), ((0,), (0,))), preferred_element_type=F32)


def bdot_l(a, b):
    return lax.dot_general(a, b, (((1,), (1,)), ((0,), (0,))), preferred_element_type=F32)


def iota(shape, axis):
    return lax.broadcasted_iota(jnp.int32, shape, axis)


def swap(a):
    return pltpu.roll(a, 64, 1)


def rms_factor(values):
    return lax.rsqrt(jnp.mean(values * values, axis=-1, keepdims=True) + EPSILON)


def rms_back(upstream, values, gain):
    factor = rms_factor(values)
    unit = values * factor
    scaled = upstream * gain
    centre = jnp.mean(scaled * unit, axis=-1, keepdims=True)
    return factor * (scaled - unit * centre), jnp.sum(upstream * unit, axis=0, keepdims=True)


def scratch_list(nz):
    n = 2 * nz
    vm = pltpu.VMEM
    dma = pltpu.SemaphoreType.DMA
    return dict(
        xin=vm((Q, L, C), BF),
        cnt=vm((G, 128), jnp.int32),
        docs=vm((n, G, 128), jnp.int32),
        cpr=vm((3, 64, C), BF),
        win=vm((Q, D), BF),
        ogp=vm((2, W, D), BF),
        cg=vm((1, C), F32),
        pg=vm((1, C), F32),
        ag=vm((1, D), F32),
        fg=vm((1, D), F32),
        cw=vm((G, C, 256), BF),
        cwt=vm((G, C, 256), BF),
        co=vm((G, 128, C), BF),
        pw=vm((C, D), BF),
        aw=vm((G, 3, D, 128), BF),
        ao=vm((G, 128, D), BF),
        fu=vm((G, D, FS), BF),
        fd=vm((G, FS, D), BF),
        low=vm((R, C), BF),
        cntm=vm((128, 128), F32),
        share=vm((GROUPS, 8, 128), F32),
        shc=vm((R, 128), F32),
        msel=vm((GROUPS, 16, 128), BF),
        live=vm((GROUPS, 128, 128), BF),
        took=vm((G if nz <= FEW else 1, R, 128), BF),
        bias=vm((GROUPS, 128, 128), BF),
        kq=vm((G, R, 256), BF),
        pt=vm((G, GROUPS, 128, 128), BF),
        pooled=vm((G, Q, 128), F32),
        gp=vm((G, Q, 128), F32),
        mean=vm((Q, C), F32),
        summ=vm((Q, C), F32),
        plow=vm((Q, C), BF),
        hid=vm((Q, D), F32),
        alow=vm((Q, D), BF),
        sec=vm((Q, D), F32),
        flow=vm((Q, D), BF),
        lay=vm((Q, D), BF),
        fsum=vm((Q, D), F32),
        lsum=vm((Q, D), F32),
        gsec=vm((Q, D), F32),
        gb=vm((Q, D), BF),
        gw=vm((Q, D), BF),
        gsum=vm((Q, C), F32),
        wsel=vm((D, 256), BF),
        kv=vm((nz * PW, 128), BF),
        marks=vm((min(n, MARKS) * KU, 128), BF),
        qd=vm((PW, 256), BF),
        top=vm((8, PW), F32),
        total=vm((8, PW), F32),
        lse=vm((8, PW), F32),
        delta=vm((8, PW), F32),
        acct=vm((128, PW), F32),
        out=vm((PW, 128), F32),
        ob=vm((PW, 128), BF),
        smx=vm((8, 64, 128), BF),
        rmx=vm((8, 64, 128), BF),
        sgm=vm((8, 64, 128), BF),
        rgm=vm((8, 64, 128), BF),
        gz=vm((PW, 128), BF),
        xg=vm((PW, 128), BF),
        dkv=vm((PW, 128), F32),
        sdk=vm((min(n, SLOTS), KU, 128), BF),
        rdk=vm((n, KU, 128), BF),
        dqb=vm((PW, 128), BF),
        sdkv=vm((8, Q, 128), BF),
        rdkv=vm((8, Q, 128), BF),
        sdq=vm((8, 64, 128), BF),
        rdq=vm((8, 64, 128), BF),
        alp=vm((PW, D), BF),
        flp=vm((PW, D), BF),
        gbp=vm((PW, D), BF),
        sag=vm((8, Q, 512), BF),
        rag=vm((PW, 512), BF),
        fw=vm((FR, 256), BF),
        frs=vm((nz, FR // nz, 256), BF),
        ffin=vm((FR // nz, 256), BF),
        aw_g=vm((AR, 256), BF),
        ars=vm((nz, AR // nz, 256), BF),
        afin=vm((AR // nz, 256), BF),
        scw=vm((G, C, 256), BF),
        rcw=vm((8, 128, 256), BF),
        zcw=vm((nz, 128, 256), BF),
        cfin=vm((128, 256), BF),
        spw=vm((C, D), BF),
        rpw=vm((8, 32, D), BF),
        zpw=vm((nz, 32, D), BF),
        pfin=vm((32, D), BF),
        gn=vm((8, D), F32),
        rgn=vm((8, 8, D), F32),
        zgn=vm((nz, 8, D), F32),
        gnf=vm((8, D), F32),
        v_layer=vm((W, D) if nz <= FEW else (16, 128), BF),
        v_words=vm((W, D) if nz <= FEW else (16, 128), BF),
        v_ffn=vm((2, FR, 256) if nz <= FEW else (16, 128), BF),
        v_att=vm((2, AR, 256) if nz <= FEW else (16, 128), BF),
        v_chr=vm((2, 128, 256) if nz <= FEW else (16, 128), BF),
        v_pool=vm((C, D) if nz <= FEW else (16, 128), BF),
        lsem=dma((32,)),
        wg_s=dma((2, 3)),
        wg_r=dma((2, 3)),
        ws_s=dma((4, 5)),
        ws_r=dma((4, 5)),
        og_s=dma((2,)),
        og_r=dma((2,)),
        mx_s=dma((8,)),
        mx_r=dma((8,)),
        gm_s=dma((8,)),
        gm_r=dma((8,)),
        dkv_s=dma((8,)),
        dkv_r=dma((8,)),
        dq_s=dma((8,)),
        dq_r=dma((8,)),
        al_s=dma((8,)),
        al_r=dma((8,)),
        fl_s=dma((8,)),
        fl_r=dma((8,)),
        gb_s=dma((8,)),
        gb_r=dma((8,)),
        ac_s=dma((8,)),
        ac_r=dma((8,)),
        cw_s=dma((8,)),
        cw_r=dma((8,)),
        pw_s=dma((8,)),
        pw_r=dma((8,)),
        pa_s=dma((8,)),
        pa_r=dma((8,)),
        gn_s=dma((8,)),
        gn_r=dma((8,)),
        kz_s=dma((n,)),
        kz_r=dma((n,)),
        dz_s=dma((nz,)),
        dz_r=dma((nz,)),
        x_s=dma((5,)),
        x_r=dma((5,)),
        dk_s=dma((n,)),
        dk_r=dma((n,)),
        xf_s=dma((nz,)),
        xf_r=dma((nz,)),
        xa_s=dma((nz,)),
        xa_r=dma((nz,)),
        fr_s=dma((nz,)),
        fr_r=dma((nz,)),
        fa_s=dma((nz,)),
        fa_r=dma((nz,)),
        ar_s=dma((nz,)),
        ar_r=dma((nz,)),
        aa_s=dma((nz,)),
        aa_r=dma((nz,)),
        cz_s=dma((nz,)),
        cz_r=dma((nz,)),
        pz_s=dma((nz,)),
        pz_r=dma((nz,)),
        gz_s=dma((nz,)),
        gz_r=dma((nz,)),
        ly_s=dma((4,)),
        ly_r=dma((4,)),
        gw_s=dma((4,)),
        gw_r=dma((4,)),
    )


def rows(index, size):
    return pl.ds(pl.multiple_of(index * size, size), size)


def layer_kernel(nz, names, *refs):
    r = SimpleNamespace(**dict(zip(names, refs)))
    s = lax.axis_index("seq")
    h = lax.axis_index("head")
    x, z = lax.rem(s, 2), lax.div(s, 2)
    y, c = lax.div(h, 2), lax.rem(h, 2)
    p = 4 * x + h
    sends = []

    def peer(mask):
        px = 1 - x if mask & 4 else x
        py = 1 - y if mask & 2 else y
        pc = 1 - c if mask & 1 else c
        ph = 2 * py + pc
        return (2 * z + px, ph), 4 * px + ph

    def plane(t):
        pz = lax.rem(z + t, nz)
        return (2 * pz + x, h), pz

    def remote(src, dst, ssem, rsem, device):
        return pltpu.make_async_remote_copy(
            src_ref=src, dst_ref=dst, send_sem=ssem, recv_sem=rsem,
            device_id=device, device_id_type=MESH,
        )

    def send(src, dst, ssem, rsem, device):
        copy = remote(src, dst, ssem, rsem, device)
        copy.start()
        sends.append(copy)

    def arrive(dst, ssem, rsem):
        remote(dst, dst, ssem, rsem, peer(1)[0]).wait_recv()

    def load(src, dst, k):
        copy = pltpu.make_async_copy(src, dst, r.lsem.at[k])
        copy.start()
        return copy

    few = nz <= FEW
    land = {}
    for name in ("layer", "words", "ffn", "att", "chr", "pool"):
        land[name] = getattr(r, ("v_" if few else "o_") + name)

    def keep_own(src, place, at, k):
        if few:
            place[at] = src[...]
            return None
        return load(src, place.at[at], k)

    low_half = iota((1, 128), 1) < 64

    def pick(a, b):
        shape = a.shape
        return jnp.where(iota(shape, 1) < 64, a, b)

    def pack(a):
        return pick(a[:64], swap(a[64:]))

    def pack_high(a):
        return pick(swap(a[:64]), a[64:])

    barrier = pltpu.get_barrier_semaphore()
    for mask in range(1, 8):
        pl.semaphore_signal(barrier, inc=1, device_id=peer(mask)[0], device_id_type=MESH)
    for t in range(1, nz):
        pl.semaphore_signal(barrier, inc=1, device_id=plane(t)[0], device_id_type=MESH)

    ld_x = load(r.char_input.at[rows(h, Q)], r.xin, 0)
    ld_cg = load(r.char_gain, r.cg, 1)
    ld_cnt = load(r.char_count, r.cnt, 2)
    ld_cp = load(r.char_proj, r.cpr, 3)
    ld_doc = load(r.document_ids, r.docs.at[s], 4)
    ld_co = load(r.char_out, r.co.at[h, pl.ds(64, 64)], 5)
    ld_pw = load(r.pool_proj, r.pw, 6)
    ld_word = load(r.word_input.at[rows(h, Q)], r.win, 7)
    ld_pg = load(r.pool_gain, r.pg, 8)
    ld_ag = load(r.attn_gain, r.ag, 9)
    ld_fg = load(r.ffn_gain, r.fg, 10)
    ld_aw = load(r.attn_proj, r.aw.at[h], 11)
    ld_ao = load(r.attn_out, r.ao.at[h], 12)
    ld_og = load(r.output_grad, r.ogp.at[x], 13)
    ld_fu = load(r.ffn_up, r.fu.at[h], 14)
    ld_fd = load(r.ffn_down, r.fd.at[h], 15)

    r.co[:, 0:64, :] = jnp.zeros((G, 64, C), BF)

    ld_cp.wait()
    place = (iota((64, 128), 0) == iota((64, 128), 1)).astype(F32).astype(BF)
    place_high = (iota((64, 128), 0) + 64 == iota((64, 128), 1)).astype(F32).astype(BF)
    wq, wk, wv = r.cpr[0], r.cpr[1], r.cpr[2]
    r.cw[h, :, 0:128] = (dot_l(wk, place) + dot_l(wq, place_high)).astype(BF)
    r.cw[h, :, 128:256] = (dot_l(wq, place) + dot_l(wv, place_high)).astype(BF)

    ld_x.wait()
    ld_cg.wait()

    def char_norm(i, carry):
        values = r.xin[pl.ds(i * 32, 32)].astype(F32).reshape(512, C)
        r.low[rows(i, 512), :] = (values * rms_factor(values) * r.cg[...]).astype(BF)
        return carry

    lax.fori_loop(0, R // 512, char_norm, 0)

    ld_cnt.wait()
    count_row = jnp.broadcast_to(r.cnt[pl.ds(h, 1), :].astype(F32), (128, 128))
    r.cntm[...] = count_row.T

    def char_masks(g, carry):
        eight = r.cntm[rows(g, 8), :]
        lane8 = iota((8, 128), 1)
        of_lane = jnp.sum(
            jnp.where(iota((8, 128), 0) == lax.div(lane8, L), eight, 0.0), axis=0, keepdims=True
        )
        lane16 = iota((16, 128), 1)
        count16 = jnp.broadcast_to(of_lane, (16, 128))
        letter16 = lax.rem(lane16, L).astype(F32)
        r.share[g] = jnp.where(letter16 < count16, 1.0 / count16, 0.0)[:8]
        r.msel[g] = jnp.where(
            (iota((16, 128), 0) == lax.div(lane16, L)) & (letter16 < count16), 1.0, 0.0
        ).astype(BF)
        row, lane = iota((128, 128), 0), iota((128, 128), 1)
        spread = jnp.where(lane == g * 8 + lax.div(row, L), 1.0, 0.0).astype(BF)
        count = dot(spread, r.cntm[...].astype(BF))
        valid = lax.rem(row, L).astype(F32) < count
        r.bias[g] = jnp.where(
            valid & (lax.div(row, L) == lax.div(lane, L)), 0.0, NEGATIVE
        ).astype(BF)
        r.shc[rows(g, 128), :] = jnp.where(valid, 1.0 / count, 0.0)
        r.live[g] = jnp.where(valid, 1.0, 0.0).astype(BF)
        return carry

    lax.fori_loop(0, GROUPS, char_masks, 0, unroll=4)

    pl.semaphore_wait(barrier, 7 + nz - 1)

    def gather_start(k, slots):
        mine = slots(h)
        send(mine, mine, r.wg_s.at[k, 0], r.wg_r.at[k, 0], peer(1)[0])
        send(mine, mine, r.wg_s.at[k, 1], r.wg_r.at[k, 1], peer(2)[0])

    def gather_forward(k, slots):
        far = slots(2 * (1 - y) + c)
        arrive(far, r.wg_s.at[k, 1], r.wg_r.at[k, 1])
        send(far, far, r.wg_s.at[k, 2], r.wg_r.at[k, 2], peer(1)[0])

    def gather_near(k, slots):
        arrive(slots(2 * y + 1 - c), r.wg_s.at[k, 0], r.wg_r.at[k, 0])

    def gather_last(k, slots):
        arrive(slots(2 * (1 - y) + 1 - c), r.wg_s.at[k, 2], r.wg_r.at[k, 2])

    def share_start(k, full, part):
        send(full(h), full(h), r.ws_s.at[k, 0], r.ws_r.at[k, 0], peer(1)[0])
        send(part(h, x), part(h, x), r.ws_s.at[k, 1], r.ws_r.at[k, 1], peer(2)[0])

    def share_middle(k, full, part):
        mine = part(2 * (1 - y) + c, x)
        arrive(mine, r.ws_s.at[k, 1], r.ws_r.at[k, 1])
        send(mine, mine, r.ws_s.at[k, 2], r.ws_r.at[k, 2], peer(4)[0])
        send(mine, mine, r.ws_s.at[k, 3], r.ws_r.at[k, 3], peer(1)[0])

    def share_end(k, full, part):
        other = part(2 * (1 - y) + c, 1 - x)
        arrive(other, r.ws_s.at[k, 2], r.ws_r.at[k, 2])
        send(other, other, r.ws_s.at[k, 4], r.ws_r.at[k, 4], peer(1)[0])

    def share_near(k, full, part):
        arrive(full(2 * y + 1 - c), r.ws_s.at[k, 0], r.ws_r.at[k, 0])

    def share_last(k, full, part):
        far = 2 * (1 - y) + 1 - c
        arrive(part(far, x), r.ws_s.at[k, 3], r.ws_r.at[k, 3])
        arrive(part(far, 1 - x), r.ws_s.at[k, 4], r.ws_r.at[k, 4])

    def fan_start(src, slots, ssem, rsem):
        for mask in (1, 2, 4, 6):
            send(src, slots.at[rows(p, Q)], ssem.at[mask], rsem.at[mask], peer(mask)[0])
        slots[rows(p, Q), :] = src[...]

    def fan_forward(slots, ssem, rsem):
        for mask in (2, 4, 6):
            got = slots.at[rows(peer(mask)[1], Q)]
            arrive(got, ssem.at[mask], rsem.at[mask])
            send(got, got, ssem.at[mask + 1], rsem.at[mask + 1], peer(1)[0])

    def fan_last(slots, ssem, rsem):
        for mask in (1, 3, 5, 7):
            arrive(slots.at[rows(peer(mask)[1], Q)], ssem.at[mask], rsem.at[mask])

    def head_rows_start(src, out, ssem, rsem):
        for mask in (1, 2):
            send(src, out.at[rows(h, Q)], ssem.at[mask], rsem.at[mask], peer(mask)[0])

    def head_rows_forward(out, ssem, rsem):
        got = out.at[rows(2 * (1 - y) + c, Q)]
        arrive(got, ssem.at[2], rsem.at[2])
        send(got, got, ssem.at[3], rsem.at[3], peer(1)[0])

    def head_rows_last(out, ssem, rsem):
        arrive(out.at[rows(2 * y + 1 - c, Q)], ssem.at[1], rsem.at[1])
        arrive(out.at[rows(2 * (1 - y) + 1 - c, Q)], ssem.at[3], rsem.at[3])

    order = [h, 2 * y + 1 - c, 2 * (1 - y) + c, 2 * (1 - y) + 1 - c]
    cw_at = lambda i: r.cw.at[i]
    co_at = lambda i: r.co.at[i, pl.ds(64, 64)]
    sh_aw = (0, lambda i: r.aw.at[i], lambda i, j: r.aw.at[i, :, rows(j, D // 2)])
    sh_ao = (1, lambda i: r.ao.at[i], lambda i, j: r.ao.at[i, rows(j, 64)])
    sh_fu = (2, lambda i: r.fu.at[i], lambda i, j: r.fu.at[i, rows(j, D // 2)])
    sh_fd = (3, lambda i: r.fd.at[i], lambda i, j: r.fd.at[i, rows(j, FS // 2)])

    gather_start(0, cw_at)
    ld_co.wait()
    gather_start(1, co_at)
    ld_doc.wait()
    send(r.docs.at[s], r.docs.at[s], r.x_s.at[0], r.x_r.at[0], peer(4)[0])
    ld_ao.wait()
    share_start(*sh_ao)
    ld_fu.wait()
    share_start(*sh_fu)
    ld_og.wait()
    og_half = lambda i, j: r.ogp.at[i, rows(j, W // 2)]
    send(og_half(x, c), og_half(x, c), r.og_s.at[0], r.og_r.at[0], peer(4)[0])

    lane_scale = jnp.where((iota((1, 256), 1) < 64) | (iota((1, 256), 1) >= 192), 1.0, 0.125)
    keep_low = jnp.where(low_half, 1.0, 0.0)
    keep_high = 1.0 - keep_low

    def char_head(hh):
        for i in range(2):
            part = pl.ds(i * (R // 2), R // 2)
            r.kq[hh, part, :] = (dot(r.low[part, :], r.cw[hh]) * lane_scale).astype(BF)
        kq = r.kq[hh, :, 0:128].reshape(GROUPS, 128, 128)
        qv = r.kq[hh, :, 128:256].astype(F32)
        query = (qv * keep_low).astype(BF).reshape(GROUPS, 128, 128)
        scores = bdot_t(kq, query) + r.bias[...].astype(F32)
        raised = jnp.exp(scores - jnp.max(scores, axis=1, keepdims=True))
        weights = (raised * (1.0 / jnp.sum(raised, axis=1, keepdims=True))).astype(BF)
        r.pt[hh] = weights
        took = bdot(weights, r.live[...]).reshape(R, 128)
        if nz <= FEW:
            r.took[hh] = took.astype(BF)
        got = jnp.sum((took * qv).reshape(Q, L, 128), axis=1)
        r.pooled[hh] = got * (1.0 / r.cntm[...]) * keep_high

    ld_aw.wait()
    first, other = r.aw[h, 0].astype(F32), r.aw[h, 1].astype(F32)
    third = r.aw[h, 2].astype(F32)
    even = x == 0
    r.wsel[:, 0:128] = (jnp.where(even, first, swap(first)) * 0.125 * keep_low).astype(BF)
    r.wsel[:, 128:256] = jnp.where(even, pick(other, swap(third)), pick(swap(other), third)).astype(BF)
    char_head(h)
    gather_near(0, cw_at)
    gather_forward(0, cw_at)
    gather_forward(1, co_at)
    gather_last(0, cw_at)

    def other_head(t, carry):
        char_head(lax.rem(h + t, G))
        return carry

    lax.fori_loop(1, G, other_head, 0)

    def char_mean(g, carry):
        block = r.xin[pl.ds(g * 8, 8)].reshape(128, C)
        r.mean[rows(g, 8), :] = dot(r.msel[g], block)[:8] * (1.0 / r.cntm[rows(g, 8), 0:1])
        return carry

    lax.fori_loop(0, GROUPS, char_mean, 0, unroll=4)
    gather_near(1, co_at)
    gather_last(1, co_at)
    summary = r.mean[...]
    for hh in range(G):
        summary = summary + dot(r.pooled[hh].astype(BF), r.co[hh])
    r.summ[...] = summary
    ld_pg.wait()
    ld_pw.wait()
    ld_word.wait()
    ld_ag.wait()
    r.plow[...] = (summary * rms_factor(summary) * r.pg[...]).astype(BF)
    hidden = r.win[...].astype(F32) + dot(r.plow[...], r.pw[...])
    r.hid[...] = hidden
    r.alow[...] = (hidden * rms_factor(hidden) * r.ag[...]).astype(BF)

    fan_start(r.alow, r.alp, r.al_s, r.al_r)
    ld_fd.wait()
    share_start(*sh_fd)
    share_start(*sh_aw)
    share_middle(*sh_ao)
    share_middle(*sh_fu)
    kv_mine = rows(z, PW)

    arrive(r.docs.at[2 * z + 1 - x], r.x_s.at[0], r.x_r.at[0])
    docs_mine = r.docs.at[pl.ds(2 * z, 2)]

    def docs_copy(t, source):
        return remote(
            r.docs.at[pl.ds(2 * source, 2)], r.docs.at[pl.ds(2 * source, 2)],
            r.dz_s.at[t], r.dz_r.at[source], (2 * lax.rem(z + t, nz) + x, h),
        )

    for t in range(1, nz):
        @pl.when(z + t < nz)
        def _():
            docs_copy(t, z).start()

    def key_marks(chunk, carry):
        row = r.docs[lax.div(chunk, 4), pl.ds(lax.rem(chunk, 4), 1), :]
        sub = iota((128, 128), 0)
        marks = jnp.where((sub < 3) & (jnp.broadcast_to(row, (128, 128)) != sub), 1.0, 0.0)
        slot = lax.rem(chunk, 4 * min(2 * nz, MARKS))
        r.marks[rows(slot, 128), :] = marks.T.astype(BF)
        return carry

    def query_marks(chunk, carry):
        row = r.docs[lax.div(z * 8 + chunk, 4), pl.ds(lax.rem(chunk, 4), 1), :]
        sub = iota((128, 128), 0)
        marks = jnp.where((sub < 3) & (jnp.broadcast_to(row, (128, 128)) == sub), NEGATIVE, 0.0)
        r.qd[rows(chunk, 128), 128:256] = marks.T.astype(BF)
        return carry

    lax.fori_loop(z * 8, z * 8 + 8, key_marks, 0)
    lax.fori_loop(0, 8, query_marks, 0)
    r.top[...] = jnp.full((8, PW), NEGATIVE, F32)
    r.total[...] = jnp.zeros((8, PW), F32)
    r.acct[...] = jnp.zeros((128, PW), F32)
    fan_forward(r.alp, r.al_s, r.al_r)
    fan_last(r.alp, r.al_s, r.al_r)
    mapped = dot(r.alp[...], r.wsel[...])
    r.qd[:, 0:128] = mapped[:, 0:128].astype(BF)
    r.kv[kv_mine, :] = mapped[:, 128:256].astype(BF)

    def unit_copy(u):
        block = r.kv.at[rows(u, KU)]
        return remote(
            block, block, r.kz_s.at[u], r.kz_r.at[u], (2 * lax.rem(z + 1, nz) + x, h)
        )

    @pl.when(z + 1 < nz)
    def _():
        unit_copy(2 * z).start()
        unit_copy(2 * z + 1).start()

    arrive(og_half(1 - x, c), r.og_s.at[0], r.og_r.at[0])
    send(og_half(1 - x, c), og_half(1 - x, c), r.og_s.at[1], r.og_r.at[1], peer(1)[0])

    def marked(kv, u):
        marks = r.marks[rows(lax.rem(u, min(2 * nz, MARKS)), KU), :]
        return jnp.concatenate([kv, marks], axis=1)

    def mark_again(u):
        if 2 * nz > MARKS:
            lax.fori_loop(4 * u, 4 * u + 4, key_marks, 0)

    def forward_tile(u, start, causal):
        at = pl.ds(start, PW - start)
        kv = r.kv[rows(u, KU), :]
        scores = dot_t(marked(kv, u), r.qd[at, :])
        if causal:
            gap = iota(scores.shape, 1) - iota(scores.shape, 0)
            scores = jnp.where(gap >= 0, scores, NEGATIVE)
        old = r.top[0:1, at]
        new = jnp.maximum(old, jnp.max(scores, axis=0, keepdims=True))
        raised = jnp.exp(scores - new)
        fade = jnp.exp(old - new)
        r.top[0:1, at] = new
        r.total[0:1, at] = r.total[0:1, at] * fade + jnp.sum(raised, axis=0, keepdims=True)
        turned = kv.astype(F32).T.astype(BF)
        r.acct[:, at] = r.acct[:, at] * fade + dot(turned, raised.astype(BF))

    forward_tile(2 * z, 0, True)
    forward_tile(2 * z + 1, KU, True)
    share_end(*sh_ao)
    share_middle(*sh_fd)
    share_end(*sh_fu)

    def wait_docs(source, carry):
        docs_copy(1, source).wait_recv()
        return carry

    lax.fori_loop(0, z, wait_docs, 0)
    if 2 * nz <= MARKS:
        lax.fori_loop(0, z * 8, key_marks, 0)

    def forward_unit(i, carry):
        u = 2 * z - 1 - i
        unit_copy(u).wait_recv()
        mark_again(u)

        @pl.when(z + 1 < nz)
        def _():
            unit_copy(u).start()

        forward_tile(u, 0, False)
        return carry

    lax.fori_loop(0, jnp.minimum(2 * z, 2), forward_unit, 0)
    share_end(*sh_fd)
    share_middle(*sh_aw)
    lax.fori_loop(jnp.minimum(2 * z, 2), 2 * z, forward_unit, 0)

    r.lse[0:1, :] = r.top[0:1, :] + jnp.log(r.total[0:1, :])
    over = 1.0 / r.total[0:1, :]
    for i in range(8):
        cols = slice(i * 128, i * 128 + 128)
        out = (r.acct[:, cols] * over[:, cols]).T * keep_high
        r.out[cols, :] = out
        r.ob[cols, :] = out.astype(BF)
        r.smx[i] = pack_high(out).astype(BF)
    for mask in range(1, 8):
        device, to = peer(mask)
        send(r.smx.at[to], r.rmx.at[p], r.mx_s.at[mask], r.mx_r.at[mask], device)
    r.rmx[p] = r.smx[p]
    share_end(*sh_aw)
    share_near(*sh_ao)
    share_last(*sh_ao)
    ld_fg.wait()
    for mask in range(1, 8):
        arrive(r.rmx.at[peer(mask)[1]], r.mx_s.at[mask], r.mx_r.at[mask])

    def two_heads(a, b):
        a, b = a.astype(F32), b.astype(F32)
        return jnp.concatenate([pick(a, swap(b)), pick(swap(a), b)], axis=0).astype(BF)

    second = r.hid[...]
    for hh in range(G):
        second = second + dot(two_heads(r.rmx[hh], r.rmx[4 + hh]), r.ao[hh])
    r.sec[...] = second
    r.flow[...] = (second * rms_factor(second) * r.fg[...]).astype(BF)

    fan_start(r.flow, r.flp, r.fl_s, r.fl_r)

    grad_rows = r.ogp[x, rows(h, Q), :]
    r.fsum[...] = jnp.zeros((Q, D), F32)
    for t in range(G):
        hh = order[t]
        if t == 1:
            share_near(*sh_fu)
            share_near(*sh_fd)
        if t == 3:
            share_last(*sh_fu)
            share_last(*sh_fd)
        upward = dot(r.flow[...], r.fu[hh])
        square = upward * upward
        inner = 0.7978845608028654 * upward * (1.0 + 0.044715 * square)
        bent = jnp.tanh(inner)
        half_up = 0.5 * (1.0 + bent)
        active = (upward * half_up).astype(BF)
        slope = half_up + 0.5 * upward * (1.0 - bent * bent) * (
            0.7978845608028654 * (1.0 + 0.134145 * square)
        )
        grad_up = (dot_t(grad_rows, r.fd[hh]) * slope).astype(BF)
        r.fsum[...] += dot_t(grad_up, r.fu[hh])
        r.sag[hh, :, 0:256] = active[:, 0:256]
        r.sag[hh, :, 256:512] = grad_up[:, 0:256]
        r.sag[4 + hh, :, 0:256] = active[:, 256:512]
        r.sag[4 + hh, :, 256:512] = grad_up[:, 256:512]
    back, gain_ffn = rms_back(r.fsum[...], r.sec[...], r.fg[...])
    grad_second = grad_rows.astype(F32) + back
    r.gsec[...] = grad_second
    r.gb[...] = grad_second.astype(BF)
    r.gn[0:1, :] = gain_ffn

    for t in range(G):
        hh = order[t]
        grad = dot_t(r.gb[...], r.ao[hh])
        r.sgm[hh] = pack(grad).astype(BF)
        r.sgm[4 + hh] = pack_high(grad).astype(BF)
        for mask in ((4,) if t == 0 else (t, t + 4)):
            device, to = peer(mask)
            send(r.sgm.at[to], r.rgm.at[p], r.gm_s.at[mask], r.gm_r.at[mask], device)
    r.rgm[p] = r.sgm[p]
    for mask in range(1, 8):
        device, to = peer(mask)
        send(r.sag.at[to], r.rag.at[rows(p, Q)], r.ac_s.at[mask], r.ac_r.at[mask], device)
    r.rag[rows(p, Q), :] = r.sag[p]
    r.acct[...] = jnp.zeros((128, PW), F32)
    r.lsum[...] = r.sec[...]

    def layer_part(hh, carry):
        r.lsum[...] += dot(r.sag[hh, :, 0:256], r.fd[hh, 0:256, :])
        r.lsum[...] += dot(r.sag[4 + hh, :, 0:256], r.fd[hh, 256:512, :])
        return carry

    lax.fori_loop(0, G, layer_part, 0)
    r.lay[...] = r.lsum[...].astype(BF)
    for mask in range(1, 8):
        arrive(r.rgm.at[peer(mask)[1]], r.gm_s.at[mask], r.gm_r.at[mask])

    for i in range(8):
        cols = slice(i * 128, i * 128 + 128)
        got = r.rgm[i].astype(F32)
        grad = jnp.concatenate([swap(got), got], axis=0) * keep_high
        r.gz[cols, :] = grad.astype(BF)
        r.xg[cols, :] = pick(r.qd[cols, 0:128].astype(F32), grad).astype(BF)
        r.delta[0:1, cols] = jnp.sum((grad * r.out[cols, :]).T, axis=0, keepdims=True)

    fan_start(r.gb, r.gbp, r.gb_s, r.gb_r)
    head_rows_start(r.lay, land["layer"], r.ly_s, r.ly_r)
    fan_forward(r.flp, r.fl_s, r.fl_r)
    st_lay = keep_own(r.lay, land["layer"], (rows(h, Q), slice(None)), 16)

    def backward_tile(u, start, causal):
        at = pl.ds(start, PW - start)
        kv = r.kv[rows(u, KU), :]
        scores = dot_t(marked(kv, u), r.qd[at, :])
        weights = jnp.exp(scores - r.lse[0:1, at])
        if causal:
            gap = iota(scores.shape, 1) - iota(scores.shape, 0)
            weights = jnp.where(gap >= 0, weights, 0.0)
        dweights = dot_t(kv, r.gz[at, :])
        dscores = (weights * (dweights - r.delta[0:1, at])).astype(BF)
        other = r.xg[at, :]
        turned = kv.astype(F32).T.astype(BF)
        r.acct[:, at] += dot(turned, dscores)
        return pick(dot(dscores, other), dot(weights.astype(BF), other))

    last = 2 * nz <= SLOTS

    def grad_slot(u):
        return lax.rem(u, min(2 * nz, SLOTS))

    def grad_copy(u):
        return remote(
            r.sdk.at[grad_slot(u)], r.rdk.at[u], r.dk_s.at[u], r.dk_r.at[u],
            (2 * lax.rem(z + nz - 1, nz) + x, h),
        )

    def grad_join(u):
        arrive(r.rdk.at[u], r.dk_s.at[u], r.dk_r.at[u])
        slot = grad_slot(u)
        r.sdk[slot] = (r.sdk[slot].astype(F32) + r.rdk[u].astype(F32)).astype(BF)

    def backward_unit(u, carry):
        mark_again(u)
        if not last:
            @pl.when(u >= SLOTS)
            def _():
                grad_copy(u - SLOTS).wait_send()
        r.sdk[grad_slot(u)] = backward_tile(u, 0, False).astype(BF)
        if last:
            @pl.when(z == nz - 1)
            def _():
                grad_copy(u).start()
        else:
            @pl.when(z < nz - 1)
            def _():
                grad_join(u)
            grad_copy(u).start()
        return carry

    def pass_on(u, carry):
        grad_join(u)
        grad_copy(u).start()
        return carry

    lax.fori_loop(0, 2 * z, backward_unit, 0)
    if last:
        lax.fori_loop(0, jnp.where(z < nz - 1, 2 * z, 0), pass_on, 0)

    def own_units():
        for own in range(2):
            mark_again(2 * z + own)
            r.dkv[own * KU : own * KU + KU, :] = backward_tile(2 * z + own, own * KU, True)

    own_units()

    def spread_copy(src, size, slots, ssem, rsem, t):
        device, pz = plane(t)
        return remote(src.at[rows(pz, size)], slots.at[z], ssem.at[t], rsem.at[z], device)

    def spread_start(src, size, slots, ssem, rsem, later):
        for t in range(1, nz):
            @pl.when((z + t < nz) if later else (z + t >= nz))
            def _():
                spread_copy(src, size, slots, ssem, rsem, t).start()
        if not later:
            for t in range(1, nz):
                sends.append(spread_copy(src, size, slots, ssem, rsem, t))

    def all_arrive(dst, ssem, rsem):
        for mask in range(1, 8):
            arrive(dst.at[rows(peer(mask)[1], Q)], ssem.at[mask], rsem.at[mask])

    def spread_sum(src, size, slots, ssem, rsem):
        slots[z] = src[rows(z, size), :]
        for t in range(1, nz):
            pz = plane(t)[1]
            arrive(slots.at[pz], ssem.at[t], rsem.at[pz])
        total = slots[0].astype(F32)
        for i in range(1, nz):
            total = total + slots[i].astype(F32)
        return total.astype(BF)

    def final_start(src, out, size, ssem, rsem, xs, xr, lk):
        mine = out.at[x, rows(z, size)]
        for t in range(1, nz):
            send(src, mine, ssem.at[t], rsem.at[z], plane(t)[0])
        send(src, mine, xs.at[z], xr.at[z], peer(4)[0])
        return keep_own(src, out, (x, rows(z, size)), lk)

    def final_cross(out, size, ssem, rsem, xs, xr):
        for t in range(1, nz):
            pz = plane(t)[1]
            part = out.at[x, rows(pz, size)]
            arrive(part, ssem.at[t], rsem.at[pz])
            send(part, part, xs.at[pz], xr.at[pz], peer(4)[0])

    def final_last(out, size, xs, xr):
        for i in range(nz):
            arrive(out.at[1 - x, rows(i, size)], xs.at[i], xr.at[i])

    all_arrive(r.rag, r.ac_s, r.ac_r)
    fan_last(r.flp, r.fl_s, r.fl_r)
    arrive(og_half(1 - x, 1 - c), r.og_s.at[1], r.og_r.at[1])
    for i in range(2):
        r.fw[i * 256 : i * 256 + 256, :] = dot_l(
            r.flp[:, i * 256 : i * 256 + 256], r.rag[:, 256:512]
        ).astype(BF)
        r.fw[512 + i * 256 : 768 + i * 256, :] = (
            dot_l(r.rag[0:W, 0:256], r.ogp[0, :, i * 256 : i * 256 + 256])
            + dot_l(r.rag[W:PW, 0:256], r.ogp[1, :, i * 256 : i * 256 + 256])
        ).astype(BF)

    spread_start(r.fw, FR // nz, r.frs, r.fr_s, r.fr_r, True)
    spread_start(r.fw, FR // nz, r.frs, r.fr_s, r.fr_r, False)

    @pl.when(z < nz - 1)
    def _():
        for own in range(2):
            u = 2 * z + own
            arrive(r.rdk.at[u], r.dk_s.at[u], r.dk_r.at[u])
            r.dkv[own * KU : own * KU + KU, :] += r.rdk[u].astype(F32)

    for i in range(8):
        cols = slice(i * 128, i * 128 + 128)
        r.sdkv[i] = r.dkv[cols, :].astype(BF)
        grad = r.acct[:, cols].T * 0.125
        r.sdq[i] = pack(grad).astype(BF)
        r.dqb[cols, :] = (grad * keep_low).astype(BF)
    for mask in range(1, 8):
        device, to = peer(mask)
        send(r.sdkv.at[to], r.rdkv.at[p], r.dkv_s.at[mask], r.dkv_r.at[mask], device)
        send(r.sdq.at[to], r.rdq.at[p], r.dq_s.at[mask], r.dq_r.at[mask], device)
    r.rdkv[p] = r.sdkv[p]
    r.rdq[p] = r.sdq[p]


    fan_forward(r.gbp, r.gb_s, r.gb_r)
    head_rows_forward(land["layer"], r.ly_s, r.ly_r)
    fan_last(r.gbp, r.gb_s, r.gb_r)
    for i in range(2):
        cols = slice(i * 256, i * 256 + 256)
        r.aw_g[cols, 0:128] = (
            dot_l(r.alp[:, cols], r.dqb[...]) + dot_l(r.gbp[:, cols], r.ob[...])
        ).astype(BF)
        r.aw_g[cols, 128:256] = dot_l(r.alp[:, cols], r.sdkv[...].reshape(PW, 128)).astype(BF)

    spread_start(r.aw_g, AR // nz, r.ars, r.ar_s, r.ar_r, True)
    spread_start(r.aw_g, AR // nz, r.ars, r.ar_s, r.ar_r, False)
    for mask in range(1, 8):
        arrive(r.rdkv.at[peer(mask)[1]], r.dkv_s.at[mask], r.dkv_r.at[mask])
        arrive(r.rdq.at[peer(mask)[1]], r.dq_s.at[mask], r.dq_r.at[mask])

    share_near(*sh_aw)
    share_last(*sh_aw)

    attn_sum = jnp.zeros((Q, D), F32)
    for hh in range(G):
        first, other = r.rdkv[hh].astype(F32), r.rdkv[4 + hh].astype(F32)
        attn_sum = attn_sum + dot_t(two_heads(r.rdq[hh], r.rdq[4 + hh]), r.aw[hh, 0])
        attn_sum = attn_sum + dot_t(pick(first, swap(other)).astype(BF), r.aw[hh, 1])
        attn_sum = attn_sum + dot_t(pick(swap(first), other).astype(BF), r.aw[hh, 2])
    back, gain_attn = rms_back(attn_sum, r.hid[...], r.ag[...])
    r.gw[...] = (r.gsec[...] + back).astype(BF)
    r.gn[1:2, :] = gain_attn
    head_rows_start(r.gw, land["words"], r.gw_s, r.gw_r)
    st_gw = keep_own(r.gw, land["words"], (rows(h, Q), slice(None)), 17)
    grad_summary, gain_pool = rms_back(dot_t(r.gw[...], r.pw[...]), r.summ[...], r.pg[...])
    r.gsum[...] = grad_summary
    gs_low = grad_summary.astype(BF)
    r.gn[2:3, 0:256] = gain_pool
    r.spw[...] = dot_l(r.plow[...], r.gw[...]).astype(BF)
    for mask in range(1, 8):
        device, to = peer(mask)
        send(r.spw.at[rows(to, 32)], r.rpw.at[p], r.pw_s.at[mask], r.pw_r.at[mask], device)
    r.rpw[p] = r.spw[rows(p, 32), :]

    ones = jnp.ones((128, 128), BF)

    def char_head_back(hh):
        r.gp[hh] = dot_t(gs_low, r.co[hh])
        w = r.cw[hh].astype(F32)
        r.cwt[hh, :, 0:128] = swap(w[:, 0:128]).astype(BF)
        r.cwt[hh, :, 128:256] = (w[:, 128:256] * keep_high).astype(BF)

        kq = r.kq[hh, :, 0:128].reshape(GROUPS, 128, 128)
        grad = jnp.broadcast_to(r.gp[hh][:, None, :], (Q, L, 128)).reshape(R, 128)
        gain = dot((r.kq[hh, :, 128:256].astype(F32) * grad).astype(BF), ones)
        gain = gain.reshape(GROUPS, 128, 128)
        weights = r.pt[hh].astype(F32)
        centre = jnp.sum(weights * gain, axis=1, keepdims=True)
        dscores = ((gain - centre) * (weights * r.share[:, 0:1, :])).astype(BF)
        dquery = (bdot_l(dscores, kq) * 0.125).reshape(R, 128)
        dkey = bdot(dscores, kq).reshape(R, 128)
        r.kq[hh, :, 0:128] = pick(dquery, dkey).astype(BF)
        if nz <= FEW:
            took = r.took[hh].astype(F32)
        else:
            took = bdot(r.pt[hh], r.live[...]).reshape(R, 128)
        r.kq[hh, :, 128:256] = (took * r.shc[...] * grad).astype(BF)
        term = dot_l(r.low[...], r.kq[hh])
        pooled = swap(r.pooled[hh]).astype(BF)
        r.scw[hh, :, 0:128] = term[:, 0:128].astype(BF)
        r.scw[hh, :, 128:256] = (term[:, 128:256] + dot_l(gs_low, pooled)).astype(BF)

    def char_term(t):
        hh = order[t]
        char_head_back(hh)
        for mask in ((4,) if t == 0 else (t, t + 4)):
            device, to = peer(mask)
            px = 1 - x if mask & 4 else x
            send(
                r.scw.at[hh, rows(px, 128)], r.rcw.at[p], r.cw_s.at[mask], r.cw_r.at[mask], device
            )

    def plane_sum(slots, ssem, rsem):
        for mask in range(1, 8):
            arrive(slots.at[peer(mask)[1]], ssem.at[mask], rsem.at[mask])
        total = slots[0].astype(F32)
        for i in range(1, 8):
            total = total + slots[i].astype(F32)
        return total

    def planes_start(slots, ssem, rsem):
        for t in range(1, nz):
            send(slots.at[z], slots.at[z], ssem.at[t], rsem.at[z], plane(t)[0])

    def planes_sum(slots, ssem, rsem):
        for t in range(1, nz):
            pz = plane(t)[1]
            arrive(slots.at[pz], ssem.at[t], rsem.at[pz])
        total = slots[0].astype(F32)
        for i in range(1, nz):
            total = total + slots[i].astype(F32)
        return total

    char_term(3)
    char_term(2)

    r.ffin[...] = spread_sum(r.fw, FR // nz, r.frs, r.fr_s, r.fr_r)
    st_ffn = final_start(r.ffin, land["ffn"], FR // nz, r.fa_s, r.fa_r, r.xf_s, r.xf_r, 18)
    head_rows_forward(land["words"], r.gw_s, r.gw_r)

    char_term(1)
    char_term(0)
    r.rcw[p] = r.scw[h, rows(x, 128), :]
    r.zpw[z] = plane_sum(r.rpw, r.pw_s, r.pw_r).astype(BF)
    planes_start(r.zpw, r.pz_s, r.pz_r)

    def char_back(i):
        part = pl.ds(i * (R // 2), R // 2)
        words = pl.ds(i * (Q // 2), Q // 2)
        upstream = dot_t(r.kq[0, part, :], r.cwt[0])
        for hh in range(1, G):
            upstream = upstream + dot_t(r.kq[hh, part, :], r.cwt[hh])
        values = r.xin[words].astype(F32).reshape(R // 2, C)
        back, gain = rms_back(upstream, values, r.cg[...])
        of_word = jnp.broadcast_to(r.gsum[words, :][:, None, :], (Q // 2, L, C))
        full = back + r.shc[part, 0:1] * of_word.reshape(R // 2, C)
        r.xin[words] = full.astype(BF).reshape(Q // 2, L, C)
        return gain

    gain_char = char_back(0)


    r.afin[...] = spread_sum(r.aw_g, AR // nz, r.ars, r.ar_s, r.ar_r)
    st_att = final_start(r.afin, land["att"], AR // nz, r.aa_s, r.aa_r, r.xa_s, r.xa_r, 19)

    r.zcw[z] = plane_sum(r.rcw, r.cw_s, r.cw_r).astype(BF)
    planes_start(r.zcw, r.cz_s, r.cz_r)
    gain_char = gain_char + char_back(1)
    st_chars = load(r.xin, r.o_chars, 20)
    r.gn[2:3, 256:512] = gain_char
    r.gn[3:8, :] = jnp.zeros((5, D), F32)
    for mask in range(1, 8):
        send(r.gn, r.rgn.at[p], r.gn_s.at[mask], r.gn_r.at[mask], peer(mask)[0])
    r.rgn[p] = r.gn[...]

    final_cross(land["ffn"], FR // nz, r.fa_s, r.fa_r, r.xf_s, r.xf_r)
    final_cross(land["att"], AR // nz, r.aa_s, r.aa_r, r.xa_s, r.xa_r)
    r.pfin[...] = planes_sum(r.zpw, r.pz_s, r.pz_r).astype(BF)
    for mask in range(1, 8):
        mine = land["pool"].at[rows(p, 32)]
        send(r.pfin, mine, r.pa_s.at[mask], r.pa_r.at[mask], peer(mask)[0])
    st_pool = keep_own(r.pfin, land["pool"], (rows(p, 32), slice(None)), 21)
    r.zgn[z] = plane_sum(r.rgn, r.gn_s, r.gn_r)
    planes_start(r.zgn, r.gz_s, r.gz_r)
    r.cfin[...] = planes_sum(r.zcw, r.cz_s, r.cz_r).astype(BF)
    send(r.cfin, land["chr"].at[x], r.x_s.at[4], r.x_r.at[4], peer(4)[0])
    st_chr = keep_own(r.cfin, land["chr"], x, 22)
    r.gnf[...] = planes_sum(r.zgn, r.gz_s, r.gz_r)
    st_gain = load(r.gnf, r.o_gain, 23)

    waiting = [st_chars, st_gain, st_ffn, st_att, st_lay, st_gw, st_pool, st_chr]

    def finish(name, k):
        if few:
            waiting.append(load(land[name], getattr(r, "o_" + name), k))

    head_rows_last(land["layer"], r.ly_s, r.ly_r)
    finish("layer", 24)
    head_rows_last(land["words"], r.gw_s, r.gw_r)
    finish("words", 25)
    final_last(land["ffn"], FR // nz, r.xf_s, r.xf_r)
    finish("ffn", 26)
    final_last(land["att"], AR // nz, r.xa_s, r.xa_r)
    finish("att", 27)
    for mask in range(1, 8):
        arrive(land["pool"].at[rows(peer(mask)[1], 32)], r.pa_s.at[mask], r.pa_r.at[mask])
    finish("pool", 28)
    arrive(land["chr"].at[1 - x], r.x_s.at[4], r.x_r.at[4])
    finish("chr", 29)
    for copy in waiting:
        if copy is not None:
            copy.wait()
    for copy in sends:
        copy.wait_send()
    for t in range(1, nz):
        @pl.when(z + t < nz)
        def _():
            docs_copy(t, z).wait_send()

    @pl.when(z + 1 < nz)
    def _():
        def sent(u, carry):
            unit_copy(u).wait_send()
            return carry

        lax.fori_loop(0, 2 * z + 2, sent, 0)

    def grads_sent(u, carry):
        grad_copy(u).wait_send()
        return carry

    lax.fori_loop(jnp.maximum(2 * z - SLOTS, 0), 2 * z, grads_sent, 0)


def per_device(nz, *arguments):
    given = dict(zip(INPUTS, arguments))
    for name in ("char_count", "document_ids"):
        given[name] = given[name].reshape(G, 128)
    given["char_proj"] = jnp.swapaxes(given["char_proj"], 1, 2)
    for name in ("char_gain", "pool_gain", "attn_gain", "ffn_gain"):
        given[name] = given[name].reshape(1, -1)
    scratch = scratch_list(nz)
    any_space = pl.BlockSpec(memory_space=pl.ANY)
    out_shape = [
        jax.ShapeDtypeStruct((W, D), BF),
        jax.ShapeDtypeStruct((W, D), BF),
        jax.ShapeDtypeStruct((Q, L, C), BF),
        jax.ShapeDtypeStruct((2, FR, 256), BF),
        jax.ShapeDtypeStruct((2, AR, 256), BF),
        jax.ShapeDtypeStruct((2, 128, 256), BF),
        jax.ShapeDtypeStruct((C, D), BF),
        jax.ShapeDtypeStruct((8, D), F32),
    ]
    names = INPUTS + OUTPUTS + list(scratch)
    layer, words, chars, ffn, att, chr_grad, pool, gain = pl.pallas_call(
        functools.partial(layer_kernel, nz, names),
        out_shape=out_shape,
        in_specs=[any_space] * len(INPUTS),
        out_specs=[any_space] * len(OUTPUTS),
        scratch_shapes=list(scratch.values()),
        compiler_params=pltpu.CompilerParams(
            collective_id=0, has_side_effects=True, vmem_limit_bytes=62 << 20
        ),
    )(*[given[name] for name in INPUTS])

    grads = [
        jax.ShapeDtypeStruct((W, D), BF),
        jax.ShapeDtypeStruct((W, D), BF),
        jax.ShapeDtypeStruct((Q, L, C), BF),
        jax.ShapeDtypeStruct((1, C), F32),
        jax.ShapeDtypeStruct((3, 64, C), F32),
        jax.ShapeDtypeStruct((64, C), F32),
        jax.ShapeDtypeStruct((1, C), F32),
        jax.ShapeDtypeStruct((C, D), F32),
        jax.ShapeDtypeStruct((1, D), F32),
        jax.ShapeDtypeStruct((3, D, 128), F32),
        jax.ShapeDtypeStruct((128, D), F32),
        jax.ShapeDtypeStruct((1, D), F32),
        jax.ShapeDtypeStruct((D, FS), F32),
        jax.ShapeDtypeStruct((FS, D), F32),
    ]
    result = pl.pallas_call(
        unpack_kernel,
        out_shape=grads,
        in_specs=[any_space] * len(out_shape),
        out_specs=[any_space] * len(grads),
        scratch_shapes=[pltpu.VMEM(a.shape, a.dtype) for a in out_shape + grads[3:]]
        + [pltpu.SemaphoreType.DMA((len(out_shape),)), pltpu.SemaphoreType.DMA((len(grads),))],
        compiler_params=pltpu.CompilerParams(vmem_limit_bytes=62 << 20),
    )(layer, words, chars, ffn, att, chr_grad, pool, gain)
    result = list(result)
    result[4] = jnp.swapaxes(result[4], 1, 2)
    for i in (3, 6, 8, 11):
        result[i] = result[i].reshape(-1)
    return tuple(result)


def unpack_kernel(*refs):
    given, out, held, made = refs[0:8], refs[8:22], refs[22:30], refs[30:41]
    in_sem, out_sem = refs[41:]
    ffn, att, chr_grad, pool, gain = held[3:]
    loads = [pltpu.make_async_copy(given[i], held[i], in_sem.at[i]) for i in range(8)]
    stores = [pltpu.make_async_copy(held[i], out[i], out_sem.at[i]) for i in range(3)]
    stores += [pltpu.make_async_copy(made[i], out[3 + i], out_sem.at[3 + i]) for i in range(11)]
    for i in (3, 4, 2, 0, 1, 6, 5, 7):
        loads[i].start()
    (g_char, g_proj, g_out, g_pool, g_pproj, g_attn, g_aproj, g_aout, g_ffn, g_up, g_down) = made

    def pick(a, b):
        return jnp.where(iota(a.shape, 1) < 64, a, b)

    loads[3].wait()
    for i in range(2):
        cols = slice(i * 256, i * 256 + 256)
        g_up[:, cols] = ffn[i, 0:512, :].astype(F32)
        g_down[cols, 0:256] = ffn[i, 512:768, :].astype(F32)
        g_down[cols, 256:512] = ffn[i, 768:1024, :].astype(F32)
    stores[12].start()
    stores[13].start()
    for i in (2, 0, 1):
        loads[i].wait()
        stores[i].start()
    loads[4].wait()
    first, other = att[0, :, 0:128].astype(F32), att[1, :, 0:128].astype(F32)
    g_aproj[0] = pick(first, swap(other))
    g_aout[...] = pick(swap(first), other).T
    first, other = att[0, :, 128:256].astype(F32), att[1, :, 128:256].astype(F32)
    g_aproj[1] = pick(first, swap(other))
    g_aproj[2] = pick(swap(first), other)
    stores[9].start()
    stores[10].start()
    loads[6].wait()
    g_pproj[...] = pool[...].astype(F32)
    stores[7].start()
    loads[5].wait()
    for i in range(2):
        cols = slice(i * 128, i * 128 + 128)
        block = chr_grad[i].astype(F32)
        first, other = block[:, 0:128].T, block[:, 128:256].T
        g_proj[0, :, cols] = first[0:64]
        g_proj[1, :, cols] = first[64:128]
        g_out[:, cols] = other[0:64]
        g_proj[2, :, cols] = other[64:128]
    stores[4].start()
    stores[5].start()
    loads[7].wait()
    g_ffn[...] = gain[0:1, :]
    g_attn[...] = gain[1:2, :]
    g_pool[...] = gain[2:3, 0:256]
    g_char[...] = gain[2:3, 256:512]
    for i in (3, 6, 8, 11):
        stores[i].start()
    for copy in stores:
        copy.wait()


def solution(mesh):
    nz = mesh.shape["seq"] // 2
    placed = (
        P("seq", None),
        P("seq", None, None),
        P("seq"),
        P("seq"),
        P("seq", None),
        P(),
        P(None, None, "head"),
        P("head", None),
        P(),
        P(),
        P(),
        P(None, None, "head"),
        P("head", None),
        P(),
        P(None, "head"),
        P("head", None),
    )
    return jax.shard_map(
        functools.partial(per_device, nz),
        mesh=mesh,
        in_specs=placed,
        out_specs=(
            P("seq", None),
            P("seq", None),
            P(("seq", "head"), None, None),
            P(),
            P(None, None, "head"),
            P("head", None),
            P(),
            P(),
            P(),
            P(None, None, "head"),
            P("head", None),
            P(),
            P(None, "head"),
            P("head", None),
        ),
        check_vma=False,
    )
```

```python
import functools
from types import SimpleNamespace

import jax
import jax.numpy as jnp
from jax import lax
from jax.experimental import pallas as pl
from jax.experimental.pallas import tpu as pltpu
from jax.sharding import PartitionSpec as P

MESH = pl.DeviceIdType.MESH
BF = jnp.bfloat16
F32 = jnp.float32
EPSILON = 1e-06
NEGATIVE = -1e30

D = 512
C = 256
L = 16
G = 4
Q = 128
W = G * Q
PW = 2 * W
R = Q * L
FS = 512
GROUPS = R // 128
KU = 512
MARKS = 8
SLOTS = 8
FR = 1024
FEW = 8
AR = 512

INPUTS = [
    "word_input",
    "char_input",
    "char_count",
    "document_ids",
    "output_grad",
    "char_gain",
    "char_proj",
    "char_out",
    "pool_gain",
    "pool_proj",
    "attn_gain",
    "attn_proj",
    "attn_out",
    "ffn_gain",
    "ffn_up",
    "ffn_down",
]
OUTPUTS = ["o_layer", "o_words", "o_chars", "o_ffn", "o_att", "o_chr", "o_pool", "o_gain"]


def dot(a, b):
    return lax.dot_general(a, b, (((1,), (0,)), ((), ())), preferred_element_type=F32)


def dot_t(a, b):
    return lax.dot_general(a, b, (((1,), (1,)), ((), ())), preferred_element_type=F32)


def dot_l(a, b):
    return lax.dot_general(a, b, (((0,), (0,)), ((), ())), preferred_element_type=F32)


def bdot(a, b):
    return lax.dot_general(a, b, (((2,), (1,)), ((0,), (0,))), preferred_element_type=F32)


def bdot_t(a, b):
    return lax.dot_general(a, b, (((2,), (2,)), ((0,), (0,))), preferred_element_type=F32)


def bdot_l(a, b):
    return lax.dot_general(a, b, (((1,), (1,)), ((0,), (0,))), preferred_element_type=F32)


def iota(shape, axis):
    return lax.broadcasted_iota(jnp.int32, shape, axis)


def swap(a):
    return pltpu.roll(a, 64, 1)


def rms_factor(values):
    return lax.rsqrt(jnp.mean(values * values, axis=-1, keepdims=True) + EPSILON)


def rms_back(upstream, values, gain):
    factor = rms_factor(values)
    unit = values * factor
    scaled = upstream * gain
    centre = jnp.mean(scaled * unit, axis=-1, keepdims=True)
    return factor * (scaled - unit * centre), jnp.sum(upstream * unit, axis=0, keepdims=True)


def scratch_list(nz):
    n = 2 * nz
    vm = pltpu.VMEM
    dma = pltpu.SemaphoreType.DMA
    return dict(
        xin=vm((Q, L, C), BF),
        cnt=vm((G, 128), jnp.int32),
        docs=vm((n, G, 128), jnp.int32),
        cpr=vm((3, 64, C), BF),
        win=vm((Q, D), BF),
        ogp=vm((2, W, D), BF),
        cg=vm((1, C), F32),
        pg=vm((1, C), F32),
        ag=vm((1, D), F32),
        fg=vm((1, D), F32),
        cw=vm((G, C, 256), BF),
        cwt=vm((G, C, 256), BF),
        co=vm((G, 128, C), BF),
        pw=vm((C, D), BF),
        aw=vm((G, 3, D, 128), BF),
        ao=vm((G, 128, D), BF),
        fu=vm((G, D, FS), BF),
        fd=vm((G, FS, D), BF),
        low=vm((R, C), BF),
        cntm=vm((128, 128), F32),
        share=vm((GROUPS, 8, 128), F32),
        shc=vm((R, 128), F32),
        msel=vm((GROUPS, 16, 128), BF),
        live=vm((GROUPS, 128, 128), BF),
        took=vm((G if nz <= FEW else 1, R, 128), BF),
        bias=vm((GROUPS, 128, 128), BF),
        kq=vm((G, R, 256), BF),
        pt=vm((G, GROUPS, 128, 128), BF),
        pooled=vm((G, Q, 128), F32),
        gp=vm((G, Q, 128), F32),
        mean=vm((Q, C), F32),
        summ=vm((Q, C), F32),
        plow=vm((Q, C), BF),
        hid=vm((Q, D), F32),
        alow=vm((Q, D), BF),
        sec=vm((Q, D), F32),
        flow=vm((Q, D), BF),
        lay=vm((Q, D), BF),
        fsum=vm((Q, D), F32),
        lsum=vm((Q, D), F32),
        gsec=vm((Q, D), F32),
        gb=vm((Q, D), BF),
        gw=vm((Q, D), BF),
        gsum=vm((Q, C), F32),
        wsel=vm((D, 256), BF),
        kv=vm((nz * PW, 128), BF),
        marks=vm((min(n, MARKS) * KU, 128), BF),
        qd=vm((PW, 256), BF),
        top=vm((8, PW), F32),
        total=vm((8, PW), F32),
        lse=vm((8, PW), F32),
        delta=vm((8, PW), F32),
        acct=vm((128, PW), F32),
        out=vm((PW, 128), F32),
        ob=vm((PW, 128), BF),
        smx=vm((8, 64, 128), BF),
        rmx=vm((8, 64, 128), BF),
        sgm=vm((8, 64, 128), BF),
        rgm=vm((8, 64, 128), BF),
        gz=vm((PW, 128), BF),
        xg=vm((PW, 128), BF),
        dkv=vm((PW, 128), F32),
        sdk=vm((min(n, SLOTS), KU, 128), BF),
        rdk=vm((n, KU, 128), BF),
        dqb=vm((PW, 128), BF),
        sdkv=vm((8, Q, 128), BF),
        rdkv=vm((8, Q, 128), BF),
        sdq=vm((8, 64, 128), BF),
        rdq=vm((8, 64, 128), BF),
        alp=vm((PW, D), BF),
        flp=vm((PW, D), BF),
        gbp=vm((PW, D), BF),
        sag=vm((8, Q, 512), BF),
        rag=vm((PW, 512), BF),
        fw=vm((FR, 256), BF),
        frs=vm((nz, FR // nz, 256), BF),
        ffin=vm((FR // nz, 256), BF),
        aw_g=vm((AR, 256), BF),
        ars=vm((nz, AR // nz, 256), BF),
        afin=vm((AR // nz, 256), BF),
        scw=vm((G, C, 256), BF),
        rcw=vm((8, 128, 256), BF),
        zcw=vm((nz, 128, 256), BF),
        cfin=vm((128, 256), BF),
        spw=vm((C, D), BF),
        rpw=vm((8, 32, D), BF),
        zpw=vm((nz, 32, D), BF),
        pfin=vm((32, D), BF),
        gn=vm((8, D), F32),
        rgn=vm((8, 8, D), F32),
        zgn=vm((nz, 8, D), F32),
        gnf=vm((8, D), F32),
        v_layer=vm((W, D) if nz <= FEW else (16, 128), BF),
        v_words=vm((W, D) if nz <= FEW else (16, 128), BF),
        v_ffn=vm((2, FR, 256) if nz <= FEW else (16, 128), BF),
        v_att=vm((2, AR, 256) if nz <= FEW else (16, 128), BF),
        v_chr=vm((2, 128, 256) if nz <= FEW else (16, 128), BF),
        v_pool=vm((C, D) if nz <= FEW else (16, 128), BF),
        lsem=dma((32,)),
        wg_s=dma((2, 3)),
        wg_r=dma((2, 3)),
        ws_s=dma((4, 5)),
        ws_r=dma((4, 5)),
        og_s=dma((2,)),
        og_r=dma((2,)),
        mx_s=dma((8,)),
        mx_r=dma((8,)),
        gm_s=dma((8,)),
        gm_r=dma((8,)),
        dkv_s=dma((8,)),
        dkv_r=dma((8,)),
        dq_s=dma((8,)),
        dq_r=dma((8,)),
        al_s=dma((8,)),
        al_r=dma((8,)),
        fl_s=dma((8,)),
        fl_r=dma((8,)),
        gb_s=dma((8,)),
        gb_r=dma((8,)),
        ac_s=dma((8,)),
        ac_r=dma((8,)),
        cw_s=dma((8,)),
        cw_r=dma((8,)),
        pw_s=dma((8,)),
        pw_r=dma((8,)),
        pa_s=dma((8,)),
        pa_r=dma((8,)),
        gn_s=dma((8,)),
        gn_r=dma((8,)),
        kz_s=dma((n,)),
        kz_r=dma((n,)),
        dz_s=dma((nz,)),
        dz_r=dma((nz,)),
        x_s=dma((5,)),
        x_r=dma((5,)),
        dk_s=dma((n,)),
        dk_r=dma((n,)),
        xf_s=dma((nz,)),
        xf_r=dma((nz,)),
        xa_s=dma((nz,)),
        xa_r=dma((nz,)),
        fr_s=dma((nz,)),
        fr_r=dma((nz,)),
        fa_s=dma((nz,)),
        fa_r=dma((nz,)),
        ar_s=dma((nz,)),
        ar_r=dma((nz,)),
        aa_s=dma((nz,)),
        aa_r=dma((nz,)),
        cz_s=dma((nz,)),
        cz_r=dma((nz,)),
        pz_s=dma((nz,)),
        pz_r=dma((nz,)),
        gz_s=dma((nz,)),
        gz_r=dma((nz,)),
        ly_s=dma((4,)),
        ly_r=dma((4,)),
        gw_s=dma((4,)),
        gw_r=dma((4,)),
    )


def rows(index, size):
    return pl.ds(pl.multiple_of(index * size, size), size)


def layer_kernel(nz, names, *refs):
    r = SimpleNamespace(**dict(zip(names, refs)))
    s = lax.axis_index("seq")
    h = lax.axis_index("head")
    x, z = lax.rem(s, 2), lax.div(s, 2)
    y, c = lax.div(h, 2), lax.rem(h, 2)
    p = 4 * x + h
    sends = []

    def peer(mask):
        px = 1 - x if mask & 4 else x
        py = 1 - y if mask & 2 else y
        pc = 1 - c if mask & 1 else c
        ph = 2 * py + pc
        return (2 * z + px, ph), 4 * px + ph

    def plane(t):
        pz = lax.rem(z + t, nz)
        return (2 * pz + x, h), pz

    def remote(src, dst, ssem, rsem, device):
        return pltpu.make_async_remote_copy(
            src_ref=src, dst_ref=dst, send_sem=ssem, recv_sem=rsem,
            device_id=device, device_id_type=MESH,
        )

    def send(src, dst, ssem, rsem, device):
        copy = remote(src, dst, ssem, rsem, device)
        copy.start()
        sends.append(copy)

    def arrive(dst, ssem, rsem):
        remote(dst, dst, ssem, rsem, peer(1)[0]).wait_recv()

    def load(src, dst, k):
        copy = pltpu.make_async_copy(src, dst, r.lsem.at[k])
        copy.start()
        return copy

    few = nz <= FEW
    land = {}
    for name in ("layer", "words", "ffn", "att", "chr", "pool"):
        land[name] = getattr(r, ("v_" if few else "o_") + name)

    def keep_own(src, place, at, k):
        if few:
            place[at] = src[...]
            return None
        return load(src, place.at[at], k)

    low_half = iota((1, 128), 1) < 64

    def pick(a, b):
        shape = a.shape
        return jnp.where(iota(shape, 1) < 64, a, b)

    def pack(a):
        return pick(a[:64], swap(a[64:]))

    def pack_high(a):
        return pick(swap(a[:64]), a[64:])

    barrier = pltpu.get_barrier_semaphore()
    for mask in range(1, 8):
        pl.semaphore_signal(barrier, inc=1, device_id=peer(mask)[0], device_id_type=MESH)
    for t in range(1, nz):
        pl.semaphore_signal(barrier, inc=1, device_id=plane(t)[0], device_id_type=MESH)

    ld_x = load(r.char_input.at[rows(h, Q)], r.xin, 0)
    ld_cg = load(r.char_gain, r.cg, 1)
    ld_cnt = load(r.char_count, r.cnt, 2)
    ld_cp = load(r.char_proj, r.cpr, 3)
    ld_doc = load(r.document_ids, r.docs.at[s], 4)
    ld_co = load(r.char_out, r.co.at[h, pl.ds(64, 64)], 5)
    ld_pw = load(r.pool_proj, r.pw, 6)
    ld_word = load(r.word_input.at[rows(h, Q)], r.win, 7)
    ld_pg = load(r.pool_gain, r.pg, 8)
    ld_ag = load(r.attn_gain, r.ag, 9)
    ld_fg = load(r.ffn_gain, r.fg, 10)
    ld_aw = load(r.attn_proj, r.aw.at[h], 11)
    ld_ao = load(r.attn_out, r.ao.at[h], 12)
    ld_og = load(r.output_grad, r.ogp.at[x], 13)
    ld_fu = load(r.ffn_up, r.fu.at[h], 14)
    ld_fd = load(r.ffn_down, r.fd.at[h], 15)

    r.co[:, 0:64, :] = jnp.zeros((G, 64, C), BF)

    ld_cp.wait()
    place = (iota((64, 128), 0) == iota((64, 128), 1)).astype(F32).astype(BF)
    place_high = (iota((64, 128), 0) + 64 == iota((64, 128), 1)).astype(F32).astype(BF)
    wq, wk, wv = r.cpr[0], r.cpr[1], r.cpr[2]
    r.cw[h, :, 0:128] = (dot_l(wk, place) + dot_l(wq, place_high)).astype(BF)
    r.cw[h, :, 128:256] = (dot_l(wq, place) + dot_l(wv, place_high)).astype(BF)

    ld_x.wait()
    ld_cg.wait()

    def char_norm(i, carry):
        values = r.xin[pl.ds(i * 32, 32)].astype(F32).reshape(512, C)
        r.low[rows(i, 512), :] = (values * rms_factor(values) * r.cg[...]).astype(BF)
        return carry

    lax.fori_loop(0, R // 512, char_norm, 0)

    ld_cnt.wait()
    count_row = jnp.broadcast_to(r.cnt[pl.ds(h, 1), :].astype(F32), (128, 128))
    r.cntm[...] = count_row.T

    def char_masks(g, carry):
        eight = r.cntm[rows(g, 8), :]
        lane8 = iota((8, 128), 1)
        of_lane = jnp.sum(
            jnp.where(iota((8, 128), 0) == lax.div(lane8, L), eight, 0.0), axis=0, keepdims=True
        )
        lane16 = iota((16, 128), 1)
        count16 = jnp.broadcast_to(of_lane, (16, 128))
        letter16 = lax.rem(lane16, L).astype(F32)
        r.share[g] = jnp.where(letter16 < count16, 1.0 / count16, 0.0)[:8]
        r.msel[g] = jnp.where(
            (iota((16, 128), 0) == lax.div(lane16, L)) & (letter16 < count16), 1.0, 0.0
        ).astype(BF)
        row, lane = iota((128, 128), 0), iota((128, 128), 1)
        spread = jnp.where(lane == g * 8 + lax.div(row, L), 1.0, 0.0).astype(BF)
        count = dot(spread, r.cntm[...].astype(BF))
        valid = lax.rem(row, L).astype(F32) < count
        r.bias[g] = jnp.where(
            valid & (lax.div(row, L) == lax.div(lane, L)), 0.0, NEGATIVE
        ).astype(BF)
        r.shc[rows(g, 128), :] = jnp.where(valid, 1.0 / count, 0.0)
        r.live[g] = jnp.where(valid, 1.0, 0.0).astype(BF)
        return carry

    lax.fori_loop(0, GROUPS, char_masks, 0, unroll=4)

    pl.semaphore_wait(barrier, 7 + nz - 1)

    def gather_start(k, slots):
        mine = slots(h)
        send(mine, mine, r.wg_s.at[k, 0], r.wg_r.at[k, 0], peer(1)[0])
        send(mine, mine, r.wg_s.at[k, 1], r.wg_r.at[k, 1], peer(2)[0])

    def gather_forward(k, slots):
        far = slots(2 * (1 - y) + c)
        arrive(far, r.wg_s.at[k, 1], r.wg_r.at[k, 1])
        send(far, far, r.wg_s.at[k, 2], r.wg_r.at[k, 2], peer(1)[0])

    def gather_near(k, slots):
        arrive(slots(2 * y + 1 - c), r.wg_s.at[k, 0], r.wg_r.at[k, 0])

    def gather_last(k, slots):
        arrive(slots(2 * (1 - y) + 1 - c), r.wg_s.at[k, 2], r.wg_r.at[k, 2])

    def share_start(k, full, part):
        send(full(h), full(h), r.ws_s.at[k, 0], r.ws_r.at[k, 0], peer(1)[0])
        send(part(h, x), part(h, x), r.ws_s.at[k, 1], r.ws_r.at[k, 1], peer(2)[0])

    def share_middle(k, full, part):
        mine = part(2 * (1 - y) + c, x)
        arrive(mine, r.ws_s.at[k, 1], r.ws_r.at[k, 1])
        send(mine, mine, r.ws_s.at[k, 2], r.ws_r.at[k, 2], peer(4)[0])
        send(mine, mine, r.ws_s.at[k, 3], r.ws_r.at[k, 3], peer(1)[0])

    def share_end(k, full, part):
        other = part(2 * (1 - y) + c, 1 - x)
        arrive(other, r.ws_s.at[k, 2], r.ws_r.at[k, 2])
        send(other, other, r.ws_s.at[k, 4], r.ws_r.at[k, 4], peer(1)[0])

    def share_near(k, full, part):
        arrive(full(2 * y + 1 - c), r.ws_s.at[k, 0], r.ws_r.at[k, 0])

    def share_last(k, full, part):
        far = 2 * (1 - y) + 1 - c
        arrive(part(far, x), r.ws_s.at[k, 3], r.ws_r.at[k, 3])
        arrive(part(far, 1 - x), r.ws_s.at[k, 4], r.ws_r.at[k, 4])

    def fan_start(src, slots, ssem, rsem):
        for mask in (1, 2, 4, 6):
            send(src, slots.at[rows(p, Q)], ssem.at[mask], rsem.at[mask], peer(mask)[0])
        slots[rows(p, Q), :] = src[...]

    def fan_forward(slots, ssem, rsem):
        for mask in (2, 4, 6):
            got = slots.at[rows(peer(mask)[1], Q)]
            arrive(got, ssem.at[mask], rsem.at[mask])
            send(got, got, ssem.at[mask + 1], rsem.at[mask + 1], peer(1)[0])

    def fan_last(slots, ssem, rsem):
        for mask in (1, 3, 5, 7):
            arrive(slots.at[rows(peer(mask)[1], Q)], ssem.at[mask], rsem.at[mask])

    def head_rows_start(src, out, ssem, rsem):
        for mask in (1, 2):
            send(src, out.at[rows(h, Q)], ssem.at[mask], rsem.at[mask], peer(mask)[0])

    def head_rows_forward(out, ssem, rsem):
        got = out.at[rows(2 * (1 - y) + c, Q)]
        arrive(got, ssem.at[2], rsem.at[2])
        send(got, got, ssem.at[3], rsem.at[3], peer(1)[0])

    def head_rows_last(out, ssem, rsem):
        arrive(out.at[rows(2 * y + 1 - c, Q)], ssem.at[1], rsem.at[1])
        arrive(out.at[rows(2 * (1 - y) + 1 - c, Q)], ssem.at[3], rsem.at[3])

    order = [h, 2 * y + 1 - c, 2 * (1 - y) + c, 2 * (1 - y) + 1 - c]
    cw_at = lambda i: r.cw.at[i]
    co_at = lambda i: r.co.at[i, pl.ds(64, 64)]
    sh_aw = (0, lambda i: r.aw.at[i], lambda i, j: r.aw.at[i, :, rows(j, D // 2)])
    sh_ao = (1, lambda i: r.ao.at[i], lambda i, j: r.ao.at[i, rows(j, 64)])
    sh_fu = (2, lambda i: r.fu.at[i], lambda i, j: r.fu.at[i, rows(j, D // 2)])
    sh_fd = (3, lambda i: r.fd.at[i], lambda i, j: r.fd.at[i, rows(j, FS // 2)])

    gather_start(0, cw_at)
    ld_co.wait()
    gather_start(1, co_at)
    ld_doc.wait()
    send(r.docs.at[s], r.docs.at[s], r.x_s.at[0], r.x_r.at[0], peer(4)[0])
    ld_ao.wait()
    share_start(*sh_ao)
    ld_fu.wait()
    share_start(*sh_fu)
    ld_og.wait()
    og_half = lambda i, j: r.ogp.at[i, rows(j, W // 2)]
    send(og_half(x, c), og_half(x, c), r.og_s.at[0], r.og_r.at[0], peer(4)[0])

    lane_scale = jnp.where((iota((1, 256), 1) < 64) | (iota((1, 256), 1) >= 192), 1.0, 0.125)
    keep_low = jnp.where(low_half, 1.0, 0.0)
    keep_high = 1.0 - keep_low

    def char_head(hh):
        for i in range(2):
            part = pl.ds(i * (R // 2), R // 2)
            r.kq[hh, part, :] = (dot(r.low[part, :], r.cw[hh]) * lane_scale).astype(BF)
        kq = r.kq[hh, :, 0:128].reshape(GROUPS, 128, 128)
        qv = r.kq[hh, :, 128:256].astype(F32)
        query = (qv * keep_low).astype(BF).reshape(GROUPS, 128, 128)
        scores = bdot_t(kq, query) + r.bias[...].astype(F32)
        raised = jnp.exp(scores - jnp.max(scores, axis=1, keepdims=True))
        weights = (raised * (1.0 / jnp.sum(raised, axis=1, keepdims=True))).astype(BF)
        r.pt[hh] = weights
        took = bdot(weights, r.live[...]).reshape(R, 128)
        if nz <= FEW:
            r.took[hh] = took.astype(BF)
        got = jnp.sum((took * qv).reshape(Q, L, 128), axis=1)
        r.pooled[hh] = got * (1.0 / r.cntm[...]) * keep_high

    ld_aw.wait()
    first, other = r.aw[h, 0].astype(F32), r.aw[h, 1].astype(F32)
    third = r.aw[h, 2].astype(F32)
    even = x == 0
    r.wsel[:, 0:128] = (jnp.where(even, first, swap(first)) * 0.125 * keep_low).astype(BF)
    r.wsel[:, 128:256] = jnp.where(even, pick(other, swap(third)), pick(swap(other), third)).astype(BF)
    char_head(h)
    gather_near(0, cw_at)
    gather_forward(0, cw_at)
    gather_forward(1, co_at)
    gather_last(0, cw_at)

    def other_head(t, carry):
        char_head(lax.rem(h + t, G))
        return carry

    lax.fori_loop(1, G, other_head, 0)

    def char_mean(g, carry):
        block = r.xin[pl.ds(g * 8, 8)].reshape(128, C)
        r.mean[rows(g, 8), :] = dot(r.msel[g], block)[:8] * (1.0 / r.cntm[rows(g, 8), 0:1])
        return carry

    lax.fori_loop(0, GROUPS, char_mean, 0, unroll=4)
    gather_near(1, co_at)
    gather_last(1, co_at)
    summary = r.mean[...]
    for hh in range(G):
        summary = summary + dot(r.pooled[hh].astype(BF), r.co[hh])
    r.summ[...] = summary
    ld_pg.wait()
    ld_pw.wait()
    ld_word.wait()
    ld_ag.wait()
    r.plow[...] = (summary * rms_factor(summary) * r.pg[...]).astype(BF)
    hidden = r.win[...].astype(F32) + dot(r.plow[...], r.pw[...])
    r.hid[...] = hidden
    r.alow[...] = (hidden * rms_factor(hidden) * r.ag[...]).astype(BF)

    fan_start(r.alow, r.alp, r.al_s, r.al_r)
    ld_fd.wait()
    share_start(*sh_fd)
    share_start(*sh_aw)
    share_middle(*sh_ao)
    share_middle(*sh_fu)
    kv_mine = rows(z, PW)

    arrive(r.docs.at[2 * z + 1 - x], r.x_s.at[0], r.x_r.at[0])
    docs_mine = r.docs.at[pl.ds(2 * z, 2)]

    def docs_copy(t, source):
        return remote(
            r.docs.at[pl.ds(2 * source, 2)], r.docs.at[pl.ds(2 * source, 2)],
            r.dz_s.at[t], r.dz_r.at[source], (2 * lax.rem(z + t, nz) + x, h),
        )

    for t in range(1, nz):
        @pl.when(z + t < nz)
        def _():
            docs_copy(t, z).start()

    def key_marks(chunk, carry):
        row = r.docs[lax.div(chunk, 4), pl.ds(lax.rem(chunk, 4), 1), :]
        sub = iota((128, 128), 0)
        marks = jnp.where((sub < 3) & (jnp.broadcast_to(row, (128, 128)) != sub), 1.0, 0.0)
        slot = lax.rem(chunk, 4 * min(2 * nz, MARKS))
        r.marks[rows(slot, 128), :] = marks.T.astype(BF)
        return carry

    def query_marks(chunk, carry):
        row = r.docs[lax.div(z * 8 + chunk, 4), pl.ds(lax.rem(chunk, 4), 1), :]
        sub = iota((128, 128), 0)
        marks = jnp.where((sub < 3) & (jnp.broadcast_to(row, (128, 128)) == sub), NEGATIVE, 0.0)
        r.qd[rows(chunk, 128), 128:256] = marks.T.astype(BF)
        return carry

    lax.fori_loop(z * 8, z * 8 + 8, key_marks, 0)
    lax.fori_loop(0, 8, query_marks, 0)
    r.top[...] = jnp.full((8, PW), NEGATIVE, F32)
    r.total[...] = jnp.zeros((8, PW), F32)
    r.acct[...] = jnp.zeros((128, PW), F32)
    fan_forward(r.alp, r.al_s, r.al_r)
    fan_last(r.alp, r.al_s, r.al_r)
    mapped = dot(r.alp[...], r.wsel[...])
    r.qd[:, 0:128] = mapped[:, 0:128].astype(BF)
    r.kv[kv_mine, :] = mapped[:, 128:256].astype(BF)

    def unit_copy(u):
        block = r.kv.at[rows(u, KU)]
        return remote(
            block, block, r.kz_s.at[u], r.kz_r.at[u], (2 * lax.rem(z + 1, nz) + x, h)
        )

    @pl.when(z + 1 < nz)
    def _():
        unit_copy(2 * z).start()
        unit_copy(2 * z + 1).start()

    arrive(og_half(1 - x, c), r.og_s.at[0], r.og_r.at[0])
    send(og_half(1 - x, c), og_half(1 - x, c), r.og_s.at[1], r.og_r.at[1], peer(1)[0])

    def marked(kv, u):
        marks = r.marks[rows(lax.rem(u, min(2 * nz, MARKS)), KU), :]
        return jnp.concatenate([kv, marks], axis=1)

    def mark_again(u):
        if 2 * nz > MARKS:
            lax.fori_loop(4 * u, 4 * u + 4, key_marks, 0)

    def forward_tile(u, start, causal):
        at = pl.ds(start, PW - start)
        kv = r.kv[rows(u, KU), :]
        scores = dot_t(marked(kv, u), r.qd[at, :])
        if causal:
            gap = iota(scores.shape, 1) - iota(scores.shape, 0)
            scores = jnp.where(gap >= 0, scores, NEGATIVE)
        old = r.top[0:1, at]
        new = jnp.maximum(old, jnp.max(scores, axis=0, keepdims=True))
        raised = jnp.exp(scores - new)
        fade = jnp.exp(old - new)
        r.top[0:1, at] = new
        r.total[0:1, at] = r.total[0:1, at] * fade + jnp.sum(raised, axis=0, keepdims=True)
        turned = kv.astype(F32).T.astype(BF)
        r.acct[:, at] = r.acct[:, at] * fade + dot(turned, raised.astype(BF))

    forward_tile(2 * z, 0, True)
    forward_tile(2 * z + 1, KU, True)
    share_end(*sh_ao)
    share_middle(*sh_fd)
    share_end(*sh_fu)

    def wait_docs(source, carry):
        docs_copy(1, source).wait_recv()
        return carry

    lax.fori_loop(0, z, wait_docs, 0)
    if 2 * nz <= MARKS:
        lax.fori_loop(0, z * 8, key_marks, 0)

    def forward_unit(i, carry):
        u = 2 * z - 1 - i
        unit_copy(u).wait_recv()
        mark_again(u)

        @pl.when(z + 1 < nz)
        def _():
            unit_copy(u).start()

        forward_tile(u, 0, False)
        return carry

    lax.fori_loop(0, jnp.minimum(2 * z, 2), forward_unit, 0)
    share_end(*sh_fd)
    share_middle(*sh_aw)
    lax.fori_loop(jnp.minimum(2 * z, 2), 2 * z, forward_unit, 0)

    r.lse[0:1, :] = r.top[0:1, :] + jnp.log(r.total[0:1, :])
    over = 1.0 / r.total[0:1, :]
    for i in range(8):
        cols = slice(i * 128, i * 128 + 128)
        out = (r.acct[:, cols] * over[:, cols]).T * keep_high
        r.out[cols, :] = out
        r.ob[cols, :] = out.astype(BF)
        r.smx[i] = pack_high(out).astype(BF)
    for mask in range(1, 8):
        device, to = peer(mask)
        send(r.smx.at[to], r.rmx.at[p], r.mx_s.at[mask], r.mx_r.at[mask], device)
    r.rmx[p] = r.smx[p]
    share_end(*sh_aw)
    share_near(*sh_ao)
    share_last(*sh_ao)
    ld_fg.wait()
    for mask in range(1, 8):
        arrive(r.rmx.at[peer(mask)[1]], r.mx_s.at[mask], r.mx_r.at[mask])

    def two_heads(a, b):
        a, b = a.astype(F32), b.astype(F32)
        return jnp.concatenate([pick(a, swap(b)), pick(swap(a), b)], axis=0).astype(BF)

    second = r.hid[...]
    for hh in range(G):
        second = second + dot(two_heads(r.rmx[hh], r.rmx[4 + hh]), r.ao[hh])
    r.sec[...] = second
    r.flow[...] = (second * rms_factor(second) * r.fg[...]).astype(BF)

    fan_start(r.flow, r.flp, r.fl_s, r.fl_r)

    grad_rows = r.ogp[x, rows(h, Q), :]
    r.fsum[...] = jnp.zeros((Q, D), F32)
    for t in range(G):
        hh = order[t]
        if t == 1:
            share_near(*sh_fu)
            share_near(*sh_fd)
        if t == 3:
            share_last(*sh_fu)
            share_last(*sh_fd)
        upward = dot(r.flow[...], r.fu[hh])
        square = upward * upward
        inner = 0.7978845608028654 * upward * (1.0 + 0.044715 * square)
        bent = jnp.tanh(inner)
        half_up = 0.5 * (1.0 + bent)
        active = (upward * half_up).astype(BF)
        slope = half_up + 0.5 * upward * (1.0 - bent * bent) * (
            0.7978845608028654 * (1.0 + 0.134145 * square)
        )
        grad_up = (dot_t(grad_rows, r.fd[hh]) * slope).astype(BF)
        r.fsum[...] += dot_t(grad_up, r.fu[hh])
        r.sag[hh, :, 0:256] = active[:, 0:256]
        r.sag[hh, :, 256:512] = grad_up[:, 0:256]
        r.sag[4 + hh, :, 0:256] = active[:, 256:512]
        r.sag[4 + hh, :, 256:512] = grad_up[:, 256:512]
    back, gain_ffn = rms_back(r.fsum[...], r.sec[...], r.fg[...])
    grad_second = grad_rows.astype(F32) + back
    r.gsec[...] = grad_second
    r.gb[...] = grad_second.astype(BF)
    r.gn[0:1, :] = gain_ffn

    for t in range(G):
        hh = order[t]
        grad = dot_t(r.gb[...], r.ao[hh])
        r.sgm[hh] = pack(grad).astype(BF)
        r.sgm[4 + hh] = pack_high(grad).astype(BF)
        for mask in ((4,) if t == 0 else (t, t + 4)):
            device, to = peer(mask)
            send(r.sgm.at[to], r.rgm.at[p], r.gm_s.at[mask], r.gm_r.at[mask], device)
    r.rgm[p] = r.sgm[p]
    for mask in range(1, 8):
        device, to = peer(mask)
        send(r.sag.at[to], r.rag.at[rows(p, Q)], r.ac_s.at[mask], r.ac_r.at[mask], device)
    r.rag[rows(p, Q), :] = r.sag[p]
    r.acct[...] = jnp.zeros((128, PW), F32)
    r.lsum[...] = r.sec[...]

    def layer_part(hh, carry):
        r.lsum[...] += dot(r.sag[hh, :, 0:256], r.fd[hh, 0:256, :])
        r.lsum[...] += dot(r.sag[4 + hh, :, 0:256], r.fd[hh, 256:512, :])
        return carry

    lax.fori_loop(0, G, layer_part, 0)
    r.lay[...] = r.lsum[...].astype(BF)
    for mask in range(1, 8):
        arrive(r.rgm.at[peer(mask)[1]], r.gm_s.at[mask], r.gm_r.at[mask])

    for i in range(8):
        cols = slice(i * 128, i * 128 + 128)
        got = r.rgm[i].astype(F32)
        grad = jnp.concatenate([swap(got), got], axis=0) * keep_high
        r.gz[cols, :] = grad.astype(BF)
        r.xg[cols, :] = pick(r.qd[cols, 0:128].astype(F32), grad).astype(BF)
        r.delta[0:1, cols] = jnp.sum((grad * r.out[cols, :]).T, axis=0, keepdims=True)

    fan_start(r.gb, r.gbp, r.gb_s, r.gb_r)
    head_rows_start(r.lay, land["layer"], r.ly_s, r.ly_r)
    fan_forward(r.flp, r.fl_s, r.fl_r)
    st_lay = keep_own(r.lay, land["layer"], (rows(h, Q), slice(None)), 16)

    def backward_tile(u, start, causal):
        at = pl.ds(start, PW - start)
        kv = r.kv[rows(u, KU), :]
        scores = dot_t(marked(kv, u), r.qd[at, :])
        weights = jnp.exp(scores - r.lse[0:1, at])
        if causal:
            gap = iota(scores.shape, 1) - iota(scores.shape, 0)
            weights = jnp.where(gap >= 0, weights, 0.0)
        dweights = dot_t(kv, r.gz[at, :])
        dscores = (weights * (dweights - r.delta[0:1, at])).astype(BF)
        other = r.xg[at, :]
        turned = kv.astype(F32).T.astype(BF)
        r.acct[:, at] += dot(turned, dscores)
        return pick(dot(dscores, other), dot(weights.astype(BF), other))

    last = 2 * nz <= SLOTS

    def grad_slot(u):
        return lax.rem(u, min(2 * nz, SLOTS))

    def grad_copy(u):
        return remote(
            r.sdk.at[grad_slot(u)], r.rdk.at[u], r.dk_s.at[u], r.dk_r.at[u],
            (2 * lax.rem(z + nz - 1, nz) + x, h),
        )

    def grad_join(u):
        arrive(r.rdk.at[u], r.dk_s.at[u], r.dk_r.at[u])
        slot = grad_slot(u)
        r.sdk[slot] = (r.sdk[slot].astype(F32) + r.rdk[u].astype(F32)).astype(BF)

    def backward_unit(u, carry):
        mark_again(u)
        if not last:
            @pl.when(u >= SLOTS)
            def _():
                grad_copy(u - SLOTS).wait_send()
        r.sdk[grad_slot(u)] = backward_tile(u, 0, False).astype(BF)
        if last:
            @pl.when(z == nz - 1)
            def _():
                grad_copy(u).start()
        else:
            @pl.when(z < nz - 1)
            def _():
                grad_join(u)
            grad_copy(u).start()
        return carry

    def pass_on(u, carry):
        grad_join(u)
        grad_copy(u).start()
        return carry

    lax.fori_loop(0, 2 * z, backward_unit, 0)
    if last:
        lax.fori_loop(0, jnp.where(z < nz - 1, 2 * z, 0), pass_on, 0)

    def own_units():
        for own in range(2):
            mark_again(2 * z + own)
            r.dkv[own * KU : own * KU + KU, :] = backward_tile(2 * z + own, own * KU, True)

    own_units()

    for i in range(8):
        cols = slice(i * 128, i * 128 + 128)
        grad = r.acct[:, cols].T * 0.125
        r.sdq[i] = pack(grad).astype(BF)
        r.dqb[cols, :] = (grad * keep_low).astype(BF)
    for mask in range(1, 8):
        device, to = peer(mask)
        send(r.sdq.at[to], r.rdq.at[p], r.dq_s.at[mask], r.dq_r.at[mask], device)
    r.rdq[p] = r.sdq[p]

    def spread_copy(src, size, slots, ssem, rsem, t):
        device, pz = plane(t)
        return remote(src.at[rows(pz, size)], slots.at[z], ssem.at[t], rsem.at[z], device)

    def spread_start(src, size, slots, ssem, rsem, later):
        for t in range(1, nz):
            @pl.when((z + t < nz) if later else (z + t >= nz))
            def _():
                spread_copy(src, size, slots, ssem, rsem, t).start()
        if not later:
            for t in range(1, nz):
                sends.append(spread_copy(src, size, slots, ssem, rsem, t))

    def all_arrive(dst, ssem, rsem):
        for mask in range(1, 8):
            arrive(dst.at[rows(peer(mask)[1], Q)], ssem.at[mask], rsem.at[mask])

    def spread_sum(src, size, slots, ssem, rsem):
        slots[z] = src[rows(z, size), :]
        for t in range(1, nz):
            pz = plane(t)[1]
            arrive(slots.at[pz], ssem.at[t], rsem.at[pz])
        total = slots[0].astype(F32)
        for i in range(1, nz):
            total = total + slots[i].astype(F32)
        return total.astype(BF)

    def final_start(src, out, size, ssem, rsem, xs, xr, lk):
        mine = out.at[x, rows(z, size)]
        for t in range(1, nz):
            send(src, mine, ssem.at[t], rsem.at[z], plane(t)[0])
        send(src, mine, xs.at[z], xr.at[z], peer(4)[0])
        return keep_own(src, out, (x, rows(z, size)), lk)

    def final_cross(out, size, ssem, rsem, xs, xr):
        for t in range(1, nz):
            pz = plane(t)[1]
            part = out.at[x, rows(pz, size)]
            arrive(part, ssem.at[t], rsem.at[pz])
            send(part, part, xs.at[pz], xr.at[pz], peer(4)[0])

    def final_last(out, size, xs, xr):
        for i in range(nz):
            arrive(out.at[1 - x, rows(i, size)], xs.at[i], xr.at[i])

    all_arrive(r.rag, r.ac_s, r.ac_r)
    fan_last(r.flp, r.fl_s, r.fl_r)
    arrive(og_half(1 - x, 1 - c), r.og_s.at[1], r.og_r.at[1])
    for i in range(2):
        r.fw[i * 256 : i * 256 + 256, :] = dot_l(
            r.flp[:, i * 256 : i * 256 + 256], r.rag[:, 256:512]
        ).astype(BF)
        r.fw[512 + i * 256 : 768 + i * 256, :] = (
            dot_l(r.rag[0:W, 0:256], r.ogp[0, :, i * 256 : i * 256 + 256])
            + dot_l(r.rag[W:PW, 0:256], r.ogp[1, :, i * 256 : i * 256 + 256])
        ).astype(BF)

    spread_start(r.fw, FR // nz, r.frs, r.fr_s, r.fr_r, True)
    spread_start(r.fw, FR // nz, r.frs, r.fr_s, r.fr_r, False)

    @pl.when(z < nz - 1)
    def _():
        for own in range(2):
            u = 2 * z + own
            arrive(r.rdk.at[u], r.dk_s.at[u], r.dk_r.at[u])
            r.dkv[own * KU : own * KU + KU, :] += r.rdk[u].astype(F32)

    for i in range(8):
        r.sdkv[i] = r.dkv[i * 128 : i * 128 + 128, :].astype(BF)
    for mask in range(1, 8):
        device, to = peer(mask)
        send(r.sdkv.at[to], r.rdkv.at[p], r.dkv_s.at[mask], r.dkv_r.at[mask], device)
    r.rdkv[p] = r.sdkv[p]


    fan_forward(r.gbp, r.gb_s, r.gb_r)
    head_rows_forward(land["layer"], r.ly_s, r.ly_r)
    fan_last(r.gbp, r.gb_s, r.gb_r)
    for i in range(2):
        cols = slice(i * 256, i * 256 + 256)
        r.aw_g[cols, 0:128] = (
            dot_l(r.alp[:, cols], r.dqb[...]) + dot_l(r.gbp[:, cols], r.ob[...])
        ).astype(BF)
        r.aw_g[cols, 128:256] = dot_l(r.alp[:, cols], r.sdkv[...].reshape(PW, 128)).astype(BF)

    spread_start(r.aw_g, AR // nz, r.ars, r.ar_s, r.ar_r, True)
    spread_start(r.aw_g, AR // nz, r.ars, r.ar_s, r.ar_r, False)
    for mask in range(1, 8):
        arrive(r.rdkv.at[peer(mask)[1]], r.dkv_s.at[mask], r.dkv_r.at[mask])
        arrive(r.rdq.at[peer(mask)[1]], r.dq_s.at[mask], r.dq_r.at[mask])

    share_near(*sh_aw)
    share_last(*sh_aw)

    attn_sum = jnp.zeros((Q, D), F32)
    for hh in range(G):
        first, other = r.rdkv[hh].astype(F32), r.rdkv[4 + hh].astype(F32)
        attn_sum = attn_sum + dot_t(two_heads(r.rdq[hh], r.rdq[4 + hh]), r.aw[hh, 0])
        attn_sum = attn_sum + dot_t(pick(first, swap(other)).astype(BF), r.aw[hh, 1])
        attn_sum = attn_sum + dot_t(pick(swap(first), other).astype(BF), r.aw[hh, 2])
    back, gain_attn = rms_back(attn_sum, r.hid[...], r.ag[...])
    r.gw[...] = (r.gsec[...] + back).astype(BF)
    r.gn[1:2, :] = gain_attn
    head_rows_start(r.gw, land["words"], r.gw_s, r.gw_r)
    st_gw = keep_own(r.gw, land["words"], (rows(h, Q), slice(None)), 17)
    grad_summary, gain_pool = rms_back(dot_t(r.gw[...], r.pw[...]), r.summ[...], r.pg[...])
    r.gsum[...] = grad_summary
    gs_low = grad_summary.astype(BF)
    r.gn[2:3, 0:256] = gain_pool
    r.spw[...] = dot_l(r.plow[...], r.gw[...]).astype(BF)
    for mask in range(1, 8):
        device, to = peer(mask)
        send(r.spw.at[rows(to, 32)], r.rpw.at[p], r.pw_s.at[mask], r.pw_r.at[mask], device)
    r.rpw[p] = r.spw[rows(p, 32), :]

    early = len(sends)

    ones = jnp.ones((128, 128), BF)

    def char_head_back(hh):
        r.gp[hh] = dot_t(gs_low, r.co[hh])
        w = r.cw[hh].astype(F32)
        r.cwt[hh, :, 0:128] = swap(w[:, 0:128]).astype(BF)
        r.cwt[hh, :, 128:256] = (w[:, 128:256] * keep_high).astype(BF)

        kq = r.kq[hh, :, 0:128].reshape(GROUPS, 128, 128)
        grad = jnp.broadcast_to(r.gp[hh][:, None, :], (Q, L, 128)).reshape(R, 128)
        gain = dot((r.kq[hh, :, 128:256].astype(F32) * grad).astype(BF), ones)
        gain = gain.reshape(GROUPS, 128, 128)
        weights = r.pt[hh].astype(F32)
        centre = jnp.sum(weights * gain, axis=1, keepdims=True)
        dscores = ((gain - centre) * (weights * r.share[:, 0:1, :])).astype(BF)
        dquery = (bdot_l(dscores, kq) * 0.125).reshape(R, 128)
        dkey = bdot(dscores, kq).reshape(R, 128)
        r.kq[hh, :, 0:128] = pick(dquery, dkey).astype(BF)
        if nz <= FEW:
            took = r.took[hh].astype(F32)
        else:
            took = bdot(r.pt[hh], r.live[...]).reshape(R, 128)
        r.kq[hh, :, 128:256] = (took * r.shc[...] * grad).astype(BF)
        term = dot_l(r.low[...], r.kq[hh])
        pooled = swap(r.pooled[hh]).astype(BF)
        r.scw[hh, :, 0:128] = term[:, 0:128].astype(BF)
        r.scw[hh, :, 128:256] = (term[:, 128:256] + dot_l(gs_low, pooled)).astype(BF)

    def char_term(t):
        hh = order[t]
        char_head_back(hh)
        for mask in ((4,) if t == 0 else (t, t + 4)):
            device, to = peer(mask)
            px = 1 - x if mask & 4 else x
            send(
                r.scw.at[hh, rows(px, 128)], r.rcw.at[p], r.cw_s.at[mask], r.cw_r.at[mask], device
            )

    def plane_sum(slots, ssem, rsem):
        for mask in range(1, 8):
            arrive(slots.at[peer(mask)[1]], ssem.at[mask], rsem.at[mask])
        total = slots[0].astype(F32)
        for i in range(1, 8):
            total = total + slots[i].astype(F32)
        return total

    def planes_start(slots, ssem, rsem):
        for t in range(1, nz):
            send(slots.at[z], slots.at[z], ssem.at[t], rsem.at[z], plane(t)[0])

    def planes_sum(slots, ssem, rsem):
        for t in range(1, nz):
            pz = plane(t)[1]
            arrive(slots.at[pz], ssem.at[t], rsem.at[pz])
        total = slots[0].astype(F32)
        for i in range(1, nz):
            total = total + slots[i].astype(F32)
        return total

    char_term(3)
    char_term(2)

    r.ffin[...] = spread_sum(r.fw, FR // nz, r.frs, r.fr_s, r.fr_r)
    st_ffn = final_start(r.ffin, land["ffn"], FR // nz, r.fa_s, r.fa_r, r.xf_s, r.xf_r, 18)
    head_rows_forward(land["words"], r.gw_s, r.gw_r)

    char_term(1)
    char_term(0)
    r.rcw[p] = r.scw[h, rows(x, 128), :]
    r.zpw[z] = plane_sum(r.rpw, r.pw_s, r.pw_r).astype(BF)
    planes_start(r.zpw, r.pz_s, r.pz_r)

    def char_back(i):
        part = pl.ds(i * (R // 2), R // 2)
        words = pl.ds(i * (Q // 2), Q // 2)
        upstream = dot_t(r.kq[0, part, :], r.cwt[0])
        for hh in range(1, G):
            upstream = upstream + dot_t(r.kq[hh, part, :], r.cwt[hh])
        values = r.xin[words].astype(F32).reshape(R // 2, C)
        back, gain = rms_back(upstream, values, r.cg[...])
        of_word = jnp.broadcast_to(r.gsum[words, :][:, None, :], (Q // 2, L, C))
        full = back + r.shc[part, 0:1] * of_word.reshape(R // 2, C)
        r.xin[words] = full.astype(BF).reshape(Q // 2, L, C)
        return gain

    gain_char = char_back(0)


    r.afin[...] = spread_sum(r.aw_g, AR // nz, r.ars, r.ar_s, r.ar_r)
    st_att = final_start(r.afin, land["att"], AR // nz, r.aa_s, r.aa_r, r.xa_s, r.xa_r, 19)

    r.zcw[z] = plane_sum(r.rcw, r.cw_s, r.cw_r).astype(BF)
    planes_start(r.zcw, r.cz_s, r.cz_r)
    gain_char = gain_char + char_back(1)
    st_chars = load(r.xin, r.o_chars, 20)
    r.gn[2:3, 256:512] = gain_char
    r.gn[3:8, :] = jnp.zeros((5, D), F32)
    for mask in range(1, 8):
        send(r.gn, r.rgn.at[p], r.gn_s.at[mask], r.gn_r.at[mask], peer(mask)[0])
    r.rgn[p] = r.gn[...]

    final_cross(land["ffn"], FR // nz, r.fa_s, r.fa_r, r.xf_s, r.xf_r)
    for copy in sends[:early]:
        copy.wait_send()
    del sends[:early]
    for t in range(1, nz):
        @pl.when(z + t < nz)
        def _():
            docs_copy(t, z).wait_send()

    @pl.when(z + 1 < nz)
    def _():
        def sent(u, carry):
            unit_copy(u).wait_send()
            return carry

        lax.fori_loop(0, 2 * z + 2, sent, 0)

    def grads_sent(u, carry):
        grad_copy(u).wait_send()
        return carry

    lax.fori_loop(jnp.maximum(2 * z - SLOTS, 0), 2 * z, grads_sent, 0)

    final_cross(land["att"], AR // nz, r.aa_s, r.aa_r, r.xa_s, r.xa_r)
    r.pfin[...] = planes_sum(r.zpw, r.pz_s, r.pz_r).astype(BF)
    for mask in range(1, 8):
        mine = land["pool"].at[rows(p, 32)]
        send(r.pfin, mine, r.pa_s.at[mask], r.pa_r.at[mask], peer(mask)[0])
    st_pool = keep_own(r.pfin, land["pool"], (rows(p, 32), slice(None)), 21)
    r.zgn[z] = plane_sum(r.rgn, r.gn_s, r.gn_r)
    planes_start(r.zgn, r.gz_s, r.gz_r)
    r.cfin[...] = planes_sum(r.zcw, r.cz_s, r.cz_r).astype(BF)
    send(r.cfin, land["chr"].at[x], r.x_s.at[4], r.x_r.at[4], peer(4)[0])
    st_chr = keep_own(r.cfin, land["chr"], x, 22)
    r.gnf[...] = planes_sum(r.zgn, r.gz_s, r.gz_r)
    st_gain = load(r.gnf, r.o_gain, 23)

    waiting = [st_chars, st_gain, st_ffn, st_att, st_lay, st_gw, st_pool, st_chr]

    def finish(name, k):
        if few:
            waiting.append(load(land[name], getattr(r, "o_" + name), k))

    head_rows_last(land["layer"], r.ly_s, r.ly_r)
    finish("layer", 24)
    head_rows_last(land["words"], r.gw_s, r.gw_r)
    finish("words", 25)
    final_last(land["ffn"], FR // nz, r.xf_s, r.xf_r)
    finish("ffn", 26)
    final_last(land["att"], AR // nz, r.xa_s, r.xa_r)
    finish("att", 27)
    for mask in range(1, 8):
        arrive(land["pool"].at[rows(peer(mask)[1], 32)], r.pa_s.at[mask], r.pa_r.at[mask])
    finish("pool", 28)
    arrive(land["chr"].at[1 - x], r.x_s.at[4], r.x_r.at[4])
    finish("chr", 29)
    for copy in waiting:
        if copy is not None:
            copy.wait()
    for copy in sends:
        copy.wait_send()


def per_device(nz, *arguments):
    given = dict(zip(INPUTS, arguments))
    for name in ("char_count", "document_ids"):
        given[name] = given[name].reshape(G, 128)
    given["char_proj"] = jnp.swapaxes(given["char_proj"], 1, 2)
    for name in ("char_gain", "pool_gain", "attn_gain", "ffn_gain"):
        given[name] = given[name].reshape(1, -1)
    scratch = scratch_list(nz)
    any_space = pl.BlockSpec(memory_space=pl.ANY)
    out_shape = [
        jax.ShapeDtypeStruct((W, D), BF),
        jax.ShapeDtypeStruct((W, D), BF),
        jax.ShapeDtypeStruct((Q, L, C), BF),
        jax.ShapeDtypeStruct((2, FR, 256), BF),
        jax.ShapeDtypeStruct((2, AR, 256), BF),
        jax.ShapeDtypeStruct((2, 128, 256), BF),
        jax.ShapeDtypeStruct((C, D), BF),
        jax.ShapeDtypeStruct((8, D), F32),
    ]
    names = INPUTS + OUTPUTS + list(scratch)
    layer, words, chars, ffn, att, chr_grad, pool, gain = pl.pallas_call(
        functools.partial(layer_kernel, nz, names),
        out_shape=out_shape,
        in_specs=[any_space] * len(INPUTS),
        out_specs=[any_space] * len(OUTPUTS),
        scratch_shapes=list(scratch.values()),
        compiler_params=pltpu.CompilerParams(
            collective_id=0, has_side_effects=True, vmem_limit_bytes=62 << 20
        ),
    )(*[given[name] for name in INPUTS])

    grads = [
        jax.ShapeDtypeStruct((W, D), BF),
        jax.ShapeDtypeStruct((W, D), BF),
        jax.ShapeDtypeStruct((Q, L, C), BF),
        jax.ShapeDtypeStruct((1, C), F32),
        jax.ShapeDtypeStruct((3, 64, C), F32),
        jax.ShapeDtypeStruct((64, C), F32),
        jax.ShapeDtypeStruct((1, C), F32),
        jax.ShapeDtypeStruct((C, D), F32),
        jax.ShapeDtypeStruct((1, D), F32),
        jax.ShapeDtypeStruct((3, D, 128), F32),
        jax.ShapeDtypeStruct((128, D), F32),
        jax.ShapeDtypeStruct((1, D), F32),
        jax.ShapeDtypeStruct((D, FS), F32),
        jax.ShapeDtypeStruct((FS, D), F32),
    ]
    result = pl.pallas_call(
        unpack_kernel,
        out_shape=grads,
        in_specs=[any_space] * len(out_shape),
        out_specs=[any_space] * len(grads),
        scratch_shapes=[pltpu.VMEM(a.shape, a.dtype) for a in out_shape + grads[3:]]
        + [pltpu.SemaphoreType.DMA((len(out_shape),)), pltpu.SemaphoreType.DMA((len(grads),))],
        compiler_params=pltpu.CompilerParams(vmem_limit_bytes=62 << 20),
    )(layer, words, chars, ffn, att, chr_grad, pool, gain)
    result = list(result)
    result[4] = jnp.swapaxes(result[4], 1, 2)
    for i in (3, 6, 8, 11):
        result[i] = result[i].reshape(-1)
    return tuple(result)


def unpack_kernel(*refs):
    given, out, held, made = refs[0:8], refs[8:22], refs[22:30], refs[30:41]
    in_sem, out_sem = refs[41:]
    ffn, att, chr_grad, pool, gain = held[3:]
    loads = [pltpu.make_async_copy(given[i], held[i], in_sem.at[i]) for i in range(8)]
    stores = [pltpu.make_async_copy(held[i], out[i], out_sem.at[i]) for i in range(3)]
    stores += [pltpu.make_async_copy(made[i], out[3 + i], out_sem.at[3 + i]) for i in range(11)]
    for i in (3, 4, 2, 0, 1, 6, 5, 7):
        loads[i].start()
    (g_char, g_proj, g_out, g_pool, g_pproj, g_attn, g_aproj, g_aout, g_ffn, g_up, g_down) = made

    def pick(a, b):
        return jnp.where(iota(a.shape, 1) < 64, a, b)

    loads[3].wait()
    for i in range(2):
        cols = slice(i * 256, i * 256 + 256)
        g_up[:, cols] = ffn[i, 0:512, :].astype(F32)
        g_down[cols, 0:256] = ffn[i, 512:768, :].astype(F32)
        g_down[cols, 256:512] = ffn[i, 768:1024, :].astype(F32)
    stores[12].start()
    stores[13].start()
    for i in (2, 0, 1):
        loads[i].wait()
        stores[i].start()
    loads[4].wait()
    first, other = att[0, :, 0:128].astype(F32), att[1, :, 0:128].astype(F32)
    g_aproj[0] = pick(first, swap(other))
    g_aout[...] = pick(swap(first), other).T
    first, other = att[0, :, 128:256].astype(F32), att[1, :, 128:256].astype(F32)
    g_aproj[1] = pick(first, swap(other))
    g_aproj[2] = pick(swap(first), other)
    stores[9].start()
    stores[10].start()
    loads[6].wait()
    g_pproj[...] = pool[...].astype(F32)
    stores[7].start()
    loads[5].wait()
    for i in range(2):
        cols = slice(i * 128, i * 128 + 128)
        block = chr_grad[i].astype(F32)
        first, other = block[:, 0:128].T, block[:, 128:256].T
        g_proj[0, :, cols] = first[0:64]
        g_proj[1, :, cols] = first[64:128]
        g_out[:, cols] = other[0:64]
        g_proj[2, :, cols] = other[64:128]
    stores[4].start()
    stores[5].start()
    loads[7].wait()
    g_ffn[...] = gain[0:1, :]
    g_attn[...] = gain[1:2, :]
    g_pool[...] = gain[2:3, 0:256]
    g_char[...] = gain[2:3, 256:512]
    for i in (3, 6, 8, 11):
        stores[i].start()
    for copy in stores:
        copy.wait()


def solution(mesh):
    nz = mesh.shape["seq"] // 2
    placed = (
        P("seq", None),
        P("seq", None, None),
        P("seq"),
        P("seq"),
        P("seq", None),
        P(),
        P(None, None, "head"),
        P("head", None),
        P(),
        P(),
        P(),
        P(None, None, "head"),
        P("head", None),
        P(),
        P(None, "head"),
        P("head", None),
    )
    return jax.shard_map(
        functools.partial(per_device, nz),
        mesh=mesh,
        in_specs=placed,
        out_specs=(
            P("seq", None),
            P("seq", None),
            P(("seq", "head"), None, None),
            P(),
            P(None, None, "head"),
            P("head", None),
            P(),
            P(),
            P(),
            P(None, None, "head"),
            P("head", None),
            P(),
            P(None, "head"),
            P("head", None),
        ),
        check_vma=False,
    )
```
